32 devices in a mesh: gx: 4 (over y, core), gy: 4 (over z), gz: 2 (over x).
Axes of the slice: x: 2, y: 2, z: 4, core: 2. Of those that a mesh axis runs over, the one named last changes fastest.
Arguments:
- initial_thermal_state: float32 [256, 128, 256], P('gx', 'gy', 'gz'), may hold values from -6 to 6
- thermal_spread_rate: float32 [256, 128, 256], P('gx', 'gy', 'gz'), may hold values from 0.25 to 4
- yz_skew_factor: bfloat16 [256, 128, 256], P('gx', 'gy', 'gz'), may hold values from -1 to 1
Outputs:
- known_source_vector: float32 [256, 128, 256], P('gx', 'gy', 'gz')
- half_step: float32 [256, 128, 256], P('gx', 'gy', 'gz')
The draws below stay inside these ranges and needn't reach their ends.
All inputs are finite; a program needn't handle non-finite values.
Results may differ from the reference program's by a relative error of at most 0.0003.
Values sent between devices are 32-bit elements; how exact they have to be, the bound alone decides.
A program may use at most 64 MiB of HBM per device.

```python
import math
import jax
import jax.numpy as jnp
from jax import lax

NODES_ALONG_X = 256
NODES_ALONG_Y = 128
NODES_ALONG_Z = 256


def block_levels(rng, dims, split, low, largest):
    level, own = 1.0, jax.random.fold_in(rng, 6)
    for axis_at, shards_of in split:
        steps = jnp.exp(jax.random.uniform(jax.random.fold_in(own, axis_at), (shards_of,), jnp.float32, low / len(split), largest / len(split)))
        level = level * jnp.repeat(steps, dims[axis_at] // shards_of).reshape([-1 if axis == axis_at else 1 for axis in range(len(dims))])
    return level


def bell_draw(stream_key, shape, deviation, reach, shards=(), kind=jnp.bfloat16):
    array = deviation * jax.random.normal(stream_key, shape, jnp.float32)
    if shards:
        array = array * block_levels(stream_key, shape, shards, -0.22, 0.18)
    return jnp.clip(array, -reach, reach).astype(kind)


def setup_inputs(seed: int = 0) -> dict:
    splits = jax.random.split(jax.random.key(seed), 4)
    initial_thermal_state = bell_draw(splits[0], (NODES_ALONG_X, NODES_ALONG_Y, NODES_ALONG_Z), 1.0, 6.0, ((0, 4), (1, 4), (2, 2)), jnp.float32)
    thermal_spread_rate = jnp.clip(jnp.exp(math.log(4.0) - 2.7725887 * jax.random.uniform(splits[1], (NODES_ALONG_X, NODES_ALONG_Y, NODES_ALONG_Z), jnp.float32) ** block_levels(splits[1], (NODES_ALONG_X, NODES_ALONG_Y, NODES_ALONG_Z), ((0, 4), (1, 4), (2, 2)), -0.2, 0.2)), 0.25, 4.0)
    yz_skew_factor = jnp.clip(jax.random.uniform(splits[2], (NODES_ALONG_X, NODES_ALONG_Y, NODES_ALONG_Z), jnp.float32, -1.0, 1.0) * block_levels(splits[2], (NODES_ALONG_X, NODES_ALONG_Y, NODES_ALONG_Z), ((0, 4), (1, 4), (2, 2)), -0.4, 0.0), -1.0, 1.0).astype(jnp.bfloat16)
    return {"initial_thermal_state": initial_thermal_state, "thermal_spread_rate": thermal_spread_rate, "yz_skew_factor": yz_skew_factor}


ratio_x = 4096.0
ratio_y = 0.2
ratio_z = 0.2
ratio_mix = 0.25


def boundary_flux_terms(padded_heat, padded_diff, yz_skew_factor):
    centre = padded_heat[:, 1:-1, 1:-1]
    centre_diff = padded_diff[:, 1:-1, 1:-1]
    plus_y = 0.5 * (centre_diff + padded_diff[:, 2:, 1:-1])
    minus_y = 0.5 * (centre_diff + padded_diff[:, :-2, 1:-1])
    plus_z = 0.5 * (centre_diff + padded_diff[:, 1:-1, 2:])
    minus_z = 0.5 * (centre_diff + padded_diff[:, 1:-1, :-2])
    flux_y = plus_y * (padded_heat[:, 2:, 1:-1] - centre) - minus_y * (centre - padded_heat[:, :-2, 1:-1])
    flux_z = plus_z * (padded_heat[:, 1:-1, 2:] - centre) - minus_z * (centre - padded_heat[:, 1:-1, :-2])
    mixed = padded_heat[:, 2:, 2:] - padded_heat[:, 2:, :-2] - padded_heat[:, :-2, 2:] + padded_heat[:, :-2, :-2]
    return centre + ratio_y * flux_y + ratio_z * flux_z + ratio_mix * yz_skew_factor.astype(jnp.float32) * mixed


def x_bands(padded_diff):
    centre = padded_diff[1:-1]
    minus_x = 0.5 * (centre + padded_diff[:-2])
    plus_x = 0.5 * (centre + padded_diff[2:])
    return -ratio_x * minus_x, 1.0 + ratio_x * (minus_x + plus_x), -ratio_x * plus_x


def thomas_solve(lower_band, main_band, upper_band, right_side):
    def forward(state, values):
        prev_upper, prev_side = state
        low_value, main_value, up_value, side_value = values
        pivot = main_value - low_value * prev_upper
        next_upper = up_value / pivot
        next_side = (side_value - low_value * prev_side) / pivot
        return (next_upper, next_side), (next_upper, next_side)

    start = (jnp.zeros_like(main_band[0]), jnp.zeros_like(right_side[0]))
    _, (uppers, sides) = lax.scan(forward, start, (lower_band, main_band, upper_band, right_side))

    def backward(later, values):
        up_value, side_value = values
        current = side_value - up_value * later
        return current, current

    _, solved = lax.scan(backward, jnp.zeros_like(right_side[0]), (uppers, sides), reverse=True)
    return solved


def reference(initial_thermal_state, thermal_spread_rate, yz_skew_factor):
    ghost_border_layer = ((0, 0), (1, 1), (1, 1))
    known_source_vector = boundary_flux_terms(jnp.pad(initial_thermal_state, ghost_border_layer), jnp.pad(thermal_spread_rate, ghost_border_layer), yz_skew_factor)
    lower_band, main_band, upper_band = x_bands(jnp.pad(thermal_spread_rate, ((1, 1), (0, 0), (0, 0))))
    half_step = thomas_solve(lower_band, main_band, upper_band, known_source_vector)
    return known_source_vector, half_step
```

```python
import functools
import math

import jax
import jax.numpy as jnp
from jax import lax
from jax.experimental import pallas as pl
from jax.experimental.pallas import tpu as pltpu
from jax.sharding import PartitionSpec as P

ratio_x = 4096.0
ratio_y = 0.2
ratio_z = 0.2
ratio_mix = 0.25
MESH = pl.DeviceIdType.MESH


def compose(second, first):
    a2, b2, c2, d2 = second
    a1, b1, c1, d1 = first
    return (a2 * a1 + b2 * c1, a2 * b1 + b2 * d1, c2 * a1 + d2 * c1, c2 * b1 + d2 * d1)


def carry(second, second_pq, first_pq):
    a2, b2, c2, d2 = second
    p1, q1 = first_pq
    return (a2 * p1 + b2 * q1 + second_pq[0], c2 * p1 + d2 * q1 + second_pq[1])


def pick(flag, yes, no):
    return tuple(jnp.where(flag, s, t) for s, t in zip(yes, no))


def kernel(
    nx, ny, nz, u_hbm, d_hbm, k_hbm, r_hbm, w_hbm,
    u_pad, d_pad, skew, rho, r_buf, w_buf,
    x_halo, y_send, y_recv, z_send, z_recv, skew_edge,
    map_send, map_recv, pq_send, pq_recv, rel_send, rel_recv,
    load_sem, store_sem, halo_send, halo_recv, line_send, line_recv,
):
    planes, rows, lanes = u_hbm.shape
    stages = int(math.log2(nx))
    gx, gy, gz = lax.axis_index("gx"), lax.axis_index("gy"), lax.axis_index("gz")
    other_z = 1 - gz
    body_rows = slice(8, 8 + rows)

    d_load = pltpu.make_async_copy(d_hbm, d_pad.at[:, body_rows, :], load_sem.at[0])
    u_load = pltpu.make_async_copy(u_hbm, u_pad.at[:, body_rows, :], load_sem.at[1])
    k_load = pltpu.make_async_copy(k_hbm, skew, load_sem.at[2])
    d_load.start()
    u_load.start()
    k_load.start()

    barrier = pltpu.get_barrier_semaphore()

    def greet(x, y, z):
        pl.semaphore_signal(barrier, inc=1, device_id=(x, y, z), device_id_type=MESH)

    partners = [gx + (1 << s) - 2 * (1 << s) * ((gx // (1 << s)) % 2) for s in range(stages)]
    for x in partners:
        greet(x, gy, gz)
    greet(gx, gy, other_z)

    @pl.when(gx > 0)
    def _():
        greet(gx - 1, gy, gz)

    @pl.when(gy > 0)
    def _():
        greet(gx, gy - 1, gz)
        greet(gx, gy - 1, other_z)

    @pl.when(gy < ny - 1)
    def _():
        greet(gx, gy + 1, gz)
        greet(gx, gy + 1, other_z)

    one = jnp.int32(1)
    zero = jnp.int32(0)
    awaited = (
        stages + 1
        + jnp.where(gx < nx - 1, one, zero)
        + 2 * jnp.where(gy > 0, one, zero)
        + 2 * jnp.where(gy < ny - 1, one, zero)
    )

    def remote(src, dst, send, recv, x, y, z):
        return pltpu.make_async_remote_copy(
            src_ref=src, dst_ref=dst, send_sem=send, recv_sem=recv,
            device_id=(x, y, z), device_id_type=MESH,
        )

    x_copy = remote(
        d_hbm.at[planes - 1], x_halo, halo_send.at[0], halo_recv.at[0], gx + 1, gy, gz
    )
    up_copy = remote(y_send.at[0], y_recv.at[1], halo_send.at[1], halo_recv.at[1], gx, gy - 1, gz)
    down_copy = remote(y_send.at[1], y_recv.at[0], halo_send.at[2], halo_recv.at[2], gx, gy + 1, gz)
    z_copy = remote(
        z_send, z_recv.at[pl.ds(8, rows), :], halo_send.at[3], halo_recv.at[3], gx, gy, other_z
    )
    up_corner = remote(
        z_send.at[pl.ds(0, 8), :], z_recv.at[pl.ds(8 + rows, 8), :],
        halo_send.at[4], halo_recv.at[4], gx, gy - 1, other_z,
    )
    down_corner = remote(
        z_send.at[pl.ds(rows - 8, 8), :], z_recv.at[pl.ds(0, 8), :],
        halo_send.at[5], halo_recv.at[5], gx, gy + 1, other_z,
    )

    pl.semaphore_wait(barrier, awaited)

    @pl.when(gx < nx - 1)
    def _():
        x_copy.start()

    @pl.when(gx == 0)
    def _():
        x_halo[...] = jnp.zeros((rows, lanes), jnp.float32)

    @pl.when(gy == 0)
    def _():
        y_recv[0] = jnp.zeros((2, planes, lanes), jnp.float32)
        z_recv[0:8, :] = jnp.zeros((8, lanes), jnp.float32)

    @pl.when(gy == ny - 1)
    def _():
        y_recv[1] = jnp.zeros((2, planes, lanes), jnp.float32)
        z_recv[8 + rows : 16 + rows, :] = jnp.zeros((8, lanes), jnp.float32)

    lane = lax.broadcasted_iota(jnp.int32, (rows, lanes), 1)
    edge = jnp.where(gz == 0, jnp.int32(lanes - 1), zero)

    d_load.wait()
    u_load.wait()
    for field, pad in enumerate((u_pad, d_pad)):
        y_send[0, field] = pad[:, 8, :]
        y_send[1, field] = pad[:, 7 + rows, :]

    @pl.when(gy > 0)
    def _():
        up_copy.start()

    @pl.when(gy < ny - 1)
    def _():
        down_copy.start()

    def gather_edge(i, acc):
        heat = pltpu.roll(u_pad[i, 8 : 8 + rows, :], lax.rem(i - edge + lanes, lanes), 1)
        diff = pltpu.roll(d_pad[i, 8 : 8 + rows, :], lax.rem(i + planes - edge + lanes, lanes), 1)
        acc = jnp.where(lane == i, heat, acc)
        return jnp.where(lane == i + planes, diff, acc)

    zeros = jnp.zeros((rows, lanes), jnp.float32)
    ones = jnp.ones((rows, lanes), jnp.float32)
    z_send[...] = lax.fori_loop(0, planes, gather_edge, zeros, unroll=8)
    z_copy.start()

    @pl.when(gy > 0)
    def _():
        up_corner.start()

    @pl.when(gy < ny - 1)
    def _():
        down_corner.start()

    k_load.wait()

    @pl.when(gx > 0)
    def _():
        x_copy.wait_recv()

    def homogeneous(i, state):
        a, b, c, d, before, acc = state
        here = d_pad[i, 8 : 8 + rows, :]
        step = 1.0 / (0.5 * ratio_x * (here + before))
        rho[i] = step
        a = a + step * c
        b = b + step * d
        bend = pltpu.roll(skew[i].astype(jnp.float32), lax.rem(i - edge + lanes, lanes), 1)
        return (a, b, c + a, d + b, here, jnp.where(lane == i, bend, acc))

    a, b, c, d, last, acc = lax.fori_loop(
        0, planes, homogeneous, (ones, zeros, zeros, ones, x_halo[...], zeros), unroll=4
    )
    skew_edge[...] = acc
    closing = jnp.where(gx == nx - 1, 1.0 / (0.5 * ratio_x * last), 0.0)
    own = (a + closing * c, b + closing * d, c, d)

    line = []

    def swap(send_buf, recv_buf, values, partner):
        at = len(line)
        for n, v in enumerate(values):
            send_buf[n] = v
        copy = remote(send_buf, recv_buf, line_send.at[at], line_recv.at[at], partner, gy, gz)
        copy.start()
        line.append(copy)
        copy.wait_recv()
        return tuple(recv_buf[n] for n in range(len(values)))

    flags = [(gx // (1 << s)) % 2 == 1 for s in range(stages)]
    group, left, right = own, (ones, zeros, zeros, ones), own
    steps = []
    for s in range(stages - 1):
        theirs = swap(map_send.at[s], map_recv.at[s], group, partners[s])
        second = pick(flags[s], group, theirs)
        first = pick(flags[s], theirs, group)
        steps.append((second, left, theirs))
        group = compose(second, first)
        left = pick(flags[s], compose(left, theirs), left)
        right = pick(flags[s], right, compose(theirs, right))
    in_right = flags[-1]
    inv_a = 1.0 / group[0]
    z_out = group[1] / group[3]
    (met,) = swap(
        rel_send.at[0], rel_recv.at[0], (jnp.where(in_right, group[1] * inv_a, z_out),), partners[-1]
    )
    z0 = jnp.where(in_right, met, 0.0)
    y0 = jnp.where(in_right, 0.0, met)
    z_in = (left[0] * z0 + left[1]) / (left[2] * z0 + left[3])
    inv_right = 1.0 / (right[0] + y0 * right[2])
    inv_sum = 1.0 / (z_in + (right[1] + y0 * right[3]) * inv_right)

    @pl.when(gy > 0)
    def _():
        down_copy.wait_recv()
        down_corner.wait_recv()

    @pl.when(gy < ny - 1)
    def _():
        up_copy.wait_recv()
        up_corner.wait_recv()

    z_copy.wait_recv()
    met_heat = z_recv[8 : 8 + rows, :]
    met_diff = pltpu.roll(met_heat, lanes - planes, 1)
    own_edge = z_send[...]
    own_diff = pltpu.roll(own_edge, lanes - planes, 1)
    met_bend = z_recv[9 : 9 + rows, :] - z_recv[7 : 7 + rows, :]
    mix_sign = jnp.where(gz == 0, jnp.float32(ratio_mix), jnp.float32(-ratio_mix))
    edge_term = (0.5 * ratio_z) * (
        own_diff * met_heat + met_diff * (met_heat - own_edge)
    ) + mix_sign * skew_edge[...] * met_bend

    first_lane = lane == 0
    last_lane = lane == lanes - 1
    edge_lane = lane == edge

    def source(i, state):
        wp, fp = state
        for field, pad in enumerate((u_pad, d_pad)):
            pad[i, 7:8, :] = y_recv[0, field, pl.ds(i, 1), :]
            pad[i, 8 + rows : 9 + rows, :] = y_recv[1, field, pl.ds(i, 1), :]
        heat = u_pad[i, 8 : 8 + rows, :]
        diff = d_pad[i, 8 : 8 + rows, :]
        heat_m = u_pad[i, 7 : 7 + rows, :]
        heat_p = u_pad[i, 9 : 9 + rows, :]
        flux_y = (diff + d_pad[i, 9 : 9 + rows, :]) * (heat_p - heat) - (
            diff + d_pad[i, 7 : 7 + rows, :]
        ) * (heat - heat_m)
        next_heat = jnp.where(last_lane, 0.0, pltpu.roll(heat, lanes - 1, 1))
        next_diff = jnp.where(last_lane, 0.0, pltpu.roll(diff, lanes - 1, 1))
        face = (diff + next_diff) * (next_heat - heat)
        before = jnp.where(first_lane, diff * heat, pltpu.roll(face, 1, 1))
        bend = heat_p - heat_m
        mixed = jnp.where(last_lane, 0.0, pltpu.roll(bend, lanes - 1, 1)) - jnp.where(
            first_lane, 0.0, pltpu.roll(bend, 1, 1)
        )
        extra = pltpu.roll(edge_term, lax.rem(edge - i + lanes, lanes), 1)
        side = (
            heat
            + (0.5 * ratio_y) * flux_y
            + (0.5 * ratio_z) * (face - before)
            + ratio_mix * skew[i].astype(jnp.float32) * mixed
            + jnp.where(edge_lane, extra, 0.0)
        )
        r_buf[i] = side
        wp = wp + rho[i] * fp
        return (wp, fp + (wp - side))

    wp, fp = lax.fori_loop(0, planes, source, (zeros, zeros), unroll=4)
    r_store = pltpu.make_async_copy(r_buf, r_hbm, store_sem.at[0])
    r_store.start()

    group_pq = (wp + closing * fp, fp)
    left_pq, right_pq = (zeros, zeros), group_pq
    for s in range(stages - 1):
        second, left_map, theirs_map = steps[s]
        theirs = swap(pq_send.at[s], pq_recv.at[s], group_pq, partners[s])
        second_pq = pick(flags[s], group_pq, theirs)
        first_pq = pick(flags[s], theirs, group_pq)
        left_pq = pick(flags[s], carry(left_map, left_pq, theirs), left_pq)
        right_pq = pick(flags[s], right_pq, carry(theirs_map, theirs, right_pq))
        group_pq = carry(second, second_pq, first_pq)
    gp, gq = group_pq
    (met,) = swap(
        rel_send.at[1], rel_recv.at[1], (jnp.where(in_right, -gp * inv_a, gp - z_out * gq),), partners[-1]
    )
    e0 = jnp.where(in_right, met, 0.0)
    g0 = jnp.where(in_right, 0.0, met)
    e_in = left[0] * e0 + left_pq[0] - z_in * (left[2] * e0 + left_pq[1])
    g_in = (g0 - right_pq[0] - y0 * right_pq[1]) * inv_right
    flux = (g_in - e_in) * inv_sum
    value = z_in * flux + e_in

    def march(i, state):
        value, flux = state
        value = value + rho[i] * flux
        w_buf[i] = value
        return (value, flux + (value - r_buf[i]))

    chunks = 4
    size = planes // chunks
    stores = []
    for n in range(chunks):
        value, flux = lax.fori_loop(n * size, (n + 1) * size, march, (value, flux), unroll=8)
        part = pl.ds(n * size, size)
        store = pltpu.make_async_copy(w_buf.at[part], w_hbm.at[part], store_sem.at[1 + n])
        store.start()
        stores.append(store)

    for copy in line:
        copy.wait_send()
    z_copy.wait_send()

    @pl.when(gx < nx - 1)
    def _():
        x_copy.wait_send()

    @pl.when(gy > 0)
    def _():
        up_copy.wait_send()
        up_corner.wait_send()

    @pl.when(gy < ny - 1)
    def _():
        down_copy.wait_send()
        down_corner.wait_send()

    r_store.wait()
    for store in stores:
        store.wait()


def body(nx, ny, nz, initial_thermal_state, thermal_spread_rate, yz_skew_factor):
    planes, rows, lanes = initial_thermal_state.shape
    stages = int(math.log2(nx))
    f32 = jnp.float32
    block = jax.ShapeDtypeStruct((planes, rows, lanes), f32)
    padded = pltpu.VMEM((planes, rows + 16, lanes), f32)
    full = pltpu.VMEM((planes, rows, lanes), f32)
    plane = pltpu.VMEM((rows, lanes), f32)
    faces = pltpu.VMEM((2, 2, planes, lanes), f32)
    maps = pltpu.VMEM((stages - 1, 4, rows, lanes), f32)
    sides = pltpu.VMEM((stages - 1, 2, rows, lanes), f32)
    relation = pltpu.VMEM((2, 1, rows, lanes), f32)
    return pl.pallas_call(
        functools.partial(kernel, nx, ny, nz),
        out_shape=(block, block),
        in_specs=[pl.BlockSpec(memory_space=pl.ANY)] * 3,
        out_specs=(pl.BlockSpec(memory_space=pl.ANY),) * 2,
        scratch_shapes=[
            padded, padded, pltpu.VMEM((planes, rows, lanes), jnp.bfloat16), full, full, full,
            plane, faces, faces, plane, pltpu.VMEM((rows + 16, lanes), f32), plane,
            maps, maps, sides, sides, relation, relation,
            pltpu.SemaphoreType.DMA((3,)),
            pltpu.SemaphoreType.DMA((5,)),
            pltpu.SemaphoreType.DMA((6,)),
            pltpu.SemaphoreType.DMA((6,)),
            pltpu.SemaphoreType.DMA((2 * stages,)),
            pltpu.SemaphoreType.DMA((2 * stages,)),
        ],
        compiler_params=pltpu.CompilerParams(
            collective_id=0, has_side_effects=True, vmem_limit_bytes=32 * 1024 * 1024
        ),
    )(initial_thermal_state, thermal_spread_rate, yz_skew_factor)


def solution(mesh):
    shape = dict(mesh.shape)
    spec = P("gx", "gy", "gz")
    return jax.shard_map(
        functools.partial(body, shape["gx"], shape["gy"], shape["gz"]),
        mesh=mesh, in_specs=(spec,) * 3, out_specs=(spec,) * 2, check_vma=False,
    )
```

```python
import functools
import math

import jax
import jax.numpy as jnp
from jax import lax
from jax.experimental import pallas as pl
from jax.experimental.pallas import tpu as pltpu
from jax.sharding import PartitionSpec as P

ratio_x = 4096.0
ratio_y = 0.2
ratio_z = 0.2
ratio_mix = 0.25
MESH = pl.DeviceIdType.MESH


def link(first, second):
    t1, z1, c1 = first
    t2, z2, c2 = second
    k1 = t1 / (1.0 + z1 * c2)
    k2 = t2 / (1.0 + z1 * c2)
    return (k1 * t2, z2 + k2 * t2 * z1, c1 + k1 * t1 * c2), (k1, k2)


def link_sides(weights, first, first_pq, second, second_pq):
    k1, k2 = weights
    p1, q1 = first_pq
    p2, q2 = second_pq
    return (p2 + k2 * (p1 - first[1] * q2), q1 + k1 * (q2 + second[2] * p1))


def pick(flag, yes, no):
    return tuple(jnp.where(flag, s, t) for s, t in zip(yes, no))


def kernel(
    nx, ny, nz, u_hbm, d_hbm, k_hbm, r_hbm, w_hbm,
    u_pad, d_pad, skew, rho, r_buf, w_buf,
    x_halo, y_send, y_recv, z_send, z_recv, skew_edge,
    map_send, map_recv, pq_send, pq_recv, rel_send, rel_recv,
    load_sem, store_sem, halo_send, halo_recv, line_send, line_recv,
):
    planes, rows, lanes = u_hbm.shape
    stages = int(math.log2(nx))
    gx, gy, gz = lax.axis_index("gx"), lax.axis_index("gy"), lax.axis_index("gz")
    other_z = 1 - gz
    pitch = rows + 16
    body_rows = pl.ds(8, rows)
    u_flat = u_pad.reshape(planes * pitch, lanes)
    d_flat = d_pad.reshape(planes * pitch, lanes)

    d_load = pltpu.make_async_copy(d_hbm, d_pad.at[:, body_rows, :], load_sem.at[0])
    u_load = pltpu.make_async_copy(u_hbm, u_pad.at[:, body_rows, :], load_sem.at[1])
    k_load = pltpu.make_async_copy(k_hbm, skew, load_sem.at[2])
    d_load.start()
    u_load.start()
    k_load.start()

    barrier = pltpu.get_barrier_semaphore()

    def greet(x, y, z):
        pl.semaphore_signal(barrier, inc=1, device_id=(x, y, z), device_id_type=MESH)

    partners = [gx + (1 << s) - 2 * (1 << s) * ((gx // (1 << s)) % 2) for s in range(stages)]
    for x in partners:
        greet(x, gy, gz)
    greet(gx, gy, other_z)

    @pl.when(gx > 0)
    def _():
        greet(gx - 1, gy, gz)

    @pl.when(gy > 0)
    def _():
        greet(gx, gy - 1, gz)
        greet(gx, gy - 1, other_z)

    @pl.when(gy < ny - 1)
    def _():
        greet(gx, gy + 1, gz)
        greet(gx, gy + 1, other_z)

    one = jnp.int32(1)
    zero = jnp.int32(0)
    awaited = (
        stages + 1
        + jnp.where(gx < nx - 1, one, zero)
        + 2 * jnp.where(gy > 0, one, zero)
        + 2 * jnp.where(gy < ny - 1, one, zero)
    )

    def remote(src, dst, send, recv, x, y, z):
        return pltpu.make_async_remote_copy(
            src_ref=src, dst_ref=dst, send_sem=send, recv_sem=recv,
            device_id=(x, y, z), device_id_type=MESH,
        )

    x_copy = remote(
        d_hbm.at[planes - 1], x_halo, halo_send.at[0], halo_recv.at[0], gx + 1, gy, gz
    )
    up_copy = remote(y_send.at[0], y_recv.at[1], halo_send.at[1], halo_recv.at[1], gx, gy - 1, gz)
    down_copy = remote(y_send.at[1], y_recv.at[0], halo_send.at[2], halo_recv.at[2], gx, gy + 1, gz)
    z_copy = remote(
        z_send, z_recv.at[pl.ds(8, rows), :], halo_send.at[3], halo_recv.at[3], gx, gy, other_z
    )
    up_corner = remote(
        z_send.at[pl.ds(0, 8), :], z_recv.at[pl.ds(8 + rows, 8), :],
        halo_send.at[4], halo_recv.at[4], gx, gy - 1, other_z,
    )
    down_corner = remote(
        z_send.at[pl.ds(rows - 8, 8), :], z_recv.at[pl.ds(0, 8), :],
        halo_send.at[5], halo_recv.at[5], gx, gy + 1, other_z,
    )

    pl.semaphore_wait(barrier, awaited)

    @pl.when(gx < nx - 1)
    def _():
        x_copy.start()

    @pl.when(gx == 0)
    def _():
        x_halo[...] = jnp.zeros((rows, lanes), jnp.float32)

    @pl.when(gy == 0)
    def _():
        y_recv[0] = jnp.zeros((2, planes, lanes), jnp.float32)
        z_recv[0:8, :] = jnp.zeros((8, lanes), jnp.float32)

    @pl.when(gy == ny - 1)
    def _():
        y_recv[1] = jnp.zeros((2, planes, lanes), jnp.float32)
        z_recv[8 + rows : 16 + rows, :] = jnp.zeros((8, lanes), jnp.float32)

    lane = lax.broadcasted_iota(jnp.int32, (rows, lanes), 1)
    edge = jnp.where(gz == 0, jnp.int32(lanes - 1), zero)

    d_load.wait()
    u_load.wait()
    for field, flat in enumerate((u_flat, d_flat)):
        y_send[0, field] = flat[pl.ds(8, planes, stride=pitch), :]
        y_send[1, field] = flat[pl.ds(7 + rows, planes, stride=pitch), :]

    @pl.when(gy > 0)
    def _():
        up_copy.start()

    @pl.when(gy < ny - 1)
    def _():
        down_copy.start()

    def gather_edge(i, acc):
        heat = pltpu.roll(u_pad[i, 8 : 8 + rows, :], lax.rem(i - edge + lanes, lanes), 1)
        diff = pltpu.roll(d_pad[i, 8 : 8 + rows, :], lax.rem(i + planes - edge + lanes, lanes), 1)
        acc = jnp.where(lane == i, heat, acc)
        return jnp.where(lane == i + planes, diff, acc)

    zeros = jnp.zeros((rows, lanes), jnp.float32)
    ones = jnp.ones((rows, lanes), jnp.float32)
    z_send[...] = lax.fori_loop(0, planes, gather_edge, zeros, unroll=8)
    z_copy.start()

    @pl.when(gy > 0)
    def _():
        up_corner.start()

    @pl.when(gy < ny - 1)
    def _():
        down_corner.start()

    k_load.wait()

    @pl.when(gx > 0)
    def _():
        x_copy.wait_recv()

    def homogeneous(i, state):
        a, b, c, d, before, acc = state
        here = d_pad[i, 8 : 8 + rows, :]
        step = 1.0 / (0.5 * ratio_x * (here + before))
        rho[i] = step
        a = a + step * c
        b = b + step * d
        bend = pltpu.roll(skew[i].astype(jnp.float32), lax.rem(i - edge + lanes, lanes), 1)
        return (a, b, c + a, d + b, here, jnp.where(lane == i, bend, acc))

    a, b, c, d, last, acc = lax.fori_loop(
        0, planes, homogeneous, (ones, zeros, zeros, ones, x_halo[...], zeros), unroll=4
    )
    skew_edge[...] = acc
    closing = jnp.where(gx == nx - 1, 1.0 / (0.5 * ratio_x * last), 0.0)
    inv_d = 1.0 / d
    own = (inv_d, b * inv_d + closing, c * inv_d)

    def post(at, send_buf, recv_buf, values, partner):
        for n, v in enumerate(values):
            send_buf[n] = v
        copy = remote(send_buf, recv_buf, line_send.at[at], line_recv.at[at], partner, gy, gz)
        copy.start()
        return copy

    line = [post(0, map_send.at[0], map_recv.at[0], own, partners[0])]

    @pl.when(gy > 0)
    def _():
        down_copy.wait_recv()
        down_corner.wait_recv()

    @pl.when(gy < ny - 1)
    def _():
        up_copy.wait_recv()
        up_corner.wait_recv()

    z_copy.wait_recv()
    met_heat = z_recv[8 : 8 + rows, :]
    met_diff = pltpu.roll(met_heat, lanes - planes, 1)
    own_edge = z_send[...]
    own_diff = pltpu.roll(own_edge, lanes - planes, 1)
    met_bend = z_recv[9 : 9 + rows, :] - z_recv[7 : 7 + rows, :]
    mix_sign = jnp.where(gz == 0, jnp.float32(ratio_mix), jnp.float32(-ratio_mix))
    edge_term = (0.5 * ratio_z) * (
        own_diff * met_heat + met_diff * (met_heat - own_edge)
    ) + mix_sign * skew_edge[...] * met_bend

    for field, flat in enumerate((u_flat, d_flat)):
        flat[pl.ds(7, planes, stride=pitch), :] = y_recv[0, field]
        flat[pl.ds(8 + rows, planes, stride=pitch), :] = y_recv[1, field]

    first_lane = lane == 0
    last_lane = lane == lanes - 1
    edge_lane = lane == edge

    def source(i, state):
        wp, fp = state
        heat = u_pad[i, 8 : 8 + rows, :]
        diff = d_pad[i, 8 : 8 + rows, :]
        heat_m = u_pad[i, 7 : 7 + rows, :]
        heat_p = u_pad[i, 9 : 9 + rows, :]
        flux_y = (diff + d_pad[i, 9 : 9 + rows, :]) * (heat_p - heat) - (
            diff + d_pad[i, 7 : 7 + rows, :]
        ) * (heat - heat_m)
        next_heat = jnp.where(last_lane, 0.0, pltpu.roll(heat, lanes - 1, 1))
        next_diff = jnp.where(last_lane, 0.0, pltpu.roll(diff, lanes - 1, 1))
        face = (diff + next_diff) * (next_heat - heat)
        before = jnp.where(first_lane, diff * heat, pltpu.roll(face, 1, 1))
        bend = heat_p - heat_m
        mixed = jnp.where(last_lane, 0.0, pltpu.roll(bend, lanes - 1, 1)) - jnp.where(
            first_lane, 0.0, pltpu.roll(bend, 1, 1)
        )
        extra = pltpu.roll(edge_term, lax.rem(edge - i + lanes, lanes), 1)
        side = (
            heat
            + (0.5 * ratio_y) * flux_y
            + (0.5 * ratio_z) * (face - before)
            + ratio_mix * skew[i].astype(jnp.float32) * mixed
            + jnp.where(edge_lane, extra, 0.0)
        )
        r_buf[i] = side
        wp = wp + rho[i] * fp
        return (wp, fp + (wp - side))

    half = planes // 2
    wp, fp = lax.fori_loop(0, half, source, (zeros, zeros), unroll=4)

    flags = [(gx // (1 << s)) % 2 == 1 for s in range(stages)]
    group, right = own, own
    left = (ones, zeros, zeros)
    steps = []
    for s in range(stages - 1):
        if s:
            line.append(post(s, map_send.at[s], map_recv.at[s], group, partners[s]))
        line[s].wait_recv()
        theirs = tuple(map_recv[s, n] for n in range(3))
        first = pick(flags[s], theirs, group)
        second = pick(flags[s], group, theirs)
        joined, weights = link(first, second)
        left_joined, left_weights = link(theirs, left)
        right_joined, right_weights = link(right, theirs)
        steps.append((theirs, first, second, weights, left, left_weights, right, right_weights))
        group = joined
        left = pick(flags[s], left_joined, left)
        right = pick(flags[s], right, right_joined)
    in_right = flags[-1]
    end_weight = group[0] / group[1]
    line.append(post(
        stages - 1, rel_send.at[0], rel_recv.at[0],
        (jnp.where(in_right, group[2] + group[0] * end_weight, group[1]),), partners[-1],
    ))

    wp, fp = lax.fori_loop(half, planes, source, (wp, fp), unroll=4)
    r_store = pltpu.make_async_copy(r_buf, r_hbm, store_sem.at[0])
    r_store.start()

    group_pq = (wp - b * inv_d * fp, fp * inv_d)
    left_pq, right_pq = (zeros, zeros), group_pq
    for s in range(stages - 1):
        copy = post(stages + s, pq_send.at[s], pq_recv.at[s], group_pq, partners[s])
        line.append(copy)
        theirs_map, first, second, weights, left_map, left_weights, right_map, right_weights = steps[s]
        copy.wait_recv()
        theirs = tuple(pq_recv[s, n] for n in range(2))
        first_pq = pick(flags[s], theirs, group_pq)
        second_pq = pick(flags[s], group_pq, theirs)
        left_pq = pick(
            flags[s], link_sides(left_weights, theirs_map, theirs, left_map, left_pq), left_pq
        )
        right_pq = pick(
            flags[s], right_pq, link_sides(right_weights, right_map, right_pq, theirs_map, theirs)
        )
        group_pq = link_sides(weights, first, first_pq, second, second_pq)
    copy = post(
        2 * stages - 1, rel_send.at[1], rel_recv.at[1],
        (jnp.where(in_right, group_pq[1] + end_weight * group_pq[0], group_pq[0]),), partners[-1],
    )
    line.append(copy)
    line[stages - 1].wait_recv()
    met = rel_recv[0, 0]
    z0 = jnp.where(in_right, met, 0.0)
    c0 = jnp.where(in_right, 0.0, met)
    left_in = left[0] / (1.0 + z0 * left[2])
    z_in = left[1] + left_in * left[0] * z0
    right_in = jnp.where(in_right, right[0] / right[1], right[0] / (1.0 + right[1] * c0))
    c_in = right[2] + right_in * jnp.where(in_right, right[0], right[0] * c0)
    inv_sum = 1.0 / (1.0 + z_in * c_in)
    copy.wait_recv()
    met = rel_recv[1, 0]
    e0 = jnp.where(in_right, met, 0.0)
    e_in = left_pq[0] + left_in * (e0 - z0 * left_pq[1])
    q_in = right_pq[1] + right_in * jnp.where(in_right, right_pq[0], met + c0 * right_pq[0])
    value = (e_in - z_in * q_in) * inv_sum
    flux = -(c_in * e_in + q_in) * inv_sum

    def march(i, state):
        value, flux = state
        value = value + rho[i] * flux
        w_buf[i] = value
        return (value, flux + (value - r_buf[i]))

    chunks = 4
    size = planes // chunks
    stores = []
    for n in range(chunks):
        value, flux = lax.fori_loop(n * size, (n + 1) * size, march, (value, flux), unroll=8)
        part = pl.ds(n * size, size)
        store = pltpu.make_async_copy(w_buf.at[part], w_hbm.at[part], store_sem.at[1 + n])
        store.start()
        stores.append(store)

    for copy in line:
        copy.wait_send()
    z_copy.wait_send()

    @pl.when(gx < nx - 1)
    def _():
        x_copy.wait_send()

    @pl.when(gy > 0)
    def _():
        up_copy.wait_send()
        up_corner.wait_send()

    @pl.when(gy < ny - 1)
    def _():
        down_copy.wait_send()
        down_corner.wait_send()

    r_store.wait()
    for store in stores:
        store.wait()


def body(nx, ny, nz, initial_thermal_state, thermal_spread_rate, yz_skew_factor):
    planes, rows, lanes = initial_thermal_state.shape
    stages = int(math.log2(nx))
    f32 = jnp.float32
    block = jax.ShapeDtypeStruct((planes, rows, lanes), f32)
    padded = pltpu.VMEM((planes, rows + 16, lanes), f32)
    full = pltpu.VMEM((planes, rows, lanes), f32)
    plane = pltpu.VMEM((rows, lanes), f32)
    faces = pltpu.VMEM((2, 2, planes, lanes), f32)
    maps = pltpu.VMEM((stages - 1, 3, rows, lanes), f32)
    sides = pltpu.VMEM((stages - 1, 2, rows, lanes), f32)
    relation = pltpu.VMEM((2, 1, rows, lanes), f32)
    return pl.pallas_call(
        functools.partial(kernel, nx, ny, nz),
        out_shape=(block, block),
        in_specs=[pl.BlockSpec(memory_space=pl.ANY)] * 3,
        out_specs=(pl.BlockSpec(memory_space=pl.ANY),) * 2,
        scratch_shapes=[
            padded, padded, pltpu.VMEM((planes, rows, lanes), jnp.bfloat16), full, full, full,
            plane, faces, faces, plane, pltpu.VMEM((rows + 16, lanes), f32), plane,
            maps, maps, sides, sides, relation, relation,
            pltpu.SemaphoreType.DMA((3,)),
            pltpu.SemaphoreType.DMA((5,)),
            pltpu.SemaphoreType.DMA((6,)),
            pltpu.SemaphoreType.DMA((6,)),
            pltpu.SemaphoreType.DMA((2 * stages,)),
            pltpu.SemaphoreType.DMA((2 * stages,)),
        ],
        compiler_params=pltpu.CompilerParams(
            collective_id=0, has_side_effects=True, vmem_limit_bytes=60 * 1024 * 1024
        ),
    )(initial_thermal_state, thermal_spread_rate, yz_skew_factor)


def solution(mesh):
    shape = dict(mesh.shape)
    spec = P("gx", "gy", "gz")
    return jax.shard_map(
        functools.partial(body, shape["gx"], shape["gy"], shape["gz"]),
        mesh=mesh, in_specs=(spec,) * 3, out_specs=(spec,) * 2, check_vma=False,
    )
```

```python
import functools
import math

import jax
import jax.numpy as jnp
from jax import lax
from jax.experimental import pallas as pl
from jax.experimental.pallas import tpu as pltpu
from jax.sharding import PartitionSpec as P

ratio_x = 4096.0
ratio_y = 0.2
ratio_z = 0.2
ratio_mix = 0.25
VMEM1 = 61 * 1024 * 1024 + 512 * 1024
VMEM2 = 48 * 1024 * 1024
MESH = pl.DeviceIdType.MESH


def link(first, second):
    t1, z1, c1 = first
    t2, z2, c2 = second
    k1 = t1 / (1.0 + z1 * c2)
    k2 = t2 / (1.0 + z1 * c2)
    return (k1 * t2, z2 + k2 * t2 * z1, c1 + k1 * t1 * c2), (k1, k2)


def link_sides(weights, first, first_pq, second, second_pq):
    k1, k2 = weights
    p1, q1 = first_pq
    p2, q2 = second_pq
    return (p2 + k2 * (p1 - first[1] * q2), q1 + k1 * (q2 + second[2] * p1))


def pick(flag, yes, no):
    return tuple(jnp.where(flag, s, t) for s, t in zip(yes, no))


def kernel(
    nx, ny, nz, u_hbm, d_hbm, k_hbm, r_buf, rho, start,
    u_pad, d_pad, skew,
    x_halo, y_send, y_recv, z_send, z_recv, skew_edge,
    map_send, map_recv, pq_send, pq_recv, rel_send, rel_recv,
    load_sem, halo_send, halo_recv, line_send, line_recv,
):
    planes, rows, lanes = u_hbm.shape
    stages = int(math.log2(nx))
    gx, gy, gz = lax.axis_index("gx"), lax.axis_index("gy"), lax.axis_index("gz")
    other_z = 1 - gz
    pitch = rows + 16
    body_rows = pl.ds(8, rows)
    u_flat = u_pad.reshape(planes * pitch, lanes)
    d_flat = d_pad.reshape(planes * pitch, lanes)

    d_load = pltpu.make_async_copy(d_hbm, d_pad.at[:, body_rows, :], load_sem.at[0])
    u_load = pltpu.make_async_copy(u_hbm, u_pad.at[:, body_rows, :], load_sem.at[1])
    k_load = pltpu.make_async_copy(k_hbm, skew, load_sem.at[2])
    d_load.start()
    u_load.start()
    k_load.start()

    barrier = pltpu.get_barrier_semaphore()

    def greet(x, y, z):
        pl.semaphore_signal(barrier, inc=1, device_id=(x, y, z), device_id_type=MESH)

    partners = [gx + (1 << s) - 2 * (1 << s) * ((gx // (1 << s)) % 2) for s in range(stages)]
    for x in partners:
        greet(x, gy, gz)
    greet(gx, gy, other_z)

    @pl.when(gx > 0)
    def _():
        greet(gx - 1, gy, gz)

    @pl.when(gy > 0)
    def _():
        greet(gx, gy - 1, gz)
        greet(gx, gy - 1, other_z)

    @pl.when(gy < ny - 1)
    def _():
        greet(gx, gy + 1, gz)
        greet(gx, gy + 1, other_z)

    one = jnp.int32(1)
    zero = jnp.int32(0)
    awaited = (
        stages + 1
        + jnp.where(gx < nx - 1, one, zero)
        + 2 * jnp.where(gy > 0, one, zero)
        + 2 * jnp.where(gy < ny - 1, one, zero)
    )

    def remote(src, dst, send, recv, x, y, z):
        return pltpu.make_async_remote_copy(
            src_ref=src, dst_ref=dst, send_sem=send, recv_sem=recv,
            device_id=(x, y, z), device_id_type=MESH,
        )

    x_copy = remote(
        d_hbm.at[planes - 1], x_halo, halo_send.at[0], halo_recv.at[0], gx + 1, gy, gz
    )
    up_copy = remote(y_send.at[0], y_recv.at[1], halo_send.at[1], halo_recv.at[1], gx, gy - 1, gz)
    down_copy = remote(y_send.at[1], y_recv.at[0], halo_send.at[2], halo_recv.at[2], gx, gy + 1, gz)
    z_copy = remote(
        z_send, z_recv.at[pl.ds(8, rows), :], halo_send.at[3], halo_recv.at[3], gx, gy, other_z
    )
    up_corner = remote(
        z_send.at[pl.ds(0, 8), :], z_recv.at[pl.ds(8 + rows, 8), :],
        halo_send.at[4], halo_recv.at[4], gx, gy - 1, other_z,
    )
    down_corner = remote(
        z_send.at[pl.ds(rows - 8, 8), :], z_recv.at[pl.ds(0, 8), :],
        halo_send.at[5], halo_recv.at[5], gx, gy + 1, other_z,
    )

    pl.semaphore_wait(barrier, awaited)

    @pl.when(gx < nx - 1)
    def _():
        x_copy.start()

    @pl.when(gx == 0)
    def _():
        x_halo[...] = jnp.zeros((rows, lanes), jnp.float32)

    @pl.when(gy == 0)
    def _():
        y_recv[0] = jnp.zeros((2, planes, lanes), jnp.float32)
        z_recv[0:8, :] = jnp.zeros((8, lanes), jnp.float32)

    @pl.when(gy == ny - 1)
    def _():
        y_recv[1] = jnp.zeros((2, planes, lanes), jnp.float32)
        z_recv[8 + rows : 16 + rows, :] = jnp.zeros((8, lanes), jnp.float32)

    lane = lax.broadcasted_iota(jnp.int32, (rows, lanes), 1)
    edge = jnp.where(gz == 0, jnp.int32(lanes - 1), zero)

    d_load.wait()
    u_load.wait()
    for field, flat in enumerate((u_flat, d_flat)):
        y_send[0, field] = flat[pl.ds(8, planes, stride=pitch), :]
        y_send[1, field] = flat[pl.ds(7 + rows, planes, stride=pitch), :]

    @pl.when(gy > 0)
    def _():
        up_copy.start()

    @pl.when(gy < ny - 1)
    def _():
        down_copy.start()

    def gather_edge(i, acc):
        heat = pltpu.roll(u_pad[i, 8 : 8 + rows, :], lax.rem(i - edge + lanes, lanes), 1)
        diff = pltpu.roll(d_pad[i, 8 : 8 + rows, :], lax.rem(i + planes - edge + lanes, lanes), 1)
        acc = jnp.where(lane == i, heat, acc)
        return jnp.where(lane == i + planes, diff, acc)

    zeros = jnp.zeros((rows, lanes), jnp.float32)
    ones = jnp.ones((rows, lanes), jnp.float32)
    z_send[...] = lax.fori_loop(0, planes, gather_edge, zeros, unroll=8)
    z_copy.start()

    @pl.when(gy > 0)
    def _():
        up_corner.start()

    @pl.when(gy < ny - 1)
    def _():
        down_corner.start()

    k_load.wait()

    @pl.when(gx > 0)
    def _():
        x_copy.wait_recv()

    def homogeneous(i, state):
        a, b, c, d, before, acc = state
        here = d_pad[i, 8 : 8 + rows, :]
        step = 1.0 / (0.5 * ratio_x * (here + before))
        rho[i] = step
        a = a + step * c
        b = b + step * d
        bend = pltpu.roll(skew[i].astype(jnp.float32), lax.rem(i - edge + lanes, lanes), 1)
        return (a, b, c + a, d + b, here, jnp.where(lane == i, bend, acc))

    a, b, c, d, last, acc = lax.fori_loop(
        0, planes, homogeneous, (ones, zeros, zeros, ones, x_halo[...], zeros), unroll=4
    )
    skew_edge[...] = acc
    closing = jnp.where(gx == nx - 1, 1.0 / (0.5 * ratio_x * last), 0.0)
    inv_d = 1.0 / d
    own = (inv_d, b * inv_d + closing, c * inv_d)

    def post(at, send_buf, recv_buf, values, partner):
        for n, v in enumerate(values):
            send_buf[n] = v
        copy = remote(send_buf, recv_buf, line_send.at[at], line_recv.at[at], partner, gy, gz)
        copy.start()
        return copy

    line = [post(0, map_send.at[0], map_recv.at[0], own, partners[0])]

    @pl.when(gy > 0)
    def _():
        down_copy.wait_recv()
        down_corner.wait_recv()

    @pl.when(gy < ny - 1)
    def _():
        up_copy.wait_recv()
        up_corner.wait_recv()

    z_copy.wait_recv()
    met_heat = z_recv[8 : 8 + rows, :]
    met_diff = pltpu.roll(met_heat, lanes - planes, 1)
    own_edge = z_send[...]
    own_diff = pltpu.roll(own_edge, lanes - planes, 1)
    met_bend = z_recv[9 : 9 + rows, :] - z_recv[7 : 7 + rows, :]
    mix_sign = jnp.where(gz == 0, jnp.float32(ratio_mix), jnp.float32(-ratio_mix))
    edge_term = (0.5 * ratio_z) * (
        own_diff * met_heat + met_diff * (met_heat - own_edge)
    ) + mix_sign * skew_edge[...] * met_bend

    for field, flat in enumerate((u_flat, d_flat)):
        flat[pl.ds(7, planes, stride=pitch), :] = y_recv[0, field]
        flat[pl.ds(8 + rows, planes, stride=pitch), :] = y_recv[1, field]

    first_lane = lane == 0
    last_lane = lane == lanes - 1
    edge_lane = lane == edge

    def source(i, state):
        wp, fp = state
        heat = u_pad[i, 8 : 8 + rows, :]
        diff = d_pad[i, 8 : 8 + rows, :]
        heat_m = u_pad[i, 7 : 7 + rows, :]
        heat_p = u_pad[i, 9 : 9 + rows, :]
        flux_y = (diff + d_pad[i, 9 : 9 + rows, :]) * (heat_p - heat) - (
            diff + d_pad[i, 7 : 7 + rows, :]
        ) * (heat - heat_m)
        next_heat = jnp.where(last_lane, 0.0, pltpu.roll(heat, lanes - 1, 1))
        next_diff = jnp.where(last_lane, 0.0, pltpu.roll(diff, lanes - 1, 1))
        face = (diff + next_diff) * (next_heat - heat)
        before = jnp.where(first_lane, diff * heat, pltpu.roll(face, 1, 1))
        bend = heat_p - heat_m
        mixed = jnp.where(last_lane, 0.0, pltpu.roll(bend, lanes - 1, 1)) - jnp.where(
            first_lane, 0.0, pltpu.roll(bend, 1, 1)
        )
        extra = pltpu.roll(edge_term, lax.rem(edge - i + lanes, lanes), 1)
        side = (
            heat
            + (0.5 * ratio_y) * flux_y
            + (0.5 * ratio_z) * (face - before)
            + ratio_mix * skew[i].astype(jnp.float32) * mixed
            + jnp.where(edge_lane, extra, 0.0)
        )
        r_buf[i] = side
        wp = wp + rho[i] * fp
        return (wp, fp + (wp - side))

    half = planes // 2
    wp, fp = lax.fori_loop(0, half, source, (zeros, zeros), unroll=4)

    flags = [(gx // (1 << s)) % 2 == 1 for s in range(stages)]
    group, right = own, own
    left = (ones, zeros, zeros)
    steps = []
    for s in range(stages - 1):
        if s:
            line.append(post(s, map_send.at[s], map_recv.at[s], group, partners[s]))
        line[s].wait_recv()
        theirs = tuple(map_recv[s, n] for n in range(3))
        first = pick(flags[s], theirs, group)
        second = pick(flags[s], group, theirs)
        joined, weights = link(first, second)
        left_joined, left_weights = link(theirs, left)
        right_joined, right_weights = link(right, theirs)
        steps.append((theirs, first, second, weights, left, left_weights, right, right_weights))
        group = joined
        left = pick(flags[s], left_joined, left)
        right = pick(flags[s], right, right_joined)
    in_right = flags[-1]
    end_weight = group[0] / group[1]
    line.append(post(
        stages - 1, rel_send.at[0], rel_recv.at[0],
        (jnp.where(in_right, group[2] + group[0] * end_weight, group[1]),), partners[-1],
    ))

    wp, fp = lax.fori_loop(half, planes, source, (wp, fp), unroll=4)
    group_pq = (wp - b * inv_d * fp, fp * inv_d)
    left_pq, right_pq = (zeros, zeros), group_pq
    for s in range(stages - 1):
        copy = post(stages + s, pq_send.at[s], pq_recv.at[s], group_pq, partners[s])
        line.append(copy)
        theirs_map, first, second, weights, left_map, left_weights, right_map, right_weights = steps[s]
        copy.wait_recv()
        theirs = tuple(pq_recv[s, n] for n in range(2))
        first_pq = pick(flags[s], theirs, group_pq)
        second_pq = pick(flags[s], group_pq, theirs)
        left_pq = pick(
            flags[s], link_sides(left_weights, theirs_map, theirs, left_map, left_pq), left_pq
        )
        right_pq = pick(
            flags[s], right_pq, link_sides(right_weights, right_map, right_pq, theirs_map, theirs)
        )
        group_pq = link_sides(weights, first, first_pq, second, second_pq)
    copy = post(
        2 * stages - 1, rel_send.at[1], rel_recv.at[1],
        (jnp.where(in_right, group_pq[1] + end_weight * group_pq[0], group_pq[0]),), partners[-1],
    )
    line.append(copy)
    line[stages - 1].wait_recv()
    met = rel_recv[0, 0]
    z0 = jnp.where(in_right, met, 0.0)
    c0 = jnp.where(in_right, 0.0, met)
    left_in = left[0] / (1.0 + z0 * left[2])
    z_in = left[1] + left_in * left[0] * z0
    right_in = jnp.where(in_right, right[0] / right[1], right[0] / (1.0 + right[1] * c0))
    c_in = right[2] + right_in * jnp.where(in_right, right[0], right[0] * c0)
    inv_sum = 1.0 / (1.0 + z_in * c_in)
    copy.wait_recv()
    met = rel_recv[1, 0]
    e0 = jnp.where(in_right, met, 0.0)
    e_in = left_pq[0] + left_in * (e0 - z0 * left_pq[1])
    q_in = right_pq[1] + right_in * jnp.where(in_right, right_pq[0], met + c0 * right_pq[0])
    value = (e_in - z_in * q_in) * inv_sum
    flux = -(c_in * e_in + q_in) * inv_sum

    start[0] = value
    start[1] = flux

    for copy in line:
        copy.wait_send()
    z_copy.wait_send()

    @pl.when(gx < nx - 1)
    def _():
        x_copy.wait_send()

    @pl.when(gy > 0)
    def _():
        up_copy.wait_send()
        up_corner.wait_send()

    @pl.when(gy < ny - 1)
    def _():
        down_copy.wait_send()
        down_corner.wait_send()


def march_kernel(r_buf, rho, start, r_hbm, w_hbm, w_buf, store_sem):
    planes = r_buf.shape[0]
    r_store = pltpu.make_async_copy(r_buf, r_hbm, store_sem.at[0])
    r_store.start()

    def march(i, state):
        value, flux = state
        value = value + rho[i] * flux
        w_buf[i] = value
        return (value, flux + (value - r_buf[i]))

    chunks = 4
    size = planes // chunks
    stores = []
    state = (start[0], start[1])
    for n in range(chunks):
        state = lax.fori_loop(n * size, (n + 1) * size, march, state, unroll=8)
        part = pl.ds(n * size, size)
        store = pltpu.make_async_copy(w_buf.at[part], w_hbm.at[part], store_sem.at[1 + n])
        store.start()
        stores.append(store)
    r_store.wait()
    for store in stores:
        store.wait()


def body(nx, ny, nz, initial_thermal_state, thermal_spread_rate, yz_skew_factor):
    planes, rows, lanes = initial_thermal_state.shape
    stages = int(math.log2(nx))
    f32 = jnp.float32
    block = jax.ShapeDtypeStruct((planes, rows, lanes), f32)
    padded = pltpu.VMEM((planes, rows + 16, lanes), f32)
    full = pltpu.VMEM((planes, rows, lanes), f32)
    plane = pltpu.VMEM((rows, lanes), f32)
    faces = pltpu.VMEM((2, 2, planes, lanes), f32)
    maps = pltpu.VMEM((stages - 1, 3, rows, lanes), f32)
    sides = pltpu.VMEM((stages - 1, 2, rows, lanes), f32)
    relation = pltpu.VMEM((2, 1, rows, lanes), f32)
    r, rho, start = pl.pallas_call(
        functools.partial(kernel, nx, ny, nz),
        out_shape=(full, full, pltpu.VMEM((2, rows, lanes), f32)),
        in_specs=[pl.BlockSpec(memory_space=pltpu.HBM)] * 3,
        out_specs=(pl.BlockSpec(memory_space=pltpu.VMEM),) * 3,
        scratch_shapes=[
            padded, padded, pltpu.VMEM((planes, rows, lanes), jnp.bfloat16),
            plane, faces, faces, plane, pltpu.VMEM((rows + 16, lanes), f32), plane,
            maps, maps, sides, sides, relation, relation,
            pltpu.SemaphoreType.DMA((3,)),
            pltpu.SemaphoreType.DMA((6,)),
            pltpu.SemaphoreType.DMA((6,)),
            pltpu.SemaphoreType.DMA((2 * stages,)),
            pltpu.SemaphoreType.DMA((2 * stages,)),
        ],
        compiler_params=pltpu.CompilerParams(
            collective_id=0, has_side_effects=True, vmem_limit_bytes=VMEM1
        ),
    )(initial_thermal_state, thermal_spread_rate, yz_skew_factor)
    return pl.pallas_call(
        march_kernel,
        out_shape=(block, block),
        in_specs=[pl.BlockSpec(memory_space=pltpu.VMEM)] * 3,
        out_specs=(pl.BlockSpec(memory_space=pl.ANY),) * 2,
        scratch_shapes=[full, pltpu.SemaphoreType.DMA((5,))],
        compiler_params=pltpu.CompilerParams(vmem_limit_bytes=VMEM2),
    )(r, rho, start)


def solution(mesh):
    shape = dict(mesh.shape)
    spec = P("gx", "gy", "gz")
    return jax.shard_map(
        functools.partial(body, shape["gx"], shape["gy"], shape["gz"]),
        mesh=mesh, in_specs=(spec,) * 3, out_specs=(spec,) * 2, check_vma=False,
    )
```

```python
import functools
import math

import jax
import jax.numpy as jnp
from jax import lax
from jax.experimental import pallas as pl
from jax.experimental.pallas import tpu as pltpu
from jax.sharding import PartitionSpec as P

ratio_x = 4096.0
ratio_y = 0.2
ratio_z = 0.2
ratio_mix = 0.25
VMEM1 = 61 * 1024 * 1024 + 512 * 1024
VMEM2 = 48 * 1024 * 1024
MESH = pl.DeviceIdType.MESH


def link(first, second):
    t1, z1, c1 = first
    t2, z2, c2 = second
    k1 = t1 / (1.0 + z1 * c2)
    k2 = t2 / (1.0 + z1 * c2)
    return (k1 * t2, z2 + k2 * t2 * z1, c1 + k1 * t1 * c2), (k1, k2)


def link_sides(weights, first, first_pq, second, second_pq):
    k1, k2 = weights
    p1, q1 = first_pq
    p2, q2 = second_pq
    return (p2 + k2 * (p1 - first[1] * q2), q1 + k1 * (q2 + second[2] * p1))


def pick(flag, yes, no):
    return tuple(jnp.where(flag, s, t) for s, t in zip(yes, no))


def kernel(
    nx, ny, nz, u_hbm, d_hbm, k_hbm, r_buf, rho, start,
    u_pad, d_pad, skew,
    x_halo, y_send, y_recv, z_send, z_recv, skew_edge,
    map_send, map_recv, pq_send, pq_recv, rel_send, rel_recv,
    load_sem, halo_send, halo_recv, line_send, line_recv,
):
    planes, rows, lanes = u_hbm.shape
    stages = int(math.log2(nx))
    gx, gy, gz = lax.axis_index("gx"), lax.axis_index("gy"), lax.axis_index("gz")
    other_z = 1 - gz
    pitch = rows + 16
    body_rows = pl.ds(8, rows)
    u_flat = u_pad.reshape(planes * pitch, lanes)
    d_flat = d_pad.reshape(planes * pitch, lanes)

    d_load = pltpu.make_async_copy(d_hbm, d_pad.at[:, body_rows, :], load_sem.at[0])
    u_load = pltpu.make_async_copy(u_hbm, u_pad.at[:, body_rows, :], load_sem.at[1])
    k_load = pltpu.make_async_copy(k_hbm, skew, load_sem.at[2])
    d_load.start()
    u_load.start()
    k_load.start()

    barrier = pltpu.get_barrier_semaphore()

    def greet(x, y, z):
        pl.semaphore_signal(barrier, inc=1, device_id=(x, y, z), device_id_type=MESH)

    partners = [gx + (1 << s) - 2 * (1 << s) * ((gx // (1 << s)) % 2) for s in range(stages)]
    for x in partners:
        greet(x, gy, gz)
    greet(gx, gy, other_z)

    @pl.when(gx > 0)
    def _():
        greet(gx - 1, gy, gz)

    @pl.when(gy > 0)
    def _():
        greet(gx, gy - 1, gz)
        greet(gx, gy - 1, other_z)

    @pl.when(gy < ny - 1)
    def _():
        greet(gx, gy + 1, gz)
        greet(gx, gy + 1, other_z)

    one = jnp.int32(1)
    zero = jnp.int32(0)
    awaited = (
        stages + 1
        + jnp.where(gx < nx - 1, one, zero)
        + 2 * jnp.where(gy > 0, one, zero)
        + 2 * jnp.where(gy < ny - 1, one, zero)
    )

    def remote(src, dst, send, recv, x, y, z):
        return pltpu.make_async_remote_copy(
            src_ref=src, dst_ref=dst, send_sem=send, recv_sem=recv,
            device_id=(x, y, z), device_id_type=MESH,
        )

    x_copy = remote(
        d_hbm.at[planes - 1], x_halo, halo_send.at[0], halo_recv.at[0], gx + 1, gy, gz
    )
    up_copy = remote(y_send.at[0], y_recv.at[1], halo_send.at[1], halo_recv.at[1], gx, gy - 1, gz)
    down_copy = remote(y_send.at[1], y_recv.at[0], halo_send.at[2], halo_recv.at[2], gx, gy + 1, gz)
    z_copy = remote(
        z_send, z_recv.at[pl.ds(8, rows), :], halo_send.at[3], halo_recv.at[3], gx, gy, other_z
    )
    up_corner = remote(
        z_send.at[pl.ds(0, 8), :], z_recv.at[pl.ds(8 + rows, 8), :],
        halo_send.at[4], halo_recv.at[4], gx, gy - 1, other_z,
    )
    down_corner = remote(
        z_send.at[pl.ds(rows - 8, 8), :], z_recv.at[pl.ds(0, 8), :],
        halo_send.at[5], halo_recv.at[5], gx, gy + 1, other_z,
    )

    @pl.when(gx == 0)
    def _():
        x_halo[...] = jnp.zeros((rows, lanes), jnp.float32)

    @pl.when(gy == 0)
    def _():
        y_recv[0] = jnp.zeros((2, planes, lanes), jnp.float32)
        z_recv[0:8, :] = jnp.zeros((8, lanes), jnp.float32)

    @pl.when(gy == ny - 1)
    def _():
        y_recv[1] = jnp.zeros((2, planes, lanes), jnp.float32)
        z_recv[8 + rows : 16 + rows, :] = jnp.zeros((8, lanes), jnp.float32)

    lane = lax.broadcasted_iota(jnp.int32, (rows, lanes), 1)
    edge = jnp.where(gz == 0, jnp.int32(lanes - 1), zero)

    zeros = jnp.zeros((rows, lanes), jnp.float32)
    ones = jnp.ones((rows, lanes), jnp.float32)

    def gather_edge(pad, place):
        def one_plane(i, acc):
            turned = pltpu.roll(
                pad[i, 8 : 8 + rows, :], lax.rem(i + place - edge + lanes, lanes), 1
            )
            return jnp.where(lane == i + place, turned, acc)

        return one_plane

    acc = zeros
    for field, load, pad, flat in ((1, d_load, d_pad, d_flat), (0, u_load, u_pad, u_flat)):
        load.wait()
        y_send[0, field] = flat[pl.ds(8, planes, stride=pitch), :]
        y_send[1, field] = flat[pl.ds(7 + rows, planes, stride=pitch), :]
        acc = lax.fori_loop(0, planes, gather_edge(pad, field * planes), acc, unroll=8)
    z_send[...] = acc

    pl.semaphore_wait(barrier, awaited)
    z_copy.start()

    @pl.when(gy > 0)
    def _():
        up_copy.start()
        up_corner.start()

    @pl.when(gy < ny - 1)
    def _():
        down_copy.start()
        down_corner.start()

    @pl.when(gx < nx - 1)
    def _():
        x_copy.start()

    k_load.wait()

    def bent(i, acc):
        bend = pltpu.roll(skew[i].astype(jnp.float32), lax.rem(i - edge + lanes, lanes), 1)
        return jnp.where(lane == i, bend, acc)

    def homogeneous(i, state):
        a, b, c, d, before, acc = state
        here = d_pad[i, 8 : 8 + rows, :]
        step = 1.0 / (0.5 * ratio_x * (here + before))
        rho[i] = step
        a = a + step * c
        b = b + step * d
        return (a, b, c + a, d + b, here, bent(i, acc))

    lead = d_pad[0, 8 : 8 + rows, :]
    a, b, c, d, last, acc = lax.fori_loop(
        1, planes, homogeneous, (ones, zeros, ones, ones, lead, bent(0, zeros)), unroll=7
    )
    skew_edge[...] = acc

    @pl.when(gx > 0)
    def _():
        x_copy.wait_recv()

    step = 1.0 / (0.5 * ratio_x * (lead + x_halo[...]))
    rho[0] = step
    b = b + a * step
    d = d + c * step
    closing = jnp.where(gx == nx - 1, 1.0 / (0.5 * ratio_x * last), 0.0)
    inv_d = 1.0 / d
    own = (inv_d, b * inv_d + closing, c * inv_d)

    def post(at, send_buf, recv_buf, values, partner):
        for n, v in enumerate(values):
            send_buf[n] = v
        copy = remote(send_buf, recv_buf, line_send.at[at], line_recv.at[at], partner, gy, gz)
        copy.start()
        return copy

    line = [post(0, map_send.at[0], map_recv.at[0], own, partners[0])]

    @pl.when(gy > 0)
    def _():
        down_copy.wait_recv()
        down_corner.wait_recv()

    @pl.when(gy < ny - 1)
    def _():
        up_copy.wait_recv()
        up_corner.wait_recv()

    z_copy.wait_recv()
    met_heat = z_recv[8 : 8 + rows, :]
    met_diff = pltpu.roll(met_heat, lanes - planes, 1)
    own_edge = z_send[...]
    own_diff = pltpu.roll(own_edge, lanes - planes, 1)
    met_bend = z_recv[9 : 9 + rows, :] - z_recv[7 : 7 + rows, :]
    mix_sign = jnp.where(gz == 0, jnp.float32(ratio_mix), jnp.float32(-ratio_mix))
    edge_term = (0.5 * ratio_z) * (
        own_diff * met_heat + met_diff * (met_heat - own_edge)
    ) + mix_sign * skew_edge[...] * met_bend

    for field, flat in enumerate((u_flat, d_flat)):
        flat[pl.ds(7, planes, stride=pitch), :] = y_recv[0, field]
        flat[pl.ds(8 + rows, planes, stride=pitch), :] = y_recv[1, field]

    first_lane = lane == 0
    last_lane = lane == lanes - 1
    edge_lane = lane == edge

    def source(i, state):
        wp, fp = state
        heat = u_pad[i, 8 : 8 + rows, :]
        diff = d_pad[i, 8 : 8 + rows, :]
        heat_m = u_pad[i, 7 : 7 + rows, :]
        heat_p = u_pad[i, 9 : 9 + rows, :]
        flux_y = (diff + d_pad[i, 9 : 9 + rows, :]) * (heat_p - heat) - (
            diff + d_pad[i, 7 : 7 + rows, :]
        ) * (heat - heat_m)
        next_heat = jnp.where(last_lane, 0.0, pltpu.roll(heat, lanes - 1, 1))
        next_diff = jnp.where(last_lane, 0.0, pltpu.roll(diff, lanes - 1, 1))
        face = (diff + next_diff) * (next_heat - heat)
        before = jnp.where(first_lane, diff * heat, pltpu.roll(face, 1, 1))
        bend = heat_p - heat_m
        mixed = jnp.where(last_lane, 0.0, pltpu.roll(bend, lanes - 1, 1)) - jnp.where(
            first_lane, 0.0, pltpu.roll(bend, 1, 1)
        )
        extra = pltpu.roll(edge_term, lax.rem(edge - i + lanes, lanes), 1)
        side = (
            heat
            + (0.5 * ratio_y) * flux_y
            + (0.5 * ratio_z) * (face - before)
            + ratio_mix * skew[i].astype(jnp.float32) * mixed
            + jnp.where(edge_lane, extra, 0.0)
        )
        r_buf[i] = side
        wp = wp + rho[i] * fp
        return (wp, fp + (wp - side))

    half = planes // 2
    wp, fp = lax.fori_loop(0, half, source, (zeros, zeros), unroll=4)

    flags = [(gx // (1 << s)) % 2 == 1 for s in range(stages)]
    group, right = own, own
    left = (ones, zeros, zeros)
    steps = []
    for s in range(stages - 1):
        if s:
            line.append(post(s, map_send.at[s], map_recv.at[s], group, partners[s]))
        line[s].wait_recv()
        theirs = tuple(map_recv[s, n] for n in range(3))
        first = pick(flags[s], theirs, group)
        second = pick(flags[s], group, theirs)
        joined, weights = link(first, second)
        left_joined, left_weights = link(theirs, left)
        right_joined, right_weights = link(right, theirs)
        steps.append((theirs, first, second, weights, left, left_weights, right, right_weights))
        group = joined
        left = pick(flags[s], left_joined, left)
        right = pick(flags[s], right, right_joined)
    in_right = flags[-1]
    end_weight = group[0] / group[1]
    line.append(post(
        stages - 1, rel_send.at[0], rel_recv.at[0],
        (jnp.where(in_right, group[2] + group[0] * end_weight, group[1]),), partners[-1],
    ))

    wp, fp = lax.fori_loop(half, planes, source, (wp, fp), unroll=4)
    group_pq = (wp - b * inv_d * fp, fp * inv_d)
    left_pq, right_pq = (zeros, zeros), group_pq
    for s in range(stages - 1):
        copy = post(stages + s, pq_send.at[s], pq_recv.at[s], group_pq, partners[s])
        line.append(copy)
        theirs_map, first, second, weights, left_map, left_weights, right_map, right_weights = steps[s]
        copy.wait_recv()
        theirs = tuple(pq_recv[s, n] for n in range(2))
        first_pq = pick(flags[s], theirs, group_pq)
        second_pq = pick(flags[s], group_pq, theirs)
        left_pq = pick(
            flags[s], link_sides(left_weights, theirs_map, theirs, left_map, left_pq), left_pq
        )
        right_pq = pick(
            flags[s], right_pq, link_sides(right_weights, right_map, right_pq, theirs_map, theirs)
        )
        group_pq = link_sides(weights, first, first_pq, second, second_pq)
    copy = post(
        2 * stages - 1, rel_send.at[1], rel_recv.at[1],
        (jnp.where(in_right, group_pq[1] + end_weight * group_pq[0], group_pq[0]),), partners[-1],
    )
    line.append(copy)
    line[stages - 1].wait_recv()
    met = rel_recv[0, 0]
    z0 = jnp.where(in_right, met, 0.0)
    c0 = jnp.where(in_right, 0.0, met)
    left_in = left[0] / (1.0 + z0 * left[2])
    z_in = left[1] + left_in * left[0] * z0
    right_in = jnp.where(in_right, right[0] / right[1], right[0] / (1.0 + right[1] * c0))
    c_in = right[2] + right_in * jnp.where(in_right, right[0], right[0] * c0)
    inv_sum = 1.0 / (1.0 + z_in * c_in)
    copy.wait_recv()
    met = rel_recv[1, 0]
    e0 = jnp.where(in_right, met, 0.0)
    e_in = left_pq[0] + left_in * (e0 - z0 * left_pq[1])
    q_in = right_pq[1] + right_in * jnp.where(in_right, right_pq[0], met + c0 * right_pq[0])
    value = (e_in - z_in * q_in) * inv_sum
    flux = -(c_in * e_in + q_in) * inv_sum

    start[0] = value
    start[1] = flux

    for copy in line:
        copy.wait_send()
    z_copy.wait_send()

    @pl.when(gx < nx - 1)
    def _():
        x_copy.wait_send()

    @pl.when(gy > 0)
    def _():
        up_copy.wait_send()
        up_corner.wait_send()

    @pl.when(gy < ny - 1)
    def _():
        down_copy.wait_send()
        down_corner.wait_send()


def march_kernel(r_buf, rho, start, r_hbm, w_hbm, w_buf, store_sem):
    planes = r_buf.shape[0]
    r_store = pltpu.make_async_copy(r_buf, r_hbm, store_sem.at[0])
    r_store.start()

    def march(i, state):
        value, flux = state
        value = value + rho[i] * flux
        w_buf[i] = value
        return (value, flux + (value - r_buf[i]))

    chunks = 4
    size = planes // chunks
    stores = []
    state = (start[0], start[1])
    for n in range(chunks):
        state = lax.fori_loop(n * size, (n + 1) * size, march, state, unroll=8)
        part = pl.ds(n * size, size)
        store = pltpu.make_async_copy(w_buf.at[part], w_hbm.at[part], store_sem.at[1 + n])
        store.start()
        stores.append(store)
    r_store.wait()
    for store in stores:
        store.wait()


def body(nx, ny, nz, initial_thermal_state, thermal_spread_rate, yz_skew_factor):
    planes, rows, lanes = initial_thermal_state.shape
    stages = int(math.log2(nx))
    f32 = jnp.float32
    block = jax.ShapeDtypeStruct((planes, rows, lanes), f32)
    padded = pltpu.VMEM((planes, rows + 16, lanes), f32)
    full = pltpu.VMEM((planes, rows, lanes), f32)
    plane = pltpu.VMEM((rows, lanes), f32)
    faces = pltpu.VMEM((2, 2, planes, lanes), f32)
    maps = pltpu.VMEM((stages - 1, 3, rows, lanes), f32)
    sides = pltpu.VMEM((stages - 1, 2, rows, lanes), f32)
    relation = pltpu.VMEM((2, 1, rows, lanes), f32)
    r, rho, start = pl.pallas_call(
        functools.partial(kernel, nx, ny, nz),
        out_shape=(full, full, pltpu.VMEM((2, rows, lanes), f32)),
        in_specs=[pl.BlockSpec(memory_space=pltpu.HBM)] * 3,
        out_specs=(pl.BlockSpec(memory_space=pltpu.VMEM),) * 3,
        scratch_shapes=[
            padded, padded, pltpu.VMEM((planes, rows, lanes), jnp.bfloat16),
            plane, faces, faces, plane, pltpu.VMEM((rows + 16, lanes), f32), plane,
            maps, maps, sides, sides, relation, relation,
            pltpu.SemaphoreType.DMA((3,)),
            pltpu.SemaphoreType.DMA((6,)),
            pltpu.SemaphoreType.DMA((6,)),
            pltpu.SemaphoreType.DMA((2 * stages,)),
            pltpu.SemaphoreType.DMA((2 * stages,)),
        ],
        compiler_params=pltpu.CompilerParams(
            collective_id=0, has_side_effects=True, vmem_limit_bytes=VMEM1
        ),
    )(initial_thermal_state, thermal_spread_rate, yz_skew_factor)
    return pl.pallas_call(
        march_kernel,
        out_shape=(block, block),
        in_specs=[pl.BlockSpec(memory_space=pltpu.VMEM)] * 3,
        out_specs=(pl.BlockSpec(memory_space=pl.ANY),) * 2,
        scratch_shapes=[full, pltpu.SemaphoreType.DMA((5,))],
        compiler_params=pltpu.CompilerParams(vmem_limit_bytes=VMEM2),
    )(r, rho, start)


def solution(mesh):
    shape = dict(mesh.shape)
    spec = P("gx", "gy", "gz")
    return jax.shard_map(
        functools.partial(body, shape["gx"], shape["gy"], shape["gz"]),
        mesh=mesh, in_specs=(spec,) * 3, out_specs=(spec,) * 2, check_vma=False,
    )
```

```python
import functools
import math

import jax
import jax.numpy as jnp
from jax import lax
from jax.experimental import pallas as pl
from jax.experimental.pallas import tpu as pltpu
from jax.sharding import PartitionSpec as P

ratio_x = 4096.0
ratio_y = 0.2
ratio_z = 0.2
ratio_mix = 0.25
VMEM1 = 61 * 1024 * 1024 + 512 * 1024
VMEM2 = 48 * 1024 * 1024
MESH = pl.DeviceIdType.MESH


def link(first, second):
    t1, z1, c1 = first
    t2, z2, c2 = second
    k1 = t1 / (1.0 + z1 * c2)
    k2 = t2 / (1.0 + z1 * c2)
    return (k1 * t2, z2 + k2 * t2 * z1, c1 + k1 * t1 * c2), (k1, k2)


def link_sides(weights, first, first_pq, second, second_pq):
    k1, k2 = weights
    p1, q1 = first_pq
    p2, q2 = second_pq
    return (p2 + k2 * (p1 - first[1] * q2), q1 + k1 * (q2 + second[2] * p1))


def pick(flag, yes, no):
    return tuple(jnp.where(flag, s, t) for s, t in zip(yes, no))


def kernel(
    nx, ny, nz, u_hbm, d_hbm, k_hbm, r_buf, rho, start,
    u_pad, d_pad, skew,
    x_halo, y_send, y_recv, z_send, z_recv, skew_edge,
    map_send, map_recv, pq_send, pq_recv, rel_send, rel_recv,
    load_sem, halo_send, halo_recv, line_send, line_recv,
):
    planes, rows, lanes = u_hbm.shape
    stages = int(math.log2(nx))
    gx, gy, gz = lax.axis_index("gx"), lax.axis_index("gy"), lax.axis_index("gz")
    other_z = 1 - gz
    pitch = rows + 16
    body_rows = pl.ds(8, rows)
    u_flat = u_pad.reshape(planes * pitch, lanes)
    d_flat = d_pad.reshape(planes * pitch, lanes)

    d_load = pltpu.make_async_copy(d_hbm, d_pad.at[:, body_rows, :], load_sem.at[0])
    u_load = pltpu.make_async_copy(u_hbm, u_pad.at[:, body_rows, :], load_sem.at[1])
    k_load = pltpu.make_async_copy(k_hbm, skew, load_sem.at[2])
    d_load.start()
    u_load.start()
    k_load.start()

    barrier = pltpu.get_barrier_semaphore()

    def greet(x, y, z):
        pl.semaphore_signal(barrier, inc=1, device_id=(x, y, z), device_id_type=MESH)

    partners = [gx + (1 << s) - 2 * (1 << s) * ((gx // (1 << s)) % 2) for s in range(stages)]
    for x in partners:
        greet(x, gy, gz)
    greet(gx, gy, other_z)

    @pl.when(gx > 0)
    def _():
        greet(gx - 1, gy, gz)

    @pl.when(gy > 0)
    def _():
        greet(gx, gy - 1, gz)
        greet(gx, gy - 1, other_z)

    @pl.when(gy < ny - 1)
    def _():
        greet(gx, gy + 1, gz)
        greet(gx, gy + 1, other_z)

    one = jnp.int32(1)
    zero = jnp.int32(0)
    awaited = (
        stages + 1
        + jnp.where(gx < nx - 1, one, zero)
        + 2 * jnp.where(gy > 0, one, zero)
        + 2 * jnp.where(gy < ny - 1, one, zero)
    )

    def remote(src, dst, send, recv, x, y, z):
        return pltpu.make_async_remote_copy(
            src_ref=src, dst_ref=dst, send_sem=send, recv_sem=recv,
            device_id=(x, y, z), device_id_type=MESH,
        )

    x_copy = remote(
        d_hbm.at[planes - 1], x_halo, halo_send.at[0], halo_recv.at[0], gx + 1, gy, gz
    )
    up_copy = remote(y_send.at[0], y_recv.at[1], halo_send.at[1], halo_recv.at[1], gx, gy - 1, gz)
    down_copy = remote(y_send.at[1], y_recv.at[0], halo_send.at[2], halo_recv.at[2], gx, gy + 1, gz)
    z_copy = remote(
        z_send, z_recv.at[pl.ds(8, rows), :], halo_send.at[3], halo_recv.at[3], gx, gy, other_z
    )
    up_corner = remote(
        z_send.at[pl.ds(0, 8), :], z_recv.at[pl.ds(8 + rows, 8), :],
        halo_send.at[4], halo_recv.at[4], gx, gy - 1, other_z,
    )
    down_corner = remote(
        z_send.at[pl.ds(rows - 8, 8), :], z_recv.at[pl.ds(0, 8), :],
        halo_send.at[5], halo_recv.at[5], gx, gy + 1, other_z,
    )

    @pl.when(gx == 0)
    def _():
        x_halo[...] = jnp.zeros((rows, lanes), jnp.float32)

    @pl.when(gy == 0)
    def _():
        y_recv[0] = jnp.zeros((2, planes, lanes), jnp.float32)
        z_recv[0:8, :] = jnp.zeros((8, lanes), jnp.float32)

    @pl.when(gy == ny - 1)
    def _():
        y_recv[1] = jnp.zeros((2, planes, lanes), jnp.float32)
        z_recv[8 + rows : 16 + rows, :] = jnp.zeros((8, lanes), jnp.float32)

    lane = lax.broadcasted_iota(jnp.int32, (rows, lanes), 1)
    edge = jnp.where(gz == 0, jnp.int32(lanes - 1), zero)

    zeros = jnp.zeros((rows, lanes), jnp.float32)
    ones = jnp.ones((rows, lanes), jnp.float32)

    def gather_edge(i, acc):
        heat = pltpu.roll(u_pad[i, 8 : 8 + rows, :], lax.rem(i - edge + lanes, lanes), 1)
        diff = pltpu.roll(d_pad[i, 8 : 8 + rows, :], lax.rem(i + planes - edge + lanes, lanes), 1)
        acc = jnp.where(lane == i, heat, acc)
        return jnp.where(lane == i + planes, diff, acc)

    d_load.wait()
    u_load.wait()
    for field, flat in enumerate((u_flat, d_flat)):
        y_send[0, field] = flat[pl.ds(8, planes, stride=pitch), :]
        y_send[1, field] = flat[pl.ds(7 + rows, planes, stride=pitch), :]
    acc = lax.fori_loop(0, planes, gather_edge, zeros, unroll=planes)
    z_send[...] = acc

    pl.semaphore_wait(barrier, awaited)
    z_copy.start()

    @pl.when(gy > 0)
    def _():
        up_copy.start()
        up_corner.start()

    @pl.when(gy < ny - 1)
    def _():
        down_copy.start()
        down_corner.start()

    @pl.when(gx < nx - 1)
    def _():
        x_copy.start()

    k_load.wait()

    def bent(i, acc):
        bend = pltpu.roll(skew[i].astype(jnp.float32), lax.rem(i - edge + lanes, lanes), 1)
        return jnp.where(lane == i, bend, acc)

    def homogeneous(i, state):
        a, b, c, d, before, acc = state
        here = d_pad[i, 8 : 8 + rows, :]
        step = 1.0 / (0.5 * ratio_x * (here + before))
        rho[i] = step
        a = a + step * c
        b = b + step * d
        return (a, b, c + a, d + b, here, bent(i, acc))

    lead = d_pad[0, 8 : 8 + rows, :]
    a, b, c, d, last, acc = lax.fori_loop(
        1, planes, homogeneous, (ones, zeros, ones, ones, lead, bent(0, zeros)), unroll=21
    )
    skew_edge[...] = acc

    @pl.when(gx > 0)
    def _():
        x_copy.wait_recv()

    step = 1.0 / (0.5 * ratio_x * (lead + x_halo[...]))
    rho[0] = step
    b = b + a * step
    d = d + c * step
    closing = jnp.where(gx == nx - 1, 1.0 / (0.5 * ratio_x * last), 0.0)
    inv_d = 1.0 / d
    own = (inv_d, b * inv_d + closing, c * inv_d)

    def post(at, send_buf, recv_buf, values, partner):
        for n, v in enumerate(values):
            send_buf[n] = v
        copy = remote(send_buf, recv_buf, line_send.at[at], line_recv.at[at], partner, gy, gz)
        copy.start()
        return copy

    line = [post(0, map_send.at[0], map_recv.at[0], own, partners[0])]

    @pl.when(gy > 0)
    def _():
        down_copy.wait_recv()
        down_corner.wait_recv()

    @pl.when(gy < ny - 1)
    def _():
        up_copy.wait_recv()
        up_corner.wait_recv()

    z_copy.wait_recv()
    met_heat = z_recv[8 : 8 + rows, :]
    met_diff = pltpu.roll(met_heat, lanes - planes, 1)
    own_edge = z_send[...]
    own_diff = pltpu.roll(own_edge, lanes - planes, 1)
    met_bend = z_recv[9 : 9 + rows, :] - z_recv[7 : 7 + rows, :]
    mix_sign = jnp.where(gz == 0, jnp.float32(ratio_mix), jnp.float32(-ratio_mix))
    edge_term = (0.5 * ratio_z) * (
        own_diff * met_heat + met_diff * (met_heat - own_edge)
    ) + mix_sign * skew_edge[...] * met_bend

    for field, flat in enumerate((u_flat, d_flat)):
        flat[pl.ds(7, planes, stride=pitch), :] = y_recv[0, field]
        flat[pl.ds(8 + rows, planes, stride=pitch), :] = y_recv[1, field]

    first_lane = lane == 0
    last_lane = lane == lanes - 1
    edge_lane = lane == edge

    def source(i, state):
        wp, fp = state
        heat = u_pad[i, 8 : 8 + rows, :]
        diff = d_pad[i, 8 : 8 + rows, :]
        heat_m = u_pad[i, 7 : 7 + rows, :]
        heat_p = u_pad[i, 9 : 9 + rows, :]
        flux_y = (diff + d_pad[i, 9 : 9 + rows, :]) * (heat_p - heat) - (
            diff + d_pad[i, 7 : 7 + rows, :]
        ) * (heat - heat_m)
        next_heat = jnp.where(last_lane, 0.0, pltpu.roll(heat, lanes - 1, 1))
        next_diff = jnp.where(last_lane, 0.0, pltpu.roll(diff, lanes - 1, 1))
        face = (diff + next_diff) * (next_heat - heat)
        before = jnp.where(first_lane, diff * heat, pltpu.roll(face, 1, 1))
        bend = heat_p - heat_m
        mixed = jnp.where(last_lane, 0.0, pltpu.roll(bend, lanes - 1, 1)) - jnp.where(
            first_lane, 0.0, pltpu.roll(bend, 1, 1)
        )
        extra = pltpu.roll(edge_term, lax.rem(edge - i + lanes, lanes), 1)
        side = (
            heat
            + (0.5 * ratio_y) * flux_y
            + (0.5 * ratio_z) * (face - before)
            + ratio_mix * skew[i].astype(jnp.float32) * mixed
            + jnp.where(edge_lane, extra, 0.0)
        )
        r_buf[i] = side
        wp = wp + rho[i] * fp
        return (wp, fp + (wp - side))

    half = planes // 2
    wp, fp = lax.fori_loop(0, half, source, (zeros, zeros), unroll=16)

    flags = [(gx // (1 << s)) % 2 == 1 for s in range(stages)]
    group, right = own, own
    left = (ones, zeros, zeros)
    steps = []
    for s in range(stages - 1):
        if s:
            line.append(post(s, map_send.at[s], map_recv.at[s], group, partners[s]))
        line[s].wait_recv()
        theirs = tuple(map_recv[s, n] for n in range(3))
        first = pick(flags[s], theirs, group)
        second = pick(flags[s], group, theirs)
        joined, weights = link(first, second)
        left_joined, left_weights = link(theirs, left)
        right_joined, right_weights = link(right, theirs)
        steps.append((theirs, first, second, weights, left, left_weights, right, right_weights))
        group = joined
        left = pick(flags[s], left_joined, left)
        right = pick(flags[s], right, right_joined)
    in_right = flags[-1]
    end_weight = group[0] / group[1]
    line.append(post(
        stages - 1, rel_send.at[0], rel_recv.at[0],
        (jnp.where(in_right, group[2] + group[0] * end_weight, group[1]),), partners[-1],
    ))

    wp, fp = lax.fori_loop(half, planes, source, (wp, fp), unroll=16)
    group_pq = (wp - b * inv_d * fp, fp * inv_d)
    left_pq, right_pq = (zeros, zeros), group_pq
    for s in range(stages - 1):
        copy = post(stages + s, pq_send.at[s], pq_recv.at[s], group_pq, partners[s])
        line.append(copy)
        theirs_map, first, second, weights, left_map, left_weights, right_map, right_weights = steps[s]
        copy.wait_recv()
        theirs = tuple(pq_recv[s, n] for n in range(2))
        first_pq = pick(flags[s], theirs, group_pq)
        second_pq = pick(flags[s], group_pq, theirs)
        left_pq = pick(
            flags[s], link_sides(left_weights, theirs_map, theirs, left_map, left_pq), left_pq
        )
        right_pq = pick(
            flags[s], right_pq, link_sides(right_weights, right_map, right_pq, theirs_map, theirs)
        )
        group_pq = link_sides(weights, first, first_pq, second, second_pq)
    copy = post(
        2 * stages - 1, rel_send.at[1], rel_recv.at[1],
        (jnp.where(in_right, group_pq[1] + end_weight * group_pq[0], group_pq[0]),), partners[-1],
    )
    line.append(copy)
    line[stages - 1].wait_recv()
    met = rel_recv[0, 0]
    z0 = jnp.where(in_right, met, 0.0)
    c0 = jnp.where(in_right, 0.0, met)
    left_in = left[0] / (1.0 + z0 * left[2])
    z_in = left[1] + left_in * left[0] * z0
    right_in = jnp.where(in_right, right[0] / right[1], right[0] / (1.0 + right[1] * c0))
    c_in = right[2] + right_in * jnp.where(in_right, right[0], right[0] * c0)
    inv_sum = 1.0 / (1.0 + z_in * c_in)
    copy.wait_recv()
    met = rel_recv[1, 0]
    e0 = jnp.where(in_right, met, 0.0)
    e_in = left_pq[0] + left_in * (e0 - z0 * left_pq[1])
    q_in = right_pq[1] + right_in * jnp.where(in_right, right_pq[0], met + c0 * right_pq[0])
    value = (e_in - z_in * q_in) * inv_sum
    flux = -(c_in * e_in + q_in) * inv_sum

    start[0] = value
    start[1] = flux

    for copy in line:
        copy.wait_send()
    z_copy.wait_send()

    @pl.when(gx < nx - 1)
    def _():
        x_copy.wait_send()

    @pl.when(gy > 0)
    def _():
        up_copy.wait_send()
        up_corner.wait_send()

    @pl.when(gy < ny - 1)
    def _():
        down_copy.wait_send()
        down_corner.wait_send()


def march_kernel(r_buf, rho, start, r_hbm, w_hbm, w_buf, store_sem):
    planes = r_buf.shape[0]
    r_store = pltpu.make_async_copy(r_buf, r_hbm, store_sem.at[0])
    r_store.start()

    def march(i, state):
        value, flux = state
        value = value + rho[i] * flux
        w_buf[i] = value
        return (value, flux + (value - r_buf[i]))

    chunks = 4
    size = planes // chunks
    stores = []
    state = (start[0], start[1])
    for n in range(chunks):
        state = lax.fori_loop(n * size, (n + 1) * size, march, state, unroll=16)
        part = pl.ds(n * size, size)
        store = pltpu.make_async_copy(w_buf.at[part], w_hbm.at[part], store_sem.at[1 + n])
        store.start()
        stores.append(store)
    r_store.wait()
    for store in stores:
        store.wait()


def body(nx, ny, nz, initial_thermal_state, thermal_spread_rate, yz_skew_factor):
    planes, rows, lanes = initial_thermal_state.shape
    stages = int(math.log2(nx))
    f32 = jnp.float32
    block = jax.ShapeDtypeStruct((planes, rows, lanes), f32)
    padded = pltpu.VMEM((planes, rows + 16, lanes), f32)
    full = pltpu.VMEM((planes, rows, lanes), f32)
    plane = pltpu.VMEM((rows, lanes), f32)
    faces = pltpu.VMEM((2, 2, planes, lanes), f32)
    maps = pltpu.VMEM((stages - 1, 3, rows, lanes), f32)
    sides = pltpu.VMEM((stages - 1, 2, rows, lanes), f32)
    relation = pltpu.VMEM((2, 1, rows, lanes), f32)
    r, rho, start = pl.pallas_call(
        functools.partial(kernel, nx, ny, nz),
        out_shape=(full, full, pltpu.VMEM((2, rows, lanes), f32)),
        in_specs=[pl.BlockSpec(memory_space=pltpu.HBM)] * 3,
        out_specs=(pl.BlockSpec(memory_space=pltpu.VMEM),) * 3,
        scratch_shapes=[
            padded, padded, pltpu.VMEM((planes, rows, lanes), jnp.bfloat16),
            plane, faces, faces, plane, pltpu.VMEM((rows + 16, lanes), f32), plane,
            maps, maps, sides, sides, relation, relation,
            pltpu.SemaphoreType.DMA((3,)),
            pltpu.SemaphoreType.DMA((6,)),
            pltpu.SemaphoreType.DMA((6,)),
            pltpu.SemaphoreType.DMA((2 * stages,)),
            pltpu.SemaphoreType.DMA((2 * stages,)),
        ],
        compiler_params=pltpu.CompilerParams(
            collective_id=0, has_side_effects=True, vmem_limit_bytes=VMEM1
        ),
    )(initial_thermal_state, thermal_spread_rate, yz_skew_factor)
    return pl.pallas_call(
        march_kernel,
        out_shape=(block, block),
        in_specs=[pl.BlockSpec(memory_space=pltpu.VMEM)] * 3,
        out_specs=(pl.BlockSpec(memory_space=pl.ANY),) * 2,
        scratch_shapes=[full, pltpu.SemaphoreType.DMA((5,))],
        compiler_params=pltpu.CompilerParams(vmem_limit_bytes=VMEM2),
    )(r, rho, start)


def solution(mesh):
    shape = dict(mesh.shape)
    spec = P("gx", "gy", "gz")
    return jax.shard_map(
        functools.partial(body, shape["gx"], shape["gy"], shape["gz"]),
        mesh=mesh, in_specs=(spec,) * 3, out_specs=(spec,) * 2, check_vma=False,
    )
```

```python
import functools
import math

import jax
import jax.numpy as jnp
from jax import lax
from jax.experimental import pallas as pl
from jax.experimental.pallas import tpu as pltpu
from jax.sharding import PartitionSpec as P

ratio_x = 4096.0
ratio_y = 0.2
ratio_z = 0.2
ratio_mix = 0.25
VMEM1 = 61 * 1024 * 1024 + 512 * 1024
VMEM2 = 48 * 1024 * 1024
MESH = pl.DeviceIdType.MESH


def inverse(x):
    guess = pl.reciprocal(x, approx=True)
    guess = guess * (2.0 - x * guess)
    return guess * (2.0 - x * guess)


def link(first, second):
    t1, z1, c1 = first
    t2, z2, c2 = second
    share = inverse(1.0 + z1 * c2)
    k1 = t1 * share
    k2 = t2 * share
    return (k1 * t2, z2 + k2 * t2 * z1, c1 + k1 * t1 * c2), (k1, k2)


def link_sides(weights, first, first_pq, second, second_pq):
    k1, k2 = weights
    p1, q1 = first_pq
    p2, q2 = second_pq
    return (p2 + k2 * (p1 - first[1] * q2), q1 + k1 * (q2 + second[2] * p1))


def pick(flag, yes, no):
    return tuple(jnp.where(flag, s, t) for s, t in zip(yes, no))


def kernel(
    nx, ny, nz, u_hbm, d_hbm, k_hbm, r_buf, rho, start,
    u_pad, d_pad, u_next, u_prev, d_next, d_prev, skew,
    x_halo, y_send, y_recv, z_send, z_recv, own_edge, skew_edge,
    map_send, map_recv, pq_send, pq_recv, rel_send, rel_recv,
    load_sem, halo_send, halo_recv, line_send, line_recv,
):
    planes, rows, lanes = u_hbm.shape
    stages = int(math.log2(nx))
    gx, gy, gz = lax.axis_index("gx"), lax.axis_index("gy"), lax.axis_index("gz")
    other_z = 1 - gz
    pitch = rows + 16
    body_rows = pl.ds(8, rows)
    u_flat = u_pad.reshape(planes * pitch, lanes)
    d_flat = d_pad.reshape(planes * pitch, lanes)

    d_load = pltpu.make_async_copy(d_hbm, d_pad.at[:, body_rows, :], load_sem.at[0])
    u_load = pltpu.make_async_copy(u_hbm, u_pad.at[:, body_rows, :], load_sem.at[1])
    k_load = pltpu.make_async_copy(k_hbm, skew, load_sem.at[2])
    d_load.start()
    u_load.start()
    k_load.start()

    barrier = pltpu.get_barrier_semaphore()

    def greet(x, y, z):
        pl.semaphore_signal(barrier, inc=1, device_id=(x, y, z), device_id_type=MESH)

    partners = [gx + (1 << s) - 2 * (1 << s) * ((gx // (1 << s)) % 2) for s in range(stages)]
    for x in partners:
        greet(x, gy, gz)
    greet(gx, gy, other_z)

    @pl.when(gx > 0)
    def _():
        greet(gx - 1, gy, gz)

    @pl.when(gy > 0)
    def _():
        greet(gx, gy - 1, gz)
        greet(gx, gy - 1, other_z)

    @pl.when(gy < ny - 1)
    def _():
        greet(gx, gy + 1, gz)
        greet(gx, gy + 1, other_z)

    one = jnp.int32(1)
    zero = jnp.int32(0)
    awaited = (
        stages + 1
        + jnp.where(gx < nx - 1, one, zero)
        + 2 * jnp.where(gy > 0, one, zero)
        + 2 * jnp.where(gy < ny - 1, one, zero)
    )

    def remote(src, dst, send, recv, x, y, z):
        return pltpu.make_async_remote_copy(
            src_ref=src, dst_ref=dst, send_sem=send, recv_sem=recv,
            device_id=(x, y, z), device_id_type=MESH,
        )

    x_copy = remote(
        d_hbm.at[planes - 1], x_halo, halo_send.at[0], halo_recv.at[0], gx + 1, gy, gz
    )
    up_copy = remote(y_send.at[0], y_recv.at[1], halo_send.at[1], halo_recv.at[1], gx, gy - 1, gz)
    down_copy = remote(y_send.at[1], y_recv.at[0], halo_send.at[2], halo_recv.at[2], gx, gy + 1, gz)
    z_copy = remote(
        z_send, z_recv.at[:, pl.ds(8, rows), :], halo_send.at[3], halo_recv.at[3], gx, gy, other_z
    )
    up_corner = remote(
        z_send.at[0, pl.ds(0, 8), :], z_recv.at[0, pl.ds(8 + rows, 8), :],
        halo_send.at[4], halo_recv.at[4], gx, gy - 1, other_z,
    )
    down_corner = remote(
        z_send.at[0, pl.ds(rows - 8, 8), :], z_recv.at[0, pl.ds(0, 8), :],
        halo_send.at[5], halo_recv.at[5], gx, gy + 1, other_z,
    )

    @pl.when(gx == 0)
    def _():
        x_halo[...] = jnp.zeros((rows, lanes), jnp.float32)

    @pl.when(gy == 0)
    def _():
        y_recv[0] = jnp.zeros((2, planes, lanes), jnp.float32)
        z_recv[0, 0:8, :] = jnp.zeros((8, lanes), jnp.float32)

    @pl.when(gy == ny - 1)
    def _():
        y_recv[1] = jnp.zeros((2, planes, lanes), jnp.float32)
        z_recv[0, 8 + rows : 16 + rows, :] = jnp.zeros((8, lanes), jnp.float32)

    assert 2 * planes <= lanes and nz == 2
    lane = lax.broadcasted_iota(jnp.int32, (rows, lanes), 1)
    owner = lax.rem((lane + 1) // 2, jnp.int32(planes))

    zeros = jnp.zeros((rows, lanes), jnp.float32)
    ones = jnp.ones((rows, lanes), jnp.float32)

    def gather_edge(i, acc):
        heat = pltpu.roll(u_pad[i, 8 : 8 + rows, :], 2 * i, 1)
        diff = pltpu.roll(d_pad[i, 8 : 8 + rows, :], 2 * i, 1)
        mine = owner == i
        return (jnp.where(mine, heat, acc[0]), jnp.where(mine, diff, acc[1]))

    d_load.wait()
    u_load.wait()
    for field, flat in enumerate((u_flat, d_flat)):
        y_send[0, field] = flat[pl.ds(8, planes, stride=pitch), :]
        y_send[1, field] = flat[pl.ds(7 + rows, planes, stride=pitch), :]
    edge_heat, edge_diff = lax.fori_loop(0, planes, gather_edge, (zeros, zeros), unroll=8)
    z_send[0] = edge_heat
    z_send[1] = edge_diff

    pl.semaphore_wait(barrier, awaited)
    z_copy.start()

    @pl.when(gy > 0)
    def _():
        up_copy.start()
        up_corner.start()

    @pl.when(gy < ny - 1)
    def _():
        down_copy.start()
        down_corner.start()

    @pl.when(gx < nx - 1)
    def _():
        x_copy.start()

    k_load.wait()

    def homogeneous(i, state):
        a, b, c, d, before, acc = state
        here = d_pad[i, 8 : 8 + rows, :]
        heat = u_pad[i, 8 : 8 + rows, :]
        u_next[i, 8 : 8 + rows, :] = pltpu.roll(heat, lanes - 1, 1)
        u_prev[i, 8 : 8 + rows, :] = pltpu.roll(heat, 1, 1)
        d_next[i] = pltpu.roll(here, lanes - 1, 1)
        d_prev[i] = pltpu.roll(here, 1, 1)
        bend = pltpu.roll(skew[i].astype(jnp.float32), 2 * i, 1)
        step = inverse((0.5 * ratio_x) * (here + before))
        rho[i] = step
        a = a + step * c
        b = b + step * d
        return (a, b, c + a, d + b, here, jnp.where(owner == i, bend, acc))

    lead = d_pad[0, 8 : 8 + rows, :]
    a, b, c, d, last, acc = lax.fori_loop(
        0, planes, homogeneous, (ones, zeros, zeros, ones, lead, zeros), unroll=4
    )
    skew_edge[...] = acc

    @pl.when(gx > 0)
    def _():
        x_copy.wait_recv()

    step = inverse((0.5 * ratio_x) * (lead + x_halo[...]))
    change = step - rho[0]
    rho[0] = step
    b = b + a * change
    d = d + c * change
    closing = jnp.where(gx == nx - 1, inverse((0.5 * ratio_x) * last), 0.0)
    inv_d = inverse(d)
    own = (inv_d, b * inv_d + closing, c * inv_d)

    def post(at, send_buf, recv_buf, values, partner):
        for n, v in enumerate(values):
            send_buf[n] = v
        copy = remote(send_buf, recv_buf, line_send.at[at], line_recv.at[at], partner, gy, gz)
        copy.start()
        return copy

    line = [post(0, map_send.at[0], map_recv.at[0], own, partners[0])]

    @pl.when(gy > 0)
    def _():
        down_copy.wait_recv()
        down_corner.wait_recv()

    @pl.when(gy < ny - 1)
    def _():
        up_copy.wait_recv()
        up_corner.wait_recv()

    z_copy.wait_recv()
    even = lax.rem(lane, jnp.int32(2)) == 0

    def across(x):
        return jnp.where(even, pltpu.roll(x, 1, 1), pltpu.roll(x, lanes - 1, 1))

    own_edge[0:8, :] = jnp.zeros((8, lanes), jnp.float32)
    own_edge[8 : 8 + rows, :] = z_send[0]
    own_edge[8 + rows : 16 + rows, :] = jnp.zeros((8, lanes), jnp.float32)
    heat, diff = z_send[0], z_send[1]
    near = jnp.where(even, 1.0, 0.0)
    near = jnp.where(gz == 0, 1.0 - near, near)
    met_heat = near * across(z_recv[0, 8 : 8 + rows, :])
    met_diff = near * across(z_recv[1, 8 : 8 + rows, :])
    met_bend = near * across(z_recv[0, 9 : 9 + rows, :] - z_recv[0, 7 : 7 + rows, :])
    wrap_bend = across(own_edge[9 : 9 + rows, :] - own_edge[7 : 7 + rows, :])
    edge_term = (0.5 * ratio_z) * (
        (diff + met_diff) * (met_heat - heat) - (diff + across(diff)) * (across(heat) - heat)
    ) + jnp.where(even, -ratio_mix, ratio_mix) * skew_edge[...] * (met_bend - wrap_bend)

    long_lane = lax.broadcasted_iota(jnp.int32, (planes, lanes), 1)
    for side, row in enumerate((7, 8 + rows)):
        at = pl.ds(row, planes, stride=pitch)
        halo = y_recv[side, 0]
        u_flat[at, :] = halo
        d_flat[at, :] = y_recv[side, 1]
        u_next.reshape(planes * pitch, lanes)[at, :] = jnp.where(
            long_lane == lanes - 1, 0.0, pltpu.roll(halo, lanes - 1, 1)
        )
        u_prev.reshape(planes * pitch, lanes)[at, :] = jnp.where(
            long_lane == 0, 0.0, pltpu.roll(halo, 1, 1)
        )

    edge_lane = (lane == 0) | (lane == lanes - 1)

    def unpacked(i):
        return pltpu.roll(edge_term, lax.rem(2 * (lanes - i), lanes), 1)

    def source(i, state):
        wp, fp, extra = state
        heat = u_pad[i, 8 : 8 + rows, :]
        diff = d_pad[i, 8 : 8 + rows, :]
        flux_y = (diff + d_pad[i, 9 : 9 + rows, :]) * (u_pad[i, 9 : 9 + rows, :] - heat) - (
            diff + d_pad[i, 7 : 7 + rows, :]
        ) * (heat - u_pad[i, 7 : 7 + rows, :])
        flux_z = (diff + d_next[i]) * (u_next[i, 8 : 8 + rows, :] - heat) - (
            diff + d_prev[i]
        ) * (heat - u_prev[i, 8 : 8 + rows, :])
        mixed = (u_next[i, 9 : 9 + rows, :] - u_next[i, 7 : 7 + rows, :]) - (
            u_prev[i, 9 : 9 + rows, :] - u_prev[i, 7 : 7 + rows, :]
        )
        side = (
            heat
            + ((0.5 * ratio_y) * flux_y + (0.5 * ratio_z) * flux_z)
            + ratio_mix * skew[i].astype(jnp.float32) * mixed
            + jnp.where(edge_lane, extra, 0.0)
        )
        r_buf[i] = side
        wp = wp + rho[i] * fp
        return (wp, fp + (wp - side), unpacked(i + 1))

    half = planes // 2
    state = lax.fori_loop(0, half, source, (zeros, zeros, unpacked(0)), unroll=2)

    flags = [(gx // (1 << s)) % 2 == 1 for s in range(stages)]
    group, right = own, own
    left = (ones, zeros, zeros)
    steps = []
    for s in range(stages - 1):
        if s:
            line.append(post(s, map_send.at[s], map_recv.at[s], group, partners[s]))
        line[s].wait_recv()
        theirs = tuple(map_recv[s, n] for n in range(3))
        first = pick(flags[s], theirs, group)
        second = pick(flags[s], group, theirs)
        joined, weights = link(first, second)
        left_joined, left_weights = link(theirs, left)
        right_joined, right_weights = link(right, theirs)
        steps.append((theirs, first, second, weights, left, left_weights, right, right_weights))
        group = joined
        left = pick(flags[s], left_joined, left)
        right = pick(flags[s], right, right_joined)
    in_right = flags[-1]
    end_weight = group[0] * inverse(group[1])
    line.append(post(
        stages - 1, rel_send.at[0], rel_recv.at[0],
        (jnp.where(in_right, group[2] + group[0] * end_weight, group[1]),), partners[-1],
    ))

    wp, fp, _ = lax.fori_loop(half, planes, source, state, unroll=2)
    group_pq = (wp - b * inv_d * fp, fp * inv_d)
    left_pq, right_pq = (zeros, zeros), group_pq
    for s in range(stages - 1):
        copy = post(stages + s, pq_send.at[s], pq_recv.at[s], group_pq, partners[s])
        line.append(copy)
        theirs_map, first, second, weights, left_map, left_weights, right_map, right_weights = steps[s]
        copy.wait_recv()
        theirs = tuple(pq_recv[s, n] for n in range(2))
        first_pq = pick(flags[s], theirs, group_pq)
        second_pq = pick(flags[s], group_pq, theirs)
        left_pq = pick(
            flags[s], link_sides(left_weights, theirs_map, theirs, left_map, left_pq), left_pq
        )
        right_pq = pick(
            flags[s], right_pq, link_sides(right_weights, right_map, right_pq, theirs_map, theirs)
        )
        group_pq = link_sides(weights, first, first_pq, second, second_pq)
    copy = post(
        2 * stages - 1, rel_send.at[1], rel_recv.at[1],
        (jnp.where(in_right, group_pq[1] + end_weight * group_pq[0], group_pq[0]),), partners[-1],
    )
    line.append(copy)
    line[stages - 1].wait_recv()
    met = rel_recv[0, 0]
    z0 = jnp.where(in_right, met, 0.0)
    c0 = jnp.where(in_right, 0.0, met)
    left_in = left[0] * inverse(1.0 + z0 * left[2])
    z_in = left[1] + left_in * left[0] * z0
    right_in = right[0] * inverse(jnp.where(in_right, right[1], 1.0 + right[1] * c0))
    c_in = right[2] + right_in * jnp.where(in_right, right[0], right[0] * c0)
    inv_sum = inverse(1.0 + z_in * c_in)
    copy.wait_recv()
    met = rel_recv[1, 0]
    e0 = jnp.where(in_right, met, 0.0)
    e_in = left_pq[0] + left_in * (e0 - z0 * left_pq[1])
    q_in = right_pq[1] + right_in * jnp.where(in_right, right_pq[0], met + c0 * right_pq[0])
    value = (e_in - z_in * q_in) * inv_sum
    flux = -(c_in * e_in + q_in) * inv_sum

    start[0] = value
    start[1] = flux

    for copy in line:
        copy.wait_send()
    z_copy.wait_send()

    @pl.when(gx < nx - 1)
    def _():
        x_copy.wait_send()

    @pl.when(gy > 0)
    def _():
        up_copy.wait_send()
        up_corner.wait_send()

    @pl.when(gy < ny - 1)
    def _():
        down_copy.wait_send()
        down_corner.wait_send()


def march_kernel(r_buf, rho, start, r_hbm, w_hbm, w_buf, store_sem):
    planes = r_buf.shape[0]
    r_store = pltpu.make_async_copy(r_buf, r_hbm, store_sem.at[0])
    r_store.start()

    def march(i, state):
        value, flux = state
        value = value + rho[i] * flux
        w_buf[i] = value
        return (value, flux + (value - r_buf[i]))

    chunks = 4
    size = planes // chunks

    def store(n):
        part = pl.ds(n * size, size)
        return pltpu.make_async_copy(w_buf.at[part], w_hbm.at[part], store_sem.at[1 + n])

    def chunk(n, state):
        state = lax.fori_loop(0, size, lambda i, s: march(n * size + i, s), state, unroll=8)
        store(n).start()
        return state

    lax.fori_loop(0, chunks, chunk, (start[0], start[1]))
    r_store.wait()
    for n in range(chunks):
        store(n).wait()


def body(nx, ny, nz, initial_thermal_state, thermal_spread_rate, yz_skew_factor):
    planes, rows, lanes = initial_thermal_state.shape
    stages = int(math.log2(nx))
    f32 = jnp.float32
    block = jax.ShapeDtypeStruct((planes, rows, lanes), f32)
    padded = pltpu.VMEM((planes, rows + 16, lanes), f32)
    full = pltpu.VMEM((planes, rows, lanes), f32)
    plane = pltpu.VMEM((rows, lanes), f32)
    faces = pltpu.VMEM((2, 2, planes, lanes), f32)
    maps = pltpu.VMEM((stages - 1, 3, rows, lanes), f32)
    sides = pltpu.VMEM((stages - 1, 2, rows, lanes), f32)
    relation = pltpu.VMEM((2, 1, rows, lanes), f32)
    r, rho, start = pl.pallas_call(
        functools.partial(kernel, nx, ny, nz),
        out_shape=(full, full, pltpu.VMEM((2, rows, lanes), f32)),
        in_specs=[pl.BlockSpec(memory_space=pltpu.HBM)] * 3,
        out_specs=(pl.BlockSpec(memory_space=pltpu.VMEM),) * 3,
        scratch_shapes=[
            padded, padded, padded, padded, full, full,
            pltpu.VMEM((planes, rows, lanes), jnp.bfloat16),
            plane, faces, faces, pltpu.VMEM((2, rows, lanes), f32), pltpu.VMEM((2, rows + 16, lanes), f32),
            pltpu.VMEM((rows + 16, lanes), f32), plane,
            maps, maps, sides, sides, relation, relation,
            pltpu.SemaphoreType.DMA((3,)),
            pltpu.SemaphoreType.DMA((6,)),
            pltpu.SemaphoreType.DMA((6,)),
            pltpu.SemaphoreType.DMA((2 * stages,)),
            pltpu.SemaphoreType.DMA((2 * stages,)),
        ],
        compiler_params=pltpu.CompilerParams(
            collective_id=0, has_side_effects=True, vmem_limit_bytes=VMEM1
        ),
    )(initial_thermal_state, thermal_spread_rate, yz_skew_factor)
    return pl.pallas_call(
        march_kernel,
        out_shape=(block, block),
        in_specs=[pl.BlockSpec(memory_space=pltpu.VMEM)] * 3,
        out_specs=(pl.BlockSpec(memory_space=pl.ANY),) * 2,
        scratch_shapes=[full, pltpu.SemaphoreType.DMA((5,))],
        compiler_params=pltpu.CompilerParams(vmem_limit_bytes=VMEM2),
    )(r, rho, start)


def solution(mesh):
    shape = dict(mesh.shape)
    spec = P("gx", "gy", "gz")
    return jax.shard_map(
        functools.partial(body, shape["gx"], shape["gy"], shape["gz"]),
        mesh=mesh, in_specs=(spec,) * 3, out_specs=(spec,) * 2, check_vma=False,
    )
```

```python
import functools
import math

import jax
import jax.numpy as jnp
from jax import lax
from jax.experimental import pallas as pl
from jax.experimental.pallas import tpu as pltpu
from jax.sharding import PartitionSpec as P

ratio_x = 4096.0
ratio_y = 0.2
ratio_z = 0.2
ratio_mix = 0.25
VMEM1 = 61 * 1024 * 1024 + 512 * 1024
VMEM2 = 48 * 1024 * 1024
MESH = pl.DeviceIdType.MESH


def inverse(x):
    guess = pl.reciprocal(x, approx=True)
    guess = guess * (2.0 - x * guess)
    return guess * (2.0 - x * guess)


def link(first, second):
    t1, z1, c1 = first
    t2, z2, c2 = second
    share = inverse(1.0 + z1 * c2)
    k1 = t1 * share
    k2 = t2 * share
    return (k1 * t2, z2 + k2 * t2 * z1, c1 + k1 * t1 * c2), (k1, k2)


def link_sides(weights, first, first_pq, second, second_pq):
    k1, k2 = weights
    p1, q1 = first_pq
    p2, q2 = second_pq
    return (p2 + k2 * (p1 - first[1] * q2), q1 + k1 * (q2 + second[2] * p1))


def pick(flag, yes, no):
    return tuple(jnp.where(flag, s, t) for s, t in zip(yes, no))


def kernel(
    nx, ny, nz, u_hbm, d_hbm, k_hbm, r_buf, rho, start,
    u_pad, d_pad, u_next, u_prev, d_next, d_prev, skew,
    x_halo, y_send, y_recv, z_send, z_recv, own_edge, skew_edge, bend_rows,
    map_send, map_recv, pq_send, pq_recv, rel_send, rel_recv,
    load_sem, halo_send, halo_recv, line_send, line_recv,
):
    planes, rows, lanes = u_hbm.shape
    stages = int(math.log2(nx))
    gx, gy, gz = lax.axis_index("gx"), lax.axis_index("gy"), lax.axis_index("gz")
    other_z = 1 - gz
    pitch = rows + 16
    body_rows = pl.ds(8, rows)
    u_flat = u_pad.reshape(planes * pitch, lanes)
    d_flat = d_pad.reshape(planes * pitch, lanes)

    d_load = pltpu.make_async_copy(d_hbm, d_pad.at[:, body_rows, :], load_sem.at[0])
    u_load = pltpu.make_async_copy(u_hbm, u_pad.at[:, body_rows, :], load_sem.at[1])
    k_load = pltpu.make_async_copy(k_hbm, skew, load_sem.at[2])
    d_load.start()
    u_load.start()
    k_load.start()

    barrier = pltpu.get_barrier_semaphore()

    def greet(x, y, z):
        pl.semaphore_signal(barrier, inc=1, device_id=(x, y, z), device_id_type=MESH)

    partners = [gx + (1 << s) - 2 * (1 << s) * ((gx // (1 << s)) % 2) for s in range(stages)]
    for x in partners:
        greet(x, gy, gz)
    greet(gx, gy, other_z)

    @pl.when(gx > 0)
    def _():
        greet(gx - 1, gy, gz)

    @pl.when(gy > 0)
    def _():
        greet(gx, gy - 1, gz)
        greet(gx, gy - 1, other_z)

    @pl.when(gy < ny - 1)
    def _():
        greet(gx, gy + 1, gz)
        greet(gx, gy + 1, other_z)

    one = jnp.int32(1)
    zero = jnp.int32(0)
    awaited = (
        stages + 1
        + jnp.where(gx < nx - 1, one, zero)
        + 2 * jnp.where(gy > 0, one, zero)
        + 2 * jnp.where(gy < ny - 1, one, zero)
    )

    def remote(src, dst, send, recv, x, y, z):
        return pltpu.make_async_remote_copy(
            src_ref=src, dst_ref=dst, send_sem=send, recv_sem=recv,
            device_id=(x, y, z), device_id_type=MESH,
        )

    x_copy = remote(
        d_hbm.at[planes - 1], x_halo, halo_send.at[0], halo_recv.at[0], gx + 1, gy, gz
    )
    up_copy, down_copy = [
        [
            remote(
                y_send.at[way, field], y_recv.at[1 - way, field],
                halo_send.at[4 + 2 * way + field], halo_recv.at[4 + 2 * way + field], gx, y, gz,
            )
            for field in range(2)
        ]
        for way, y in ((0, gy - 1), (1, gy + 1))
    ]
    z_copy = remote(
        z_send, z_recv.at[:, pl.ds(8, rows), :], halo_send.at[1], halo_recv.at[1], gx, gy, other_z
    )
    up_corner = remote(
        z_send.at[0, pl.ds(0, 8), :], z_recv.at[0, pl.ds(8 + rows, 8), :],
        halo_send.at[2], halo_recv.at[2], gx, gy - 1, other_z,
    )
    down_corner = remote(
        z_send.at[0, pl.ds(rows - 8, 8), :], z_recv.at[0, pl.ds(0, 8), :],
        halo_send.at[3], halo_recv.at[3], gx, gy + 1, other_z,
    )

    @pl.when(gx == 0)
    def _():
        x_halo[...] = jnp.zeros((rows, lanes), jnp.float32)

    @pl.when(gy == 0)
    def _():
        y_recv[0] = jnp.zeros((2, planes, lanes), jnp.float32)
        z_recv[0, 0:8, :] = jnp.zeros((8, lanes), jnp.float32)

    @pl.when(gy == ny - 1)
    def _():
        y_recv[1] = jnp.zeros((2, planes, lanes), jnp.float32)
        z_recv[0, 8 + rows : 16 + rows, :] = jnp.zeros((8, lanes), jnp.float32)

    assert 2 * planes <= lanes and nz == 2
    lane = lax.broadcasted_iota(jnp.int32, (rows, lanes), 1)
    owner = lax.rem((lane + 1) // 2, jnp.int32(planes))

    zeros = jnp.zeros((rows, lanes), jnp.float32)
    ones = jnp.ones((rows, lanes), jnp.float32)

    def gather_edge(i, acc):
        heat = pltpu.roll(u_pad[i, 8 : 8 + rows, :], 2 * i, 1)
        diff = pltpu.roll(d_pad[i, 8 : 8 + rows, :], 2 * i, 1)
        mine = owner == i
        return (jnp.where(mine, heat, acc[0]), jnp.where(mine, diff, acc[1]))

    for field, load, flat in ((1, d_load, d_flat), (0, u_load, u_flat)):
        load.wait()
        y_send[0, field] = flat[pl.ds(8, planes, stride=pitch), :]
        y_send[1, field] = flat[pl.ds(7 + rows, planes, stride=pitch), :]
        if field:
            pl.semaphore_wait(barrier, awaited)

            @pl.when(gx < nx - 1)
            def _():
                x_copy.start()

        @pl.when(gy > 0)
        def _():
            up_copy[field].start()

        @pl.when(gy < ny - 1)
        def _():
            down_copy[field].start()

    edge_heat, edge_diff = lax.fori_loop(0, planes, gather_edge, (zeros, zeros), unroll=8)
    z_send[0] = edge_heat
    z_send[1] = edge_diff

    z_copy.start()

    @pl.when(gy > 0)
    def _():
        up_corner.start()

    @pl.when(gy < ny - 1)
    def _():
        down_corner.start()

    k_load.wait()

    def homogeneous(i, state):
        a, b, c, d, before, acc = state
        here = d_pad[i, 8 : 8 + rows, :]
        heat = u_pad[i, 8 : 8 + rows, :]
        u_next[i, 8 : 8 + rows, :] = pltpu.roll(heat, lanes - 1, 1)
        u_prev[i, 8 : 8 + rows, :] = pltpu.roll(heat, 1, 1)
        d_next[i] = pltpu.roll(here, lanes - 1, 1)
        d_prev[i] = pltpu.roll(here, 1, 1)
        bend = pltpu.roll(skew[i].astype(jnp.float32), 2 * i, 1)
        step = inverse((0.5 * ratio_x) * (here + before))
        rho[i] = step
        a = a + step * c
        b = b + step * d
        return (a, b, c + a, d + b, here, jnp.where(owner == i, bend, acc))

    lead = d_pad[0, 8 : 8 + rows, :]
    a, b, c, d, last, acc = lax.fori_loop(
        0, planes, homogeneous, (ones, zeros, zeros, ones, lead, zeros), unroll=4
    )
    skew_edge[...] = acc

    @pl.when(gx > 0)
    def _():
        x_copy.wait_recv()

    step = inverse((0.5 * ratio_x) * (lead + x_halo[...]))
    change = step - rho[0]
    rho[0] = step
    b = b + a * change
    d = d + c * change
    closing = jnp.where(gx == nx - 1, inverse((0.5 * ratio_x) * last), 0.0)
    inv_d = inverse(d)
    own = (inv_d, b * inv_d + closing, c * inv_d)

    def post(at, send_buf, recv_buf, values, partner):
        for n, v in enumerate(values):
            send_buf[n] = v
        copy = remote(send_buf, recv_buf, line_send.at[at], line_recv.at[at], partner, gy, gz)
        copy.start()
        return copy

    line = [post(0, map_send.at[0], map_recv.at[0], own, partners[0])]

    for pad in (u_pad, d_pad, u_next, u_prev):
        flat = pad.reshape(planes * pitch, lanes)
        for row in (7, 8 + rows):
            flat[pl.ds(row, planes, stride=pitch), :] = jnp.zeros((planes, lanes), jnp.float32)

    def source(i, carried):
        heat = u_pad[i, 8 : 8 + rows, :]
        diff = d_pad[i, 8 : 8 + rows, :]
        flux_y = (diff + d_pad[i, 9 : 9 + rows, :]) * (u_pad[i, 9 : 9 + rows, :] - heat) - (
            diff + d_pad[i, 7 : 7 + rows, :]
        ) * (heat - u_pad[i, 7 : 7 + rows, :])
        flux_z = (diff + d_next[i]) * (u_next[i, 8 : 8 + rows, :] - heat) - (
            diff + d_prev[i]
        ) * (heat - u_prev[i, 8 : 8 + rows, :])
        mixed = (u_next[i, 9 : 9 + rows, :] - u_next[i, 7 : 7 + rows, :]) - (
            u_prev[i, 9 : 9 + rows, :] - u_prev[i, 7 : 7 + rows, :]
        )
        bend = skew[i].astype(jnp.float32)
        bend_rows[0, pl.ds(i, 1), :] = bend[0:1, :]
        bend_rows[1, pl.ds(i, 1), :] = bend[rows - 1 : rows, :]
        r_buf[i] = (
            heat
            + ((0.5 * ratio_y) * flux_y + (0.5 * ratio_z) * flux_z)
            + ratio_mix * bend * mixed
        )
        return carried

    lax.fori_loop(0, planes, source, zero, unroll=2)

    flags = [(gx // (1 << s)) % 2 == 1 for s in range(stages)]
    group, right = own, own
    left = (ones, zeros, zeros)
    steps = []
    for s in range(stages - 1):
        if s:
            line.append(post(s, map_send.at[s], map_recv.at[s], group, partners[s]))
        line[s].wait_recv()
        theirs = tuple(map_recv[s, n] for n in range(3))
        first = pick(flags[s], theirs, group)
        second = pick(flags[s], group, theirs)
        joined, weights = link(first, second)
        left_joined, left_weights = link(theirs, left)
        right_joined, right_weights = link(right, theirs)
        steps.append((theirs, first, second, weights, left, left_weights, right, right_weights))
        group = joined
        left = pick(flags[s], left_joined, left)
        right = pick(flags[s], right, right_joined)
    in_right = flags[-1]
    end_weight = group[0] * inverse(group[1])
    line.append(post(
        stages - 1, rel_send.at[0], rel_recv.at[0],
        (jnp.where(in_right, group[2] + group[0] * end_weight, group[1]),), partners[-1],
    ))

    @pl.when(gy > 0)
    def _():
        for copy in down_copy:
            copy.wait_recv()
        down_corner.wait_recv()

    @pl.when(gy < ny - 1)
    def _():
        for copy in up_copy:
            copy.wait_recv()
        up_corner.wait_recv()

    z_copy.wait_recv()
    long_lane = lax.broadcasted_iota(jnp.int32, (planes, lanes), 1)
    r_flat = r_buf.reshape(planes * rows, lanes)
    for way, row, sign in ((0, 0, -ratio_mix), (1, rows - 1, ratio_mix)):
        heat, diff = y_send[way, 0], y_send[way, 1]
        halo, halo_diff = y_recv[way, 0], y_recv[way, 1]
        bend = jnp.where(long_lane == lanes - 1, 0.0, pltpu.roll(halo, lanes - 1, 1)) - jnp.where(
            long_lane == 0, 0.0, pltpu.roll(halo, 1, 1)
        )
        at = pl.ds(row, planes, stride=rows)
        r_flat[at, :] += (0.5 * ratio_y) * (
            diff * halo + halo_diff * (halo - heat)
        ) + sign * bend_rows[way] * bend

    even = lax.rem(lane, jnp.int32(2)) == 0

    def across(x):
        return jnp.where(even, pltpu.roll(x, 1, 1), pltpu.roll(x, lanes - 1, 1))

    own_edge[0:8, :] = jnp.zeros((8, lanes), jnp.float32)
    own_edge[8 : 8 + rows, :] = z_send[0]
    own_edge[8 + rows : 16 + rows, :] = jnp.zeros((8, lanes), jnp.float32)
    heat, diff = z_send[0], z_send[1]
    near = jnp.where(even, 1.0, 0.0)
    near = jnp.where(gz == 0, 1.0 - near, near)
    met_heat = near * across(z_recv[0, 8 : 8 + rows, :])
    met_diff = near * across(z_recv[1, 8 : 8 + rows, :])
    met_bend = near * across(z_recv[0, 9 : 9 + rows, :] - z_recv[0, 7 : 7 + rows, :])
    wrap_bend = across(own_edge[9 : 9 + rows, :] - own_edge[7 : 7 + rows, :])
    edge_term = (0.5 * ratio_z) * (
        (diff + met_diff) * (met_heat - heat) - (diff + across(diff)) * (across(heat) - heat)
    ) + jnp.where(even, -ratio_mix, ratio_mix) * skew_edge[...] * (met_bend - wrap_bend)

    edge_lane = (lane == 0) | (lane == lanes - 1)

    def unpacked(i):
        return pltpu.roll(edge_term, lax.rem(2 * (lanes - i), lanes), 1)

    def particular(i, state):
        wp, fp, extra = state
        side = r_buf[i] + jnp.where(edge_lane, extra, 0.0)
        r_buf[i] = side
        wp = wp + rho[i] * fp
        return (wp, fp + (wp - side), unpacked(i + 1))

    wp, fp, _ = lax.fori_loop(0, planes, particular, (zeros, zeros, unpacked(0)), unroll=4)

    group_pq = (wp - b * inv_d * fp, fp * inv_d)
    left_pq, right_pq = (zeros, zeros), group_pq
    for s in range(stages - 1):
        copy = post(stages + s, pq_send.at[s], pq_recv.at[s], group_pq, partners[s])
        line.append(copy)
        theirs_map, first, second, weights, left_map, left_weights, right_map, right_weights = steps[s]
        copy.wait_recv()
        theirs = tuple(pq_recv[s, n] for n in range(2))
        first_pq = pick(flags[s], theirs, group_pq)
        second_pq = pick(flags[s], group_pq, theirs)
        left_pq = pick(
            flags[s], link_sides(left_weights, theirs_map, theirs, left_map, left_pq), left_pq
        )
        right_pq = pick(
            flags[s], right_pq, link_sides(right_weights, right_map, right_pq, theirs_map, theirs)
        )
        group_pq = link_sides(weights, first, first_pq, second, second_pq)
    copy = post(
        2 * stages - 1, rel_send.at[1], rel_recv.at[1],
        (jnp.where(in_right, group_pq[1] + end_weight * group_pq[0], group_pq[0]),), partners[-1],
    )
    line.append(copy)
    line[stages - 1].wait_recv()
    met = rel_recv[0, 0]
    z0 = jnp.where(in_right, met, 0.0)
    c0 = jnp.where(in_right, 0.0, met)
    left_in = left[0] * inverse(1.0 + z0 * left[2])
    z_in = left[1] + left_in * left[0] * z0
    right_in = right[0] * inverse(jnp.where(in_right, right[1], 1.0 + right[1] * c0))
    c_in = right[2] + right_in * jnp.where(in_right, right[0], right[0] * c0)
    inv_sum = inverse(1.0 + z_in * c_in)
    copy.wait_recv()
    met = rel_recv[1, 0]
    e0 = jnp.where(in_right, met, 0.0)
    e_in = left_pq[0] + left_in * (e0 - z0 * left_pq[1])
    q_in = right_pq[1] + right_in * jnp.where(in_right, right_pq[0], met + c0 * right_pq[0])
    value = (e_in - z_in * q_in) * inv_sum
    flux = -(c_in * e_in + q_in) * inv_sum

    start[0] = value
    start[1] = flux

    for copy in line:
        copy.wait_send()
    z_copy.wait_send()

    @pl.when(gx < nx - 1)
    def _():
        x_copy.wait_send()

    @pl.when(gy > 0)
    def _():
        for copy in up_copy:
            copy.wait_send()
        up_corner.wait_send()

    @pl.when(gy < ny - 1)
    def _():
        for copy in down_copy:
            copy.wait_send()
        down_corner.wait_send()


def march_kernel(r_buf, rho, start, r_hbm, w_hbm, w_buf, store_sem):
    planes = r_buf.shape[0]
    r_store = pltpu.make_async_copy(r_buf, r_hbm, store_sem.at[0])
    r_store.start()

    def march(i, state):
        value, flux = state
        value = value + rho[i] * flux
        w_buf[i] = value
        return (value, flux + (value - r_buf[i]))

    chunks = 4
    size = planes // chunks

    def store(n):
        part = pl.ds(n * size, size)
        return pltpu.make_async_copy(w_buf.at[part], w_hbm.at[part], store_sem.at[1 + n])

    def chunk(n, state):
        state = lax.fori_loop(0, size, lambda i, s: march(n * size + i, s), state, unroll=8)
        store(n).start()
        return state

    lax.fori_loop(0, chunks, chunk, (start[0], start[1]))
    r_store.wait()
    for n in range(chunks):
        store(n).wait()


def body(nx, ny, nz, initial_thermal_state, thermal_spread_rate, yz_skew_factor):
    planes, rows, lanes = initial_thermal_state.shape
    stages = int(math.log2(nx))
    f32 = jnp.float32
    block = jax.ShapeDtypeStruct((planes, rows, lanes), f32)
    padded = pltpu.VMEM((planes, rows + 16, lanes), f32)
    full = pltpu.VMEM((planes, rows, lanes), f32)
    plane = pltpu.VMEM((rows, lanes), f32)
    faces = pltpu.VMEM((2, 2, planes, lanes), f32)
    maps = pltpu.VMEM((stages - 1, 3, rows, lanes), f32)
    sides = pltpu.VMEM((stages - 1, 2, rows, lanes), f32)
    relation = pltpu.VMEM((2, 1, rows, lanes), f32)
    r, rho, start = pl.pallas_call(
        functools.partial(kernel, nx, ny, nz),
        out_shape=(full, full, pltpu.VMEM((2, rows, lanes), f32)),
        in_specs=[pl.BlockSpec(memory_space=pltpu.HBM)] * 3,
        out_specs=(pl.BlockSpec(memory_space=pltpu.VMEM),) * 3,
        scratch_shapes=[
            padded, padded, padded, padded, full, full,
            pltpu.VMEM((planes, rows, lanes), jnp.bfloat16),
            plane, faces, faces, pltpu.VMEM((2, rows, lanes), f32), pltpu.VMEM((2, rows + 16, lanes), f32),
            pltpu.VMEM((rows + 16, lanes), f32), plane, pltpu.VMEM((2, planes, lanes), f32),
            maps, maps, sides, sides, relation, relation,
            pltpu.SemaphoreType.DMA((3,)),
            pltpu.SemaphoreType.DMA((8,)),
            pltpu.SemaphoreType.DMA((8,)),
            pltpu.SemaphoreType.DMA((2 * stages,)),
            pltpu.SemaphoreType.DMA((2 * stages,)),
        ],
        compiler_params=pltpu.CompilerParams(
            collective_id=0, has_side_effects=True, vmem_limit_bytes=VMEM1
        ),
    )(initial_thermal_state, thermal_spread_rate, yz_skew_factor)
    return pl.pallas_call(
        march_kernel,
        out_shape=(block, block),
        in_specs=[pl.BlockSpec(memory_space=pltpu.VMEM)] * 3,
        out_specs=(pl.BlockSpec(memory_space=pl.ANY),) * 2,
        scratch_shapes=[full, pltpu.SemaphoreType.DMA((5,))],
        compiler_params=pltpu.CompilerParams(vmem_limit_bytes=VMEM2),
    )(r, rho, start)


def solution(mesh):
    shape = dict(mesh.shape)
    spec = P("gx", "gy", "gz")
    return jax.shard_map(
        functools.partial(body, shape["gx"], shape["gy"], shape["gz"]),
        mesh=mesh, in_specs=(spec,) * 3, out_specs=(spec,) * 2, check_vma=False,
    )
```

```python
import functools
import math

import jax
import jax.numpy as jnp
from jax import lax
from jax.experimental import pallas as pl
from jax.experimental.pallas import tpu as pltpu
from jax.sharding import PartitionSpec as P

ratio_x = 4096.0
ratio_y = 0.2
ratio_z = 0.2
ratio_mix = 0.25
VMEM1 = 61 * 1024 * 1024 + 512 * 1024
VMEM2 = 48 * 1024 * 1024
MESH = pl.DeviceIdType.MESH


def inverse(x):
    guess = pl.reciprocal(x, approx=True)
    guess = guess * (2.0 - x * guess)
    return guess * (2.0 - x * guess)


def link(first, second):
    t1, z1, c1 = first
    t2, z2, c2 = second
    share = inverse(1.0 + z1 * c2)
    k1 = t1 * share
    k2 = t2 * share
    return (k1 * t2, z2 + k2 * t2 * z1, c1 + k1 * t1 * c2), (k1, k2)


def link_sides(weights, first, first_pq, second, second_pq):
    k1, k2 = weights
    p1, q1 = first_pq
    p2, q2 = second_pq
    return (p2 + k2 * (p1 - first[1] * q2), q1 + k1 * (q2 + second[2] * p1))


def pick(flag, yes, no):
    return tuple(jnp.where(flag, s, t) for s, t in zip(yes, no))


def kernel(
    nx, ny, nz, u_hbm, d_hbm, k_hbm, r_buf, rho, start,
    u_pad, d_pad, u_next, u_prev, d_next, d_prev, skew,
    x_halo, y_send, y_recv, z_send, z_recv, own_edge, skew_edge, bend_rows,
    map_send, map_recv, pq_send, pq_recv, rel_send, rel_recv,
    load_sem, halo_send, halo_recv, line_send, line_recv,
):
    planes, rows, lanes = u_hbm.shape
    stages = int(math.log2(nx))
    gx, gy, gz = lax.axis_index("gx"), lax.axis_index("gy"), lax.axis_index("gz")
    other_z = 1 - gz
    pitch = rows + 16
    body_rows = pl.ds(8, rows)
    u_flat = u_pad.reshape(planes * pitch, lanes)
    d_flat = d_pad.reshape(planes * pitch, lanes)

    d_load = pltpu.make_async_copy(d_hbm, d_pad.at[:, body_rows, :], load_sem.at[0])
    u_load = pltpu.make_async_copy(u_hbm, u_pad.at[:, body_rows, :], load_sem.at[1])
    k_load = pltpu.make_async_copy(k_hbm, skew, load_sem.at[2])
    d_load.start()
    u_load.start()
    k_load.start()

    barrier = pltpu.get_barrier_semaphore()

    def greet(x, y, z):
        pl.semaphore_signal(barrier, inc=1, device_id=(x, y, z), device_id_type=MESH)

    partners = [gx + (1 << s) - 2 * (1 << s) * ((gx // (1 << s)) % 2) for s in range(stages)]
    diagonal = partners[-1] + partners[-2] - gx
    for x in (*partners, diagonal):
        greet(x, gy, gz)
    greet(gx, gy, other_z)

    @pl.when(gx > 0)
    def _():
        greet(gx - 1, gy, gz)

    @pl.when(gy > 0)
    def _():
        greet(gx, gy - 1, gz)
        greet(gx, gy - 1, other_z)

    @pl.when(gy < ny - 1)
    def _():
        greet(gx, gy + 1, gz)
        greet(gx, gy + 1, other_z)

    one = jnp.int32(1)
    zero = jnp.int32(0)
    awaited = (
        stages + 2
        + jnp.where(gx < nx - 1, one, zero)
        + 2 * jnp.where(gy > 0, one, zero)
        + 2 * jnp.where(gy < ny - 1, one, zero)
    )

    def remote(src, dst, send, recv, x, y, z):
        return pltpu.make_async_remote_copy(
            src_ref=src, dst_ref=dst, send_sem=send, recv_sem=recv,
            device_id=(x, y, z), device_id_type=MESH,
        )

    x_copy = remote(
        d_hbm.at[planes - 1], x_halo, halo_send.at[0], halo_recv.at[0], gx + 1, gy, gz
    )
    up_copy, down_copy = [
        [
            remote(
                y_send.at[way, field], y_recv.at[1 - way, field],
                halo_send.at[4 + 2 * way + field], halo_recv.at[4 + 2 * way + field], gx, y, gz,
            )
            for field in range(2)
        ]
        for way, y in ((0, gy - 1), (1, gy + 1))
    ]
    z_copy = remote(
        z_send, z_recv.at[:, pl.ds(8, rows), :], halo_send.at[1], halo_recv.at[1], gx, gy, other_z
    )
    up_corner = remote(
        z_send.at[0, pl.ds(0, 8), :], z_recv.at[0, pl.ds(8 + rows, 8), :],
        halo_send.at[2], halo_recv.at[2], gx, gy - 1, other_z,
    )
    down_corner = remote(
        z_send.at[0, pl.ds(rows - 8, 8), :], z_recv.at[0, pl.ds(0, 8), :],
        halo_send.at[3], halo_recv.at[3], gx, gy + 1, other_z,
    )

    @pl.when(gx == 0)
    def _():
        x_halo[...] = jnp.zeros((rows, lanes), jnp.float32)

    @pl.when(gy == 0)
    def _():
        y_recv[0] = jnp.zeros((2, planes, lanes), jnp.float32)
        z_recv[0, 0:8, :] = jnp.zeros((8, lanes), jnp.float32)

    @pl.when(gy == ny - 1)
    def _():
        y_recv[1] = jnp.zeros((2, planes, lanes), jnp.float32)
        z_recv[0, 8 + rows : 16 + rows, :] = jnp.zeros((8, lanes), jnp.float32)

    assert 2 * planes <= lanes and nz == 2
    lane = lax.broadcasted_iota(jnp.int32, (rows, lanes), 1)
    owner = lax.rem((lane + 1) // 2, jnp.int32(planes))

    zeros = jnp.zeros((rows, lanes), jnp.float32)
    ones = jnp.ones((rows, lanes), jnp.float32)

    def gather_edge(i, acc):
        heat = pltpu.roll(u_pad[i, 8 : 8 + rows, :], 2 * i, 1)
        diff = pltpu.roll(d_pad[i, 8 : 8 + rows, :], 2 * i, 1)
        mine = owner == i
        return (jnp.where(mine, heat, acc[0]), jnp.where(mine, diff, acc[1]))

    for field, load, flat in ((1, d_load, d_flat), (0, u_load, u_flat)):
        load.wait()
        y_send[0, field] = flat[pl.ds(8, planes, stride=pitch), :]
        y_send[1, field] = flat[pl.ds(7 + rows, planes, stride=pitch), :]
        if field:
            pl.semaphore_wait(barrier, awaited)

            @pl.when(gx < nx - 1)
            def _():
                x_copy.start()

        @pl.when(gy > 0)
        def _():
            up_copy[field].start()

        @pl.when(gy < ny - 1)
        def _():
            down_copy[field].start()

    edge_heat, edge_diff = lax.fori_loop(0, planes, gather_edge, (zeros, zeros), unroll=8)
    z_send[0] = edge_heat
    z_send[1] = edge_diff

    z_copy.start()

    @pl.when(gy > 0)
    def _():
        up_corner.start()

    @pl.when(gy < ny - 1)
    def _():
        down_corner.start()

    k_load.wait()

    def homogeneous(i, state):
        a, b, c, d, before, acc = state
        here = d_pad[i, 8 : 8 + rows, :]
        heat = u_pad[i, 8 : 8 + rows, :]
        u_next[i, 8 : 8 + rows, :] = pltpu.roll(heat, lanes - 1, 1)
        u_prev[i, 8 : 8 + rows, :] = pltpu.roll(heat, 1, 1)
        d_next[i] = pltpu.roll(here, lanes - 1, 1)
        d_prev[i] = pltpu.roll(here, 1, 1)
        bend = pltpu.roll(skew[i].astype(jnp.float32), 2 * i, 1)
        step = inverse((0.5 * ratio_x) * (here + before))
        rho[i] = step
        a = a + step * c
        b = b + step * d
        return (a, b, c + a, d + b, here, jnp.where(owner == i, bend, acc))

    lead = d_pad[0, 8 : 8 + rows, :]
    a, b, c, d, last, acc = lax.fori_loop(
        0, planes, homogeneous, (ones, zeros, zeros, ones, lead, zeros), unroll=4
    )
    skew_edge[...] = acc

    @pl.when(gx > 0)
    def _():
        x_copy.wait_recv()

    step = inverse((0.5 * ratio_x) * (lead + x_halo[...]))
    change = step - rho[0]
    rho[0] = step
    b = b + a * change
    d = d + c * change
    closing = jnp.where(gx == nx - 1, inverse((0.5 * ratio_x) * last), 0.0)
    inv_d = inverse(d)
    own = (inv_d, b * inv_d + closing, c * inv_d)

    def post(at, send_buf, recv_buf, values, partner):
        for n, v in enumerate(values):
            send_buf[n] = v
        copy = remote(send_buf, recv_buf, line_send.at[at], line_recv.at[at], partner, gy, gz)
        copy.start()
        return copy

    line = [post(0, map_send.at[0], map_recv.at[0], own, partners[0])]

    for pad in (u_pad, d_pad, u_next, u_prev):
        flat = pad.reshape(planes * pitch, lanes)
        for row in (7, 8 + rows):
            flat[pl.ds(row, planes, stride=pitch), :] = jnp.zeros((planes, lanes), jnp.float32)

    def source(i, carried):
        heat = u_pad[i, 8 : 8 + rows, :]
        diff = d_pad[i, 8 : 8 + rows, :]
        flux_y = (diff + d_pad[i, 9 : 9 + rows, :]) * (u_pad[i, 9 : 9 + rows, :] - heat) - (
            diff + d_pad[i, 7 : 7 + rows, :]
        ) * (heat - u_pad[i, 7 : 7 + rows, :])
        flux_z = (diff + d_next[i]) * (u_next[i, 8 : 8 + rows, :] - heat) - (
            diff + d_prev[i]
        ) * (heat - u_prev[i, 8 : 8 + rows, :])
        mixed = (u_next[i, 9 : 9 + rows, :] - u_next[i, 7 : 7 + rows, :]) - (
            u_prev[i, 9 : 9 + rows, :] - u_prev[i, 7 : 7 + rows, :]
        )
        bend = skew[i].astype(jnp.float32)
        bend_rows[0, pl.ds(i, 1), :] = bend[0:1, :]
        bend_rows[1, pl.ds(i, 1), :] = bend[rows - 1 : rows, :]
        r_buf[i] = (
            heat
            + ((0.5 * ratio_y) * flux_y + (0.5 * ratio_z) * flux_z)
            + ratio_mix * bend * mixed
        )
        return carried

    lax.fori_loop(0, planes, source, zero, unroll=2)

    flags = [(gx // (1 << s)) % 2 == 1 for s in range(stages)]
    group, right = own, own
    left = (ones, zeros, zeros)
    steps = []
    for s in range(stages - 1):
        if s:
            line.append(post(s, map_send.at[s], map_recv.at[s], group, partners[s]))
        line[s].wait_recv()
        theirs = tuple(map_recv[s, n] for n in range(3))
        first = pick(flags[s], theirs, group)
        second = pick(flags[s], group, theirs)
        joined, weights = link(first, second)
        if s == stages - 2:
            break
        left_joined, left_weights = link(theirs, left)
        right_joined, right_weights = link(right, theirs)
        steps.append((theirs, first, second, weights, left, left_weights, right, right_weights))
        group = joined
        left = pick(flags[s], left_joined, left)
        right = pick(flags[s], right, right_joined)
    in_right, is_second = flags[-1], flags[-2]
    end = joined[2] + joined[0] * joined[0] * inverse(joined[1])
    line.append(post(
        stages - 1, rel_send.at[0], rel_recv.at[0],
        (jnp.where(in_right, end, joined[1]),), partners[-1],
    ))

    @pl.when(gy > 0)
    def _():
        for copy in down_copy:
            copy.wait_recv()
        down_corner.wait_recv()

    @pl.when(gy < ny - 1)
    def _():
        for copy in up_copy:
            copy.wait_recv()
        up_corner.wait_recv()

    z_copy.wait_recv()
    long_lane = lax.broadcasted_iota(jnp.int32, (planes, lanes), 1)
    r_flat = r_buf.reshape(planes * rows, lanes)
    for way, row, sign in ((0, 0, -ratio_mix), (1, rows - 1, ratio_mix)):
        heat, diff = y_send[way, 0], y_send[way, 1]
        halo, halo_diff = y_recv[way, 0], y_recv[way, 1]
        bend = jnp.where(long_lane == lanes - 1, 0.0, pltpu.roll(halo, lanes - 1, 1)) - jnp.where(
            long_lane == 0, 0.0, pltpu.roll(halo, 1, 1)
        )
        at = pl.ds(row, planes, stride=rows)
        r_flat[at, :] += (0.5 * ratio_y) * (
            diff * halo + halo_diff * (halo - heat)
        ) + sign * bend_rows[way] * bend

    even = lax.rem(lane, jnp.int32(2)) == 0

    def across(x):
        return jnp.where(even, pltpu.roll(x, 1, 1), pltpu.roll(x, lanes - 1, 1))

    own_edge[0:8, :] = jnp.zeros((8, lanes), jnp.float32)
    own_edge[8 : 8 + rows, :] = z_send[0]
    own_edge[8 + rows : 16 + rows, :] = jnp.zeros((8, lanes), jnp.float32)
    heat, diff = z_send[0], z_send[1]
    near = jnp.where(even, 1.0, 0.0)
    near = jnp.where(gz == 0, 1.0 - near, near)
    met_heat = near * across(z_recv[0, 8 : 8 + rows, :])
    met_diff = near * across(z_recv[1, 8 : 8 + rows, :])
    met_bend = near * across(z_recv[0, 9 : 9 + rows, :] - z_recv[0, 7 : 7 + rows, :])
    wrap_bend = across(own_edge[9 : 9 + rows, :] - own_edge[7 : 7 + rows, :])
    edge_term = (0.5 * ratio_z) * (
        (diff + met_diff) * (met_heat - heat) - (diff + across(diff)) * (across(heat) - heat)
    ) + jnp.where(even, -ratio_mix, ratio_mix) * skew_edge[...] * (met_bend - wrap_bend)

    edge_lane = (lane == 0) | (lane == lanes - 1)

    def unpacked(i):
        return pltpu.roll(edge_term, lax.rem(2 * (lanes - i), lanes), 1)

    line[stages - 1].wait_recv()
    met = rel_recv[0, 0]
    z0 = jnp.where(in_right, met, 0.0)
    c0 = jnp.where(in_right, 0.0, met)
    t1, z1, c1 = first
    t2, z2, c2 = second
    e_first = t1 * inverse(1.0 + z0 * c1)
    z_mid = z1 + t1 * e_first * z0
    e_second = t2 * inverse(1.0 + z_mid * c2)
    q_second = t2 * inverse(jnp.where(in_right, z2, 1.0 + z2 * c0))
    p_second = jnp.where(in_right, q_second, q_second * c0)
    c_mid = c2 + t2 * p_second
    q_first = t1 * inverse(1.0 + z1 * c_mid)
    p_first = q_first * c_mid
    z_in = jnp.where(is_second, z_mid, z0)
    c_in = jnp.where(is_second, c_mid, c1 + t1 * p_first)
    e_from_q = jnp.where(is_second, e_second, e_first) * z_in
    q_from_p = jnp.where(is_second, p_second, p_first)
    to_middle = jnp.where(
        in_right, jnp.where(is_second, q_first, 1.0), jnp.where(is_second, 1.0, e_second)
    )
    inv_sum = inverse(1.0 + z_in * c_in)

    def particular(i, state):
        wp, fp, extra = state
        side = r_buf[i] + jnp.where(edge_lane, extra, 0.0)
        r_buf[i] = side
        wp = wp + rho[i] * fp
        return (wp, fp + (wp - side), unpacked(i + 1))

    wp, fp, _ = lax.fori_loop(0, planes, particular, (zeros, zeros, unpacked(0)), unroll=4)

    group_pq = (wp - b * inv_d * fp, fp * inv_d)
    left_pq, right_pq = (zeros, zeros), group_pq
    for s in range(stages - 2):
        copy = post(stages + s, pq_send.at[s], pq_recv.at[s], group_pq, partners[s])
        line.append(copy)
        theirs_map, one_map, two_map, weights, left_map, left_weights, right_map, right_weights = steps[s]
        copy.wait_recv()
        theirs = tuple(pq_recv[s, n] for n in range(2))
        first_pq = pick(flags[s], theirs, group_pq)
        second_pq = pick(flags[s], group_pq, theirs)
        left_pq = pick(
            flags[s], link_sides(left_weights, theirs_map, theirs, left_map, left_pq), left_pq
        )
        right_pq = pick(
            flags[s], right_pq, link_sides(right_weights, right_map, right_pq, theirs_map, theirs)
        )
        group_pq = link_sides(weights, one_map, first_pq, two_map, second_pq)
    e_part = group_pq[0] - e_from_q * group_pq[1]
    q_part = group_pq[1] + q_from_p * group_pq[0]
    at = 2 * stages - 2
    rel_send[2, 0] = jnp.where(in_right, q_part, e_part) * to_middle
    for n, partner in enumerate((diagonal, partners[-1])):
        copy = remote(
            rel_send.at[2], rel_recv.at[2 + n], line_send.at[at + n], line_recv.at[at + n],
            partner, gy, gz,
        )
        copy.start()
        line.append(copy)
    pair = post(
        at + 2, rel_send.at[1], rel_recv.at[1],
        (jnp.where(is_second, q_part, e_part),), partners[-2],
    )
    pair.wait_recv()
    met = rel_recv[1, 0]
    for copy in line[-2:]:
        copy.wait_recv()
    line.append(pair)
    middle = rel_recv[2, 0] + rel_recv[3, 0]
    e0 = jnp.where(in_right, middle, 0.0)
    q0 = jnp.where(in_right, 0.0, middle)
    e_in = jnp.where(is_second, met + e_first * e0, e0)
    q_mid = jnp.where(is_second, q_part, met) + q_second * q0
    q_in = jnp.where(is_second, q_mid, q_part + q_first * q_mid)
    if stages > 2:
        last_one = in_right & is_second
        c_end = jnp.where(is_second, c0, c_mid)
        q_end = jnp.where(is_second, q0, q_mid)
        share = left[0] * inverse(1.0 + z_in * left[2])
        e_in = left_pq[0] + share * (e_in - z_in * left_pq[1])
        z_in = left[1] + share * left[0] * z_in
        share = right[0] * inverse(jnp.where(last_one, right[1], 1.0 + right[1] * c_end))
        c_in = right[2] + right[0] * jnp.where(last_one, share, share * c_end)
        q_in = right_pq[1] + share * jnp.where(last_one, right_pq[0], q_end + c_end * right_pq[0])
        inv_sum = inverse(1.0 + z_in * c_in)
    value = (e_in - z_in * q_in) * inv_sum
    flux = -(c_in * e_in + q_in) * inv_sum

    start[0] = value
    start[1] = flux

    for copy in line:
        copy.wait_send()
    z_copy.wait_send()

    @pl.when(gx < nx - 1)
    def _():
        x_copy.wait_send()

    @pl.when(gy > 0)
    def _():
        for copy in up_copy:
            copy.wait_send()
        up_corner.wait_send()

    @pl.when(gy < ny - 1)
    def _():
        for copy in down_copy:
            copy.wait_send()
        down_corner.wait_send()


def march_kernel(r_buf, rho, start, r_hbm, w_hbm, w_buf, store_sem):
    planes = r_buf.shape[0]
    r_store = pltpu.make_async_copy(r_buf, r_hbm, store_sem.at[0])
    r_store.start()

    def march(i, state):
        value, flux = state
        value = value + rho[i] * flux
        w_buf[i] = value
        return (value, flux + (value - r_buf[i]))

    chunks = 4
    size = planes // chunks

    def store(n):
        part = pl.ds(n * size, size)
        return pltpu.make_async_copy(w_buf.at[part], w_hbm.at[part], store_sem.at[1 + n])

    def chunk(n, state):
        state = lax.fori_loop(0, size, lambda i, s: march(n * size + i, s), state, unroll=8)
        store(n).start()
        return state

    lax.fori_loop(0, chunks, chunk, (start[0], start[1]))
    r_store.wait()
    for n in range(chunks):
        store(n).wait()


def body(nx, ny, nz, initial_thermal_state, thermal_spread_rate, yz_skew_factor):
    planes, rows, lanes = initial_thermal_state.shape
    stages = int(math.log2(nx))
    f32 = jnp.float32
    block = jax.ShapeDtypeStruct((planes, rows, lanes), f32)
    padded = pltpu.VMEM((planes, rows + 16, lanes), f32)
    full = pltpu.VMEM((planes, rows, lanes), f32)
    plane = pltpu.VMEM((rows, lanes), f32)
    faces = pltpu.VMEM((2, 2, planes, lanes), f32)
    maps = pltpu.VMEM((stages - 1, 3, rows, lanes), f32)
    sides = pltpu.VMEM((stages - 1, 2, rows, lanes), f32)
    relation = pltpu.VMEM((4, 1, rows, lanes), f32)
    r, rho, start = pl.pallas_call(
        functools.partial(kernel, nx, ny, nz),
        out_shape=(full, full, pltpu.VMEM((2, rows, lanes), f32)),
        in_specs=[pl.BlockSpec(memory_space=pltpu.HBM)] * 3,
        out_specs=(pl.BlockSpec(memory_space=pltpu.VMEM),) * 3,
        scratch_shapes=[
            padded, padded, padded, padded, full, full,
            pltpu.VMEM((planes, rows, lanes), jnp.bfloat16),
            plane, faces, faces, pltpu.VMEM((2, rows, lanes), f32), pltpu.VMEM((2, rows + 16, lanes), f32),
            pltpu.VMEM((rows + 16, lanes), f32), plane, pltpu.VMEM((2, planes, lanes), f32),
            maps, maps, sides, sides, relation, relation,
            pltpu.SemaphoreType.DMA((3,)),
            pltpu.SemaphoreType.DMA((8,)),
            pltpu.SemaphoreType.DMA((8,)),
            pltpu.SemaphoreType.DMA((2 * stages + 1,)),
            pltpu.SemaphoreType.DMA((2 * stages + 1,)),
        ],
        compiler_params=pltpu.CompilerParams(
            collective_id=0, has_side_effects=True, vmem_limit_bytes=VMEM1
        ),
    )(initial_thermal_state, thermal_spread_rate, yz_skew_factor)
    return pl.pallas_call(
        march_kernel,
        out_shape=(block, block),
        in_specs=[pl.BlockSpec(memory_space=pltpu.VMEM)] * 3,
        out_specs=(pl.BlockSpec(memory_space=pl.ANY),) * 2,
        scratch_shapes=[full, pltpu.SemaphoreType.DMA((5,))],
        compiler_params=pltpu.CompilerParams(vmem_limit_bytes=VMEM2),
    )(r, rho, start)


def solution(mesh):
    shape = dict(mesh.shape)
    spec = P("gx", "gy", "gz")
    return jax.shard_map(
        functools.partial(body, shape["gx"], shape["gy"], shape["gz"]),
        mesh=mesh, in_specs=(spec,) * 3, out_specs=(spec,) * 2, check_vma=False,
    )
```

```python
import functools
import math

import jax
import jax.numpy as jnp
from jax import lax
from jax.experimental import pallas as pl
from jax.experimental.pallas import tpu as pltpu
from jax.sharding import PartitionSpec as P

ratio_x = 4096.0
ratio_y = 0.2
ratio_z = 0.2
ratio_mix = 0.25
VMEM1 = 61 * 1024 * 1024 + 512 * 1024
VMEM2 = 48 * 1024 * 1024
MESH = pl.DeviceIdType.MESH


def inverse(x):
    guess = pl.reciprocal(x, approx=True)
    guess = guess * (2.0 - x * guess)
    return guess * (2.0 - x * guess)


def link(first, second):
    t1, z1, c1 = first
    t2, z2, c2 = second
    share = inverse(1.0 + z1 * c2)
    k1 = t1 * share
    k2 = t2 * share
    return (k1 * t2, z2 + k2 * t2 * z1, c1 + k1 * t1 * c2), (k1, k2)


def link_sides(weights, first, first_pq, second, second_pq):
    k1, k2 = weights
    p1, q1 = first_pq
    p2, q2 = second_pq
    return (p2 + k2 * (p1 - first[1] * q2), q1 + k1 * (q2 + second[2] * p1))


def pick(flag, yes, no):
    return tuple(jnp.where(flag, s, t) for s, t in zip(yes, no))


def kernel(
    nx, ny, nz, u_hbm, d_hbm, k_hbm, r_buf, rho, start,
    u_pad, d_pad, u_next, u_prev, d_next, d_prev, skew,
    x_halo, y_send, y_recv, z_send, z_recv, own_edge, skew_edge, bend_rows,
    map_send, map_recv, pq_send, pq_recv, rel_send, rel_recv,
    load_sem, halo_send, halo_recv, line_send, line_recv,
):
    planes, rows, lanes = u_hbm.shape
    stages = int(math.log2(nx))
    gx, gy, gz = lax.axis_index("gx"), lax.axis_index("gy"), lax.axis_index("gz")
    other_z = 1 - gz
    pitch = rows + 16
    body_rows = pl.ds(8, rows)
    u_flat = u_pad.reshape(planes * pitch, lanes)
    d_flat = d_pad.reshape(planes * pitch, lanes)

    d_load = pltpu.make_async_copy(d_hbm, d_pad.at[:, body_rows, :], load_sem.at[0])
    u_load = pltpu.make_async_copy(u_hbm, u_pad.at[:, body_rows, :], load_sem.at[1])
    k_load = pltpu.make_async_copy(k_hbm, skew, load_sem.at[2])
    d_load.start()
    u_load.start()
    k_load.start()

    barrier = pltpu.get_barrier_semaphore()

    def greet(x, y, z):
        pl.semaphore_signal(barrier, inc=1, device_id=(x, y, z), device_id_type=MESH)

    partners = [gx + (1 << s) - 2 * (1 << s) * ((gx // (1 << s)) % 2) for s in range(stages)]
    diagonal = partners[-1] + partners[-2] - gx
    for x in (*partners, diagonal):
        greet(x, gy, gz)
    greet(gx, gy, other_z)

    @pl.when(gx > 0)
    def _():
        greet(gx - 1, gy, gz)

    @pl.when(gy > 0)
    def _():
        greet(gx, gy - 1, gz)
        greet(gx, gy - 1, other_z)

    @pl.when(gy < ny - 1)
    def _():
        greet(gx, gy + 1, gz)
        greet(gx, gy + 1, other_z)

    one = jnp.int32(1)
    zero = jnp.int32(0)
    awaited = (
        stages + 2
        + jnp.where(gx < nx - 1, one, zero)
        + 2 * jnp.where(gy > 0, one, zero)
        + 2 * jnp.where(gy < ny - 1, one, zero)
    )

    def remote(src, dst, send, recv, x, y, z):
        return pltpu.make_async_remote_copy(
            src_ref=src, dst_ref=dst, send_sem=send, recv_sem=recv,
            device_id=(x, y, z), device_id_type=MESH,
        )

    x_copy = remote(
        d_hbm.at[planes - 1], x_halo, halo_send.at[0], halo_recv.at[0], gx + 1, gy, gz
    )
    up_copy, down_copy = [
        [
            remote(
                y_send.at[way, field], y_recv.at[1 - way, field],
                halo_send.at[4 + 2 * way + field], halo_recv.at[4 + 2 * way + field], gx, y, gz,
            )
            for field in range(2)
        ]
        for way, y in ((0, gy - 1), (1, gy + 1))
    ]
    z_copy = remote(
        z_send, z_recv.at[:, pl.ds(8, rows), :], halo_send.at[1], halo_recv.at[1], gx, gy, other_z
    )
    up_corner = remote(
        z_send.at[0, pl.ds(0, 8), :], z_recv.at[0, pl.ds(8 + rows, 8), :],
        halo_send.at[2], halo_recv.at[2], gx, gy - 1, other_z,
    )
    down_corner = remote(
        z_send.at[0, pl.ds(rows - 8, 8), :], z_recv.at[0, pl.ds(0, 8), :],
        halo_send.at[3], halo_recv.at[3], gx, gy + 1, other_z,
    )

    @pl.when(gx == 0)
    def _():
        x_halo[...] = jnp.zeros((rows, lanes), jnp.float32)

    @pl.when(gy == 0)
    def _():
        y_recv[0] = jnp.zeros((2, planes, lanes), jnp.float32)
        z_recv[0, 0:8, :] = jnp.zeros((8, lanes), jnp.float32)

    @pl.when(gy == ny - 1)
    def _():
        y_recv[1] = jnp.zeros((2, planes, lanes), jnp.float32)
        z_recv[0, 8 + rows : 16 + rows, :] = jnp.zeros((8, lanes), jnp.float32)

    assert 2 * planes <= lanes and nz == 2
    lane = lax.broadcasted_iota(jnp.int32, (rows, lanes), 1)
    owner = lax.rem((lane + 1) // 2, jnp.int32(planes))

    zeros = jnp.zeros((rows, lanes), jnp.float32)
    ones = jnp.ones((rows, lanes), jnp.float32)

    def gather_edge(i, acc):
        heat = pltpu.roll(u_pad[i, 8 : 8 + rows, :], 2 * i, 1)
        diff = pltpu.roll(d_pad[i, 8 : 8 + rows, :], 2 * i, 1)
        mine = owner == i
        return (jnp.where(mine, heat, acc[0]), jnp.where(mine, diff, acc[1]))

    for field, load, flat in ((1, d_load, d_flat), (0, u_load, u_flat)):
        load.wait()
        y_send[0, field] = flat[pl.ds(8, planes, stride=pitch), :]
        y_send[1, field] = flat[pl.ds(7 + rows, planes, stride=pitch), :]
        if field:
            pl.semaphore_wait(barrier, awaited)

            @pl.when(gx < nx - 1)
            def _():
                x_copy.start()

        @pl.when(gy > 0)
        def _():
            up_copy[field].start()

        @pl.when(gy < ny - 1)
        def _():
            down_copy[field].start()

    edge_heat, edge_diff = lax.fori_loop(0, planes, gather_edge, (zeros, zeros), unroll=8)
    z_send[0] = edge_heat
    z_send[1] = edge_diff

    z_copy.start()

    @pl.when(gy > 0)
    def _():
        up_corner.start()

    @pl.when(gy < ny - 1)
    def _():
        down_corner.start()

    k_load.wait()

    def homogeneous(i, state):
        a, b, c, d, before, acc = state
        here = d_pad[i, 8 : 8 + rows, :]
        heat = u_pad[i, 8 : 8 + rows, :]
        u_next[i, 8 : 8 + rows, :] = pltpu.roll(heat, lanes - 1, 1)
        u_prev[i, 8 : 8 + rows, :] = pltpu.roll(heat, 1, 1)
        d_next[i] = pltpu.roll(here, lanes - 1, 1)
        d_prev[i] = pltpu.roll(here, 1, 1)
        bend = pltpu.roll(skew[i].astype(jnp.float32), 2 * i, 1)
        step = inverse((0.5 * ratio_x) * (here + before))
        rho[i] = step
        a = a + step * c
        b = b + step * d
        return (a, b, c + a, d + b, here, jnp.where(owner == i, bend, acc))

    lead = d_pad[0, 8 : 8 + rows, :]
    a, b, c, d, last, acc = lax.fori_loop(
        0, planes, homogeneous, (ones, zeros, zeros, ones, lead, zeros), unroll=4
    )
    skew_edge[...] = acc

    @pl.when(gx > 0)
    def _():
        x_copy.wait_recv()

    step = inverse((0.5 * ratio_x) * (lead + x_halo[...]))
    change = step - rho[0]
    rho[0] = step
    b = b + a * change
    d = d + c * change
    closing = jnp.where(gx == nx - 1, inverse((0.5 * ratio_x) * last), 0.0)
    inv_d = inverse(d)
    own = (inv_d, b * inv_d + closing, c * inv_d)

    def post(at, send_buf, recv_buf, values, partner):
        for n, v in enumerate(values):
            send_buf[n] = v
        copy = remote(send_buf, recv_buf, line_send.at[at], line_recv.at[at], partner, gy, gz)
        copy.start()
        return copy

    line = [post(0, map_send.at[0], map_recv.at[0], own, partners[0])]

    for pad in (u_pad, d_pad, u_next, u_prev):
        flat = pad.reshape(planes * pitch, lanes)
        for row in (7, 8 + rows):
            flat[pl.ds(row, planes, stride=pitch), :] = jnp.zeros((planes, lanes), jnp.float32)

    def source(i, carried):
        heat = u_pad[i, 8 : 8 + rows, :]
        diff = d_pad[i, 8 : 8 + rows, :]
        flux_y = (diff + d_pad[i, 9 : 9 + rows, :]) * (u_pad[i, 9 : 9 + rows, :] - heat) - (
            diff + d_pad[i, 7 : 7 + rows, :]
        ) * (heat - u_pad[i, 7 : 7 + rows, :])
        flux_z = (diff + d_next[i]) * (u_next[i, 8 : 8 + rows, :] - heat) - (
            diff + d_prev[i]
        ) * (heat - u_prev[i, 8 : 8 + rows, :])
        mixed = (u_next[i, 9 : 9 + rows, :] - u_next[i, 7 : 7 + rows, :]) - (
            u_prev[i, 9 : 9 + rows, :] - u_prev[i, 7 : 7 + rows, :]
        )
        bend = skew[i].astype(jnp.float32)
        bend_rows[0, pl.ds(i, 1), :] = bend[0:1, :]
        bend_rows[1, pl.ds(i, 1), :] = bend[rows - 1 : rows, :]
        r_buf[i] = (
            heat
            + ((0.5 * ratio_y) * flux_y + (0.5 * ratio_z) * flux_z)
            + ratio_mix * bend * mixed
        )
        return carried

    lax.fori_loop(0, planes // 2, source, zero, unroll=2)

    flags = [(gx // (1 << s)) % 2 == 1 for s in range(stages)]
    group, right = own, own
    left = (ones, zeros, zeros)
    steps = []
    for s in range(stages - 1):
        if s:
            line.append(post(s, map_send.at[s], map_recv.at[s], group, partners[s]))
        line[s].wait_recv()
        theirs = tuple(map_recv[s, n] for n in range(3))
        first = pick(flags[s], theirs, group)
        second = pick(flags[s], group, theirs)
        joined, weights = link(first, second)
        if s == stages - 2:
            break
        left_joined, left_weights = link(theirs, left)
        right_joined, right_weights = link(right, theirs)
        steps.append((theirs, first, second, weights, left, left_weights, right, right_weights))
        group = joined
        left = pick(flags[s], left_joined, left)
        right = pick(flags[s], right, right_joined)
    in_right, is_second = flags[-1], flags[-2]
    end = joined[2] + joined[0] * joined[0] * inverse(joined[1])
    line.append(post(
        stages - 1, rel_send.at[0], rel_recv.at[0],
        (jnp.where(in_right, end, joined[1]),), partners[-1],
    ))

    lax.fori_loop(planes // 2, planes, source, zero, unroll=2)

    @pl.when(gy > 0)
    def _():
        for copy in down_copy:
            copy.wait_recv()
        down_corner.wait_recv()

    @pl.when(gy < ny - 1)
    def _():
        for copy in up_copy:
            copy.wait_recv()
        up_corner.wait_recv()

    z_copy.wait_recv()
    long_lane = lax.broadcasted_iota(jnp.int32, (planes, lanes), 1)
    r_flat = r_buf.reshape(planes * rows, lanes)
    for way, row, sign in ((0, 0, -ratio_mix), (1, rows - 1, ratio_mix)):
        heat, diff = y_send[way, 0], y_send[way, 1]
        halo, halo_diff = y_recv[way, 0], y_recv[way, 1]
        bend = jnp.where(long_lane == lanes - 1, 0.0, pltpu.roll(halo, lanes - 1, 1)) - jnp.where(
            long_lane == 0, 0.0, pltpu.roll(halo, 1, 1)
        )
        at = pl.ds(row, planes, stride=rows)
        r_flat[at, :] += (0.5 * ratio_y) * (
            diff * halo + halo_diff * (halo - heat)
        ) + sign * bend_rows[way] * bend

    even = lax.rem(lane, jnp.int32(2)) == 0

    def across(x):
        return jnp.where(even, pltpu.roll(x, 1, 1), pltpu.roll(x, lanes - 1, 1))

    own_edge[0:8, :] = jnp.zeros((8, lanes), jnp.float32)
    own_edge[8 : 8 + rows, :] = z_send[0]
    own_edge[8 + rows : 16 + rows, :] = jnp.zeros((8, lanes), jnp.float32)
    heat, diff = z_send[0], z_send[1]
    near = jnp.where(even, 1.0, 0.0)
    near = jnp.where(gz == 0, 1.0 - near, near)
    met_heat = near * across(z_recv[0, 8 : 8 + rows, :])
    met_diff = near * across(z_recv[1, 8 : 8 + rows, :])
    met_bend = near * across(z_recv[0, 9 : 9 + rows, :] - z_recv[0, 7 : 7 + rows, :])
    wrap_bend = across(own_edge[9 : 9 + rows, :] - own_edge[7 : 7 + rows, :])
    edge_term = (0.5 * ratio_z) * (
        (diff + met_diff) * (met_heat - heat) - (diff + across(diff)) * (across(heat) - heat)
    ) + jnp.where(even, -ratio_mix, ratio_mix) * skew_edge[...] * (met_bend - wrap_bend)

    edge_lane = (lane == 0) | (lane == lanes - 1)

    def unpacked(i):
        return pltpu.roll(edge_term, lax.rem(2 * (lanes - i), lanes), 1)

    def particular(i, state):
        wp, fp, extra = state
        side = r_buf[i] + jnp.where(edge_lane, extra, 0.0)
        r_buf[i] = side
        wp = wp + rho[i] * fp
        return (wp, fp + (wp - side), unpacked(i + 1))

    wp, fp, _ = lax.fori_loop(0, planes, particular, (zeros, zeros, unpacked(0)), unroll=4)

    group_pq = (wp - b * inv_d * fp, fp * inv_d)
    left_pq, right_pq = (zeros, zeros), group_pq
    for s in range(stages - 2):
        copy = post(stages + s, pq_send.at[s], pq_recv.at[s], group_pq, partners[s])
        line.append(copy)
        theirs_map, one_map, two_map, weights, left_map, left_weights, right_map, right_weights = steps[s]
        copy.wait_recv()
        theirs = tuple(pq_recv[s, n] for n in range(2))
        first_pq = pick(flags[s], theirs, group_pq)
        second_pq = pick(flags[s], group_pq, theirs)
        left_pq = pick(
            flags[s], link_sides(left_weights, theirs_map, theirs, left_map, left_pq), left_pq
        )
        right_pq = pick(
            flags[s], right_pq, link_sides(right_weights, right_map, right_pq, theirs_map, theirs)
        )
        group_pq = link_sides(weights, one_map, first_pq, two_map, second_pq)
    line[stages - 1].wait_recv()
    met = rel_recv[0, 0]
    z0 = jnp.where(in_right, met, 0.0)
    c0 = jnp.where(in_right, 0.0, met)
    t1, z1, c1 = first
    t2, z2, c2 = second
    e_first = t1 * inverse(1.0 + z0 * c1)
    z_mid = z1 + t1 * e_first * z0
    e_second = t2 * inverse(1.0 + z_mid * c2)
    q_second = t2 * inverse(jnp.where(in_right, z2, 1.0 + z2 * c0))
    p_second = jnp.where(in_right, q_second, q_second * c0)
    c_mid = c2 + t2 * p_second
    q_first = t1 * inverse(1.0 + z1 * c_mid)
    p_first = q_first * c_mid
    z_in = jnp.where(is_second, z_mid, z0)
    c_in = jnp.where(is_second, c_mid, c1 + t1 * p_first)
    e_from_q = jnp.where(is_second, e_second, e_first) * z_in
    q_from_p = jnp.where(is_second, p_second, p_first)
    to_middle = jnp.where(
        in_right, jnp.where(is_second, q_first, 1.0), jnp.where(is_second, 1.0, e_second)
    )
    inv_sum = inverse(1.0 + z_in * c_in)

    e_part = group_pq[0] - e_from_q * group_pq[1]
    q_part = group_pq[1] + q_from_p * group_pq[0]
    at = 2 * stages - 2
    rel_send[2, 0] = jnp.where(in_right, q_part, e_part) * to_middle
    for n, partner in enumerate((diagonal, partners[-1])):
        copy = remote(
            rel_send.at[2], rel_recv.at[2 + n], line_send.at[at + n], line_recv.at[at + n],
            partner, gy, gz,
        )
        copy.start()
        line.append(copy)
    pair = post(
        at + 2, rel_send.at[1], rel_recv.at[1],
        (jnp.where(is_second, q_part, e_part),), partners[-2],
    )
    pair.wait_recv()
    met = rel_recv[1, 0]
    for copy in line[-2:]:
        copy.wait_recv()
    line.append(pair)
    middle = rel_recv[2, 0] + rel_recv[3, 0]
    e0 = jnp.where(in_right, middle, 0.0)
    q0 = jnp.where(in_right, 0.0, middle)
    e_in = jnp.where(is_second, met + e_first * e0, e0)
    q_mid = jnp.where(is_second, q_part, met) + q_second * q0
    q_in = jnp.where(is_second, q_mid, q_part + q_first * q_mid)
    if stages > 2:
        last_one = in_right & is_second
        c_end = jnp.where(is_second, c0, c_mid)
        q_end = jnp.where(is_second, q0, q_mid)
        share = left[0] * inverse(1.0 + z_in * left[2])
        e_in = left_pq[0] + share * (e_in - z_in * left_pq[1])
        z_in = left[1] + share * left[0] * z_in
        share = right[0] * inverse(jnp.where(last_one, right[1], 1.0 + right[1] * c_end))
        c_in = right[2] + right[0] * jnp.where(last_one, share, share * c_end)
        q_in = right_pq[1] + share * jnp.where(last_one, right_pq[0], q_end + c_end * right_pq[0])
        inv_sum = inverse(1.0 + z_in * c_in)
    value = (e_in - z_in * q_in) * inv_sum
    flux = -(c_in * e_in + q_in) * inv_sum

    start[0] = value
    start[1] = flux

    for copy in line:
        copy.wait_send()
    z_copy.wait_send()

    @pl.when(gx < nx - 1)
    def _():
        x_copy.wait_send()

    @pl.when(gy > 0)
    def _():
        for copy in up_copy:
            copy.wait_send()
        up_corner.wait_send()

    @pl.when(gy < ny - 1)
    def _():
        for copy in down_copy:
            copy.wait_send()
        down_corner.wait_send()


def march_kernel(r_buf, rho, start, r_hbm, w_hbm, w_buf, store_sem):
    planes = r_buf.shape[0]
    r_store = pltpu.make_async_copy(r_buf, r_hbm, store_sem.at[0])
    r_store.start()

    def march(i, state):
        value, flux = state
        value = value + rho[i] * flux
        w_buf[i] = value
        return (value, flux + (value - r_buf[i]))

    chunks = 4
    size = planes // chunks

    def store(n):
        part = pl.ds(n * size, size)
        return pltpu.make_async_copy(w_buf.at[part], w_hbm.at[part], store_sem.at[1 + n])

    def chunk(n, state):
        state = lax.fori_loop(0, size, lambda i, s: march(n * size + i, s), state, unroll=8)
        store(n).start()
        return state

    lax.fori_loop(0, chunks, chunk, (start[0], start[1]))
    r_store.wait()
    for n in range(chunks):
        store(n).wait()


def body(nx, ny, nz, initial_thermal_state, thermal_spread_rate, yz_skew_factor):
    planes, rows, lanes = initial_thermal_state.shape
    stages = int(math.log2(nx))
    f32 = jnp.float32
    block = jax.ShapeDtypeStruct((planes, rows, lanes), f32)
    padded = pltpu.VMEM((planes, rows + 16, lanes), f32)
    full = pltpu.VMEM((planes, rows, lanes), f32)
    plane = pltpu.VMEM((rows, lanes), f32)
    faces = pltpu.VMEM((2, 2, planes, lanes), f32)
    maps = pltpu.VMEM((stages - 1, 3, rows, lanes), f32)
    sides = pltpu.VMEM((stages - 1, 2, rows, lanes), f32)
    relation = pltpu.VMEM((4, 1, rows, lanes), f32)
    r, rho, start = pl.pallas_call(
        functools.partial(kernel, nx, ny, nz),
        out_shape=(full, full, pltpu.VMEM((2, rows, lanes), f32)),
        in_specs=[pl.BlockSpec(memory_space=pltpu.HBM)] * 3,
        out_specs=(pl.BlockSpec(memory_space=pltpu.VMEM),) * 3,
        scratch_shapes=[
            padded, padded, padded, padded, full, full,
            pltpu.VMEM((planes, rows, lanes), jnp.bfloat16),
            plane, faces, faces, pltpu.VMEM((2, rows, lanes), f32), pltpu.VMEM((2, rows + 16, lanes), f32),
            pltpu.VMEM((rows + 16, lanes), f32), plane, pltpu.VMEM((2, planes, lanes), f32),
            maps, maps, sides, sides, relation, relation,
            pltpu.SemaphoreType.DMA((3,)),
            pltpu.SemaphoreType.DMA((8,)),
            pltpu.SemaphoreType.DMA((8,)),
            pltpu.SemaphoreType.DMA((2 * stages + 1,)),
            pltpu.SemaphoreType.DMA((2 * stages + 1,)),
        ],
        compiler_params=pltpu.CompilerParams(
            collective_id=0, has_side_effects=True, vmem_limit_bytes=VMEM1
        ),
    )(initial_thermal_state, thermal_spread_rate, yz_skew_factor)
    return pl.pallas_call(
        march_kernel,
        out_shape=(block, block),
        in_specs=[pl.BlockSpec(memory_space=pltpu.VMEM)] * 3,
        out_specs=(pl.BlockSpec(memory_space=pl.ANY),) * 2,
        scratch_shapes=[full, pltpu.SemaphoreType.DMA((5,))],
        compiler_params=pltpu.CompilerParams(vmem_limit_bytes=VMEM2),
    )(r, rho, start)


def solution(mesh):
    shape = dict(mesh.shape)
    spec = P("gx", "gy", "gz")
    return jax.shard_map(
        functools.partial(body, shape["gx"], shape["gy"], shape["gz"]),
        mesh=mesh, in_specs=(spec,) * 3, out_specs=(spec,) * 2, check_vma=False,
    )
```

```python
import functools
import math

import jax
import jax.numpy as jnp
from jax import lax
from jax.experimental import pallas as pl
from jax.experimental.pallas import tpu as pltpu
from jax.sharding import PartitionSpec as P

ratio_x = 4096.0
ratio_y = 0.2
ratio_z = 0.2
ratio_mix = 0.25
VMEM1 = 61 * 1024 * 1024 + 512 * 1024
VMEM2 = 48 * 1024 * 1024
MESH = pl.DeviceIdType.MESH


def inverse(x):
    guess = pl.reciprocal(x, approx=True)
    guess = guess * (2.0 - x * guess)
    return guess * (2.0 - x * guess)


def link(first, second):
    t1, z1, c1 = first
    t2, z2, c2 = second
    share = inverse(1.0 + z1 * c2)
    k1 = t1 * share
    k2 = t2 * share
    return (k1 * t2, z2 + k2 * t2 * z1, c1 + k1 * t1 * c2), (k1, k2)


def link_sides(weights, first, first_pq, second, second_pq):
    k1, k2 = weights
    p1, q1 = first_pq
    p2, q2 = second_pq
    return (p2 + k2 * (p1 - first[1] * q2), q1 + k1 * (q2 + second[2] * p1))


def pick(flag, yes, no):
    return tuple(jnp.where(flag, s, t) for s, t in zip(yes, no))


def kernel(
    nx, ny, nz, u_hbm, d_hbm, k_hbm, r_buf, rho, start,
    u_pad, d_pad, u_next, u_prev, d_next, d_prev, skew,
    x_halo, y_send, y_recv, z_send, z_recv, own_edge, skew_edge, bend_rows,
    map_send, map_recv, pq_send, pq_recv, rel_send, rel_recv,
    load_sem, halo_send, halo_recv, line_send, line_recv,
):
    planes, rows, lanes = u_hbm.shape
    stages = int(math.log2(nx))
    gx, gy, gz = lax.axis_index("gx"), lax.axis_index("gy"), lax.axis_index("gz")
    other_z = 1 - gz
    pitch = rows + 16
    body_rows = pl.ds(8, rows)
    u_flat = u_pad.reshape(planes * pitch, lanes)
    d_flat = d_pad.reshape(planes * pitch, lanes)

    d_load = pltpu.make_async_copy(d_hbm, d_pad.at[:, body_rows, :], load_sem.at[0])
    u_load = pltpu.make_async_copy(u_hbm, u_pad.at[:, body_rows, :], load_sem.at[1])
    k_load = pltpu.make_async_copy(k_hbm, skew, load_sem.at[2])
    d_load.start()
    u_load.start()
    k_load.start()

    barrier = pltpu.get_barrier_semaphore()

    def greet(x, y, z):
        pl.semaphore_signal(barrier, inc=1, device_id=(x, y, z), device_id_type=MESH)

    partners = [gx + (1 << s) - 2 * (1 << s) * ((gx // (1 << s)) % 2) for s in range(stages)]
    diagonal = partners[-1] + partners[-2] - gx
    for x in (*partners, diagonal):
        greet(x, gy, gz)
    greet(gx, gy, other_z)

    @pl.when(gx > 0)
    def _():
        greet(gx - 1, gy, gz)

    @pl.when(gy > 0)
    def _():
        greet(gx, gy - 1, gz)
        greet(gx, gy - 1, other_z)

    @pl.when(gy < ny - 1)
    def _():
        greet(gx, gy + 1, gz)
        greet(gx, gy + 1, other_z)

    one = jnp.int32(1)
    zero = jnp.int32(0)
    awaited = (
        stages + 2
        + jnp.where(gx < nx - 1, one, zero)
        + 2 * jnp.where(gy > 0, one, zero)
        + 2 * jnp.where(gy < ny - 1, one, zero)
    )

    def remote(src, dst, send, recv, x, y, z):
        return pltpu.make_async_remote_copy(
            src_ref=src, dst_ref=dst, send_sem=send, recv_sem=recv,
            device_id=(x, y, z), device_id_type=MESH,
        )

    x_copy = remote(
        d_hbm.at[planes - 1], x_halo, halo_send.at[0], halo_recv.at[0], gx + 1, gy, gz
    )
    up_copy, down_copy = [
        [
            remote(
                y_send.at[way, field], y_recv.at[1 - way, field],
                halo_send.at[4 + 2 * way + field], halo_recv.at[4 + 2 * way + field], gx, y, gz,
            )
            for field in range(2)
        ]
        for way, y in ((0, gy - 1), (1, gy + 1))
    ]
    z_copy = remote(
        z_send, z_recv.at[:, pl.ds(8, rows), :], halo_send.at[1], halo_recv.at[1], gx, gy, other_z
    )
    up_corner = remote(
        z_send.at[0, pl.ds(0, 8), :], z_recv.at[0, pl.ds(8 + rows, 8), :],
        halo_send.at[2], halo_recv.at[2], gx, gy - 1, other_z,
    )
    down_corner = remote(
        z_send.at[0, pl.ds(rows - 8, 8), :], z_recv.at[0, pl.ds(0, 8), :],
        halo_send.at[3], halo_recv.at[3], gx, gy + 1, other_z,
    )

    @pl.when(gx == 0)
    def _():
        x_halo[...] = jnp.zeros((rows, lanes), jnp.float32)

    @pl.when(gy == 0)
    def _():
        y_recv[0] = jnp.zeros((2, planes, lanes), jnp.float32)
        z_recv[0, 0:8, :] = jnp.zeros((8, lanes), jnp.float32)

    @pl.when(gy == ny - 1)
    def _():
        y_recv[1] = jnp.zeros((2, planes, lanes), jnp.float32)
        z_recv[0, 8 + rows : 16 + rows, :] = jnp.zeros((8, lanes), jnp.float32)

    assert 2 * planes <= lanes and nz == 2
    lane = lax.broadcasted_iota(jnp.int32, (rows, lanes), 1)
    owner = lax.rem((lane + 1) // 2, jnp.int32(planes))

    zeros = jnp.zeros((rows, lanes), jnp.float32)
    ones = jnp.ones((rows, lanes), jnp.float32)

    def gather_edge(i, acc):
        heat = pltpu.roll(u_pad[i, 8 : 8 + rows, :], 2 * i, 1)
        diff = pltpu.roll(d_pad[i, 8 : 8 + rows, :], 2 * i, 1)
        mine = owner == i
        return (jnp.where(mine, heat, acc[0]), jnp.where(mine, diff, acc[1]))

    for pad in (u_next, u_prev):
        flat = pad.reshape(planes * pitch, lanes)
        for row in (7, 8 + rows):
            flat[pl.ds(row, planes, stride=pitch), :] = jnp.zeros((planes, lanes), jnp.float32)

    for field, load, flat in ((1, d_load, d_flat), (0, u_load, u_flat)):
        load.wait()
        y_send[0, field] = flat[pl.ds(8, planes, stride=pitch), :]
        y_send[1, field] = flat[pl.ds(7 + rows, planes, stride=pitch), :]
        if field:
            pl.semaphore_wait(barrier, awaited)

            @pl.when(gx < nx - 1)
            def _():
                x_copy.start()

        @pl.when(gy > 0)
        def _():
            up_copy[field].start()

        @pl.when(gy < ny - 1)
        def _():
            down_copy[field].start()

    edge_heat, edge_diff = lax.fori_loop(0, planes, gather_edge, (zeros, zeros), unroll=8)
    z_send[0] = edge_heat
    z_send[1] = edge_diff

    z_copy.start()

    @pl.when(gy > 0)
    def _():
        up_corner.start()

    @pl.when(gy < ny - 1)
    def _():
        down_corner.start()

    k_load.wait()

    def homogeneous(i, state):
        a, b, c, d, before, acc = state
        here = d_pad[i, 8 : 8 + rows, :]
        heat = u_pad[i, 8 : 8 + rows, :]
        u_next[i, 8 : 8 + rows, :] = pltpu.roll(heat, lanes - 1, 1)
        u_prev[i, 8 : 8 + rows, :] = pltpu.roll(heat, 1, 1)
        d_next[i] = pltpu.roll(here, lanes - 1, 1)
        d_prev[i] = pltpu.roll(here, 1, 1)
        bend = pltpu.roll(skew[i].astype(jnp.float32), 2 * i, 1)
        step = inverse((0.5 * ratio_x) * (here + before))
        rho[i] = step
        a = a + step * c
        b = b + step * d
        return (a, b, c + a, d + b, here, jnp.where(owner == i, bend, acc))

    lead = d_pad[0, 8 : 8 + rows, :]
    a, b, c, d, last, acc = lax.fori_loop(
        0, planes, homogeneous, (ones, zeros, zeros, ones, lead, zeros), unroll=4
    )
    skew_edge[...] = acc

    @pl.when(gx > 0)
    def _():
        x_copy.wait_recv()

    step = inverse((0.5 * ratio_x) * (lead + x_halo[...]))
    change = step - rho[0]
    rho[0] = step
    b = b + a * change
    d = d + c * change
    closing = jnp.where(gx == nx - 1, inverse((0.5 * ratio_x) * last), 0.0)
    inv_d = inverse(d)
    own = (inv_d, b * inv_d + closing, c * inv_d)

    def post(at, send_buf, recv_buf, values, partner):
        for n, v in enumerate(values):
            send_buf[n] = v
        copy = remote(send_buf, recv_buf, line_send.at[at], line_recv.at[at], partner, gy, gz)
        copy.start()
        return copy

    line = [post(0, map_send.at[0], map_recv.at[0], own, partners[0])]

    for pad in (u_pad, d_pad):
        flat = pad.reshape(planes * pitch, lanes)
        for row in (7, 8 + rows):
            flat[pl.ds(row, planes, stride=pitch), :] = jnp.zeros((planes, lanes), jnp.float32)

    def source(i, carried):
        heat = u_pad[i, 8 : 8 + rows, :]
        diff = d_pad[i, 8 : 8 + rows, :]
        flux_y = (diff + d_pad[i, 9 : 9 + rows, :]) * (u_pad[i, 9 : 9 + rows, :] - heat) - (
            diff + d_pad[i, 7 : 7 + rows, :]
        ) * (heat - u_pad[i, 7 : 7 + rows, :])
        flux_z = (diff + d_next[i]) * (u_next[i, 8 : 8 + rows, :] - heat) - (
            diff + d_prev[i]
        ) * (heat - u_prev[i, 8 : 8 + rows, :])
        mixed = (u_next[i, 9 : 9 + rows, :] - u_next[i, 7 : 7 + rows, :]) - (
            u_prev[i, 9 : 9 + rows, :] - u_prev[i, 7 : 7 + rows, :]
        )
        bend = skew[i].astype(jnp.float32)
        bend_rows[0, pl.ds(i, 1), :] = bend[0:1, :]
        bend_rows[1, pl.ds(i, 1), :] = bend[rows - 1 : rows, :]
        r_buf[i] = (
            heat
            + ((0.5 * ratio_y) * flux_y + (0.5 * ratio_z) * flux_z)
            + ratio_mix * bend * mixed
        )
        return carried

    lax.fori_loop(0, planes // 2, source, zero, unroll=4)

    flags = [(gx // (1 << s)) % 2 == 1 for s in range(stages)]
    group, right = own, own
    left = (ones, zeros, zeros)
    steps = []
    for s in range(stages - 1):
        if s:
            line.append(post(s, map_send.at[s], map_recv.at[s], group, partners[s]))
        line[s].wait_recv()
        theirs = tuple(map_recv[s, n] for n in range(3))
        first = pick(flags[s], theirs, group)
        second = pick(flags[s], group, theirs)
        joined, weights = link(first, second)
        if s == stages - 2:
            break
        left_joined, left_weights = link(theirs, left)
        right_joined, right_weights = link(right, theirs)
        steps.append((theirs, first, second, weights, left, left_weights, right, right_weights))
        group = joined
        left = pick(flags[s], left_joined, left)
        right = pick(flags[s], right, right_joined)
    in_right, is_second = flags[-1], flags[-2]
    end = joined[2] + joined[0] * joined[0] * inverse(joined[1])
    line.append(post(
        stages - 1, rel_send.at[0], rel_recv.at[0],
        (jnp.where(in_right, end, joined[1]),), partners[-1],
    ))

    lax.fori_loop(planes // 2, planes, source, zero, unroll=4)

    @pl.when(gy > 0)
    def _():
        for copy in down_copy:
            copy.wait_recv()
        down_corner.wait_recv()

    @pl.when(gy < ny - 1)
    def _():
        for copy in up_copy:
            copy.wait_recv()
        up_corner.wait_recv()

    z_copy.wait_recv()
    long_lane = lax.broadcasted_iota(jnp.int32, (planes, lanes), 1)
    r_flat = r_buf.reshape(planes * rows, lanes)
    for way, row, sign in ((0, 0, -ratio_mix), (1, rows - 1, ratio_mix)):
        heat, diff = y_send[way, 0], y_send[way, 1]
        halo, halo_diff = y_recv[way, 0], y_recv[way, 1]
        bend = jnp.where(long_lane == lanes - 1, 0.0, pltpu.roll(halo, lanes - 1, 1)) - jnp.where(
            long_lane == 0, 0.0, pltpu.roll(halo, 1, 1)
        )
        at = pl.ds(row, planes, stride=rows)
        r_flat[at, :] += (0.5 * ratio_y) * (
            diff * halo + halo_diff * (halo - heat)
        ) + sign * bend_rows[way] * bend

    even = lax.rem(lane, jnp.int32(2)) == 0

    def across(x):
        return jnp.where(even, pltpu.roll(x, 1, 1), pltpu.roll(x, lanes - 1, 1))

    own_edge[0:8, :] = jnp.zeros((8, lanes), jnp.float32)
    own_edge[8 : 8 + rows, :] = z_send[0]
    own_edge[8 + rows : 16 + rows, :] = jnp.zeros((8, lanes), jnp.float32)
    heat, diff = z_send[0], z_send[1]
    near = jnp.where(even, 1.0, 0.0)
    near = jnp.where(gz == 0, 1.0 - near, near)
    met_heat = near * across(z_recv[0, 8 : 8 + rows, :])
    met_diff = near * across(z_recv[1, 8 : 8 + rows, :])
    met_bend = near * across(z_recv[0, 9 : 9 + rows, :] - z_recv[0, 7 : 7 + rows, :])
    wrap_bend = across(own_edge[9 : 9 + rows, :] - own_edge[7 : 7 + rows, :])
    edge_term = (0.5 * ratio_z) * (
        (diff + met_diff) * (met_heat - heat) - (diff + across(diff)) * (across(heat) - heat)
    ) + jnp.where(even, -ratio_mix, ratio_mix) * skew_edge[...] * (met_bend - wrap_bend)

    edge_lane = (lane == 0) | (lane == lanes - 1)

    def unpacked(i):
        return pltpu.roll(edge_term, lax.rem(2 * (lanes - i), lanes), 1)

    def particular(i, state):
        wp, fp, extra = state
        side = r_buf[i] + jnp.where(edge_lane, extra, 0.0)
        r_buf[i] = side
        wp = wp + rho[i] * fp
        return (wp, fp + (wp - side), unpacked(i + 1))

    wp, fp, _ = lax.fori_loop(0, planes, particular, (zeros, zeros, unpacked(0)), unroll=4)

    group_pq = (wp - b * inv_d * fp, fp * inv_d)
    left_pq, right_pq = (zeros, zeros), group_pq
    for s in range(stages - 2):
        copy = post(stages + s, pq_send.at[s], pq_recv.at[s], group_pq, partners[s])
        line.append(copy)
        theirs_map, one_map, two_map, weights, left_map, left_weights, right_map, right_weights = steps[s]
        copy.wait_recv()
        theirs = tuple(pq_recv[s, n] for n in range(2))
        first_pq = pick(flags[s], theirs, group_pq)
        second_pq = pick(flags[s], group_pq, theirs)
        left_pq = pick(
            flags[s], link_sides(left_weights, theirs_map, theirs, left_map, left_pq), left_pq
        )
        right_pq = pick(
            flags[s], right_pq, link_sides(right_weights, right_map, right_pq, theirs_map, theirs)
        )
        group_pq = link_sides(weights, one_map, first_pq, two_map, second_pq)
    line[stages - 1].wait_recv()
    met = rel_recv[0, 0]
    z0 = jnp.where(in_right, met, 0.0)
    c0 = jnp.where(in_right, 0.0, met)
    t1, z1, c1 = first
    t2, z2, c2 = second
    e_first = t1 * inverse(1.0 + z0 * c1)
    z_mid = z1 + t1 * e_first * z0
    e_second = t2 * inverse(1.0 + z_mid * c2)
    q_second = t2 * inverse(jnp.where(in_right, z2, 1.0 + z2 * c0))
    p_second = jnp.where(in_right, q_second, q_second * c0)
    c_mid = c2 + t2 * p_second
    q_first = t1 * inverse(1.0 + z1 * c_mid)
    p_first = q_first * c_mid
    z_in = jnp.where(is_second, z_mid, z0)
    c_in = jnp.where(is_second, c_mid, c1 + t1 * p_first)
    e_from_q = jnp.where(is_second, e_second, e_first) * z_in
    q_from_p = jnp.where(is_second, p_second, p_first)
    to_middle = jnp.where(
        in_right, jnp.where(is_second, q_first, 1.0), jnp.where(is_second, 1.0, e_second)
    )
    inv_sum = inverse(1.0 + z_in * c_in)

    e_part = group_pq[0] - e_from_q * group_pq[1]
    q_part = group_pq[1] + q_from_p * group_pq[0]
    at = 2 * stages - 2
    rel_send[2, 0] = jnp.where(in_right, q_part, e_part) * to_middle
    for n, partner in enumerate((diagonal, partners[-1])):
        copy = remote(
            rel_send.at[2], rel_recv.at[2 + n], line_send.at[at + n], line_recv.at[at + n],
            partner, gy, gz,
        )
        copy.start()
        line.append(copy)
    pair = post(
        at + 2, rel_send.at[1], rel_recv.at[1],
        (jnp.where(is_second, q_part, e_part),), partners[-2],
    )
    pair.wait_recv()
    met = rel_recv[1, 0]
    for copy in line[-2:]:
        copy.wait_recv()
    line.append(pair)
    middle = rel_recv[2, 0] + rel_recv[3, 0]
    e0 = jnp.where(in_right, middle, 0.0)
    q0 = jnp.where(in_right, 0.0, middle)
    e_in = jnp.where(is_second, met + e_first * e0, e0)
    q_mid = jnp.where(is_second, q_part, met) + q_second * q0
    q_in = jnp.where(is_second, q_mid, q_part + q_first * q_mid)
    if stages > 2:
        last_one = in_right & is_second
        c_end = jnp.where(is_second, c0, c_mid)
        q_end = jnp.where(is_second, q0, q_mid)
        share = left[0] * inverse(1.0 + z_in * left[2])
        e_in = left_pq[0] + share * (e_in - z_in * left_pq[1])
        z_in = left[1] + share * left[0] * z_in
        share = right[0] * inverse(jnp.where(last_one, right[1], 1.0 + right[1] * c_end))
        c_in = right[2] + right[0] * jnp.where(last_one, share, share * c_end)
        q_in = right_pq[1] + share * jnp.where(last_one, right_pq[0], q_end + c_end * right_pq[0])
        inv_sum = inverse(1.0 + z_in * c_in)
    value = (e_in - z_in * q_in) * inv_sum
    flux = -(c_in * e_in + q_in) * inv_sum

    start[0] = value
    start[1] = flux

    for copy in line:
        copy.wait_send()
    z_copy.wait_send()

    @pl.when(gx < nx - 1)
    def _():
        x_copy.wait_send()

    @pl.when(gy > 0)
    def _():
        for copy in up_copy:
            copy.wait_send()
        up_corner.wait_send()

    @pl.when(gy < ny - 1)
    def _():
        for copy in down_copy:
            copy.wait_send()
        down_corner.wait_send()


def march_kernel(r_buf, rho, start, r_hbm, w_hbm, w_buf, store_sem):
    planes = r_buf.shape[0]
    r_store = pltpu.make_async_copy(r_buf, r_hbm, store_sem.at[0])
    r_store.start()

    def march(i, state):
        value, flux = state
        value = value + rho[i] * flux
        w_buf[i] = value
        return (value, flux + (value - r_buf[i]))

    chunks = 4
    size = planes // chunks

    def store(n):
        part = pl.ds(n * size, size)
        return pltpu.make_async_copy(w_buf.at[part], w_hbm.at[part], store_sem.at[1 + n])

    def chunk(n, state):
        state = lax.fori_loop(0, size, lambda i, s: march(n * size + i, s), state, unroll=8)
        store(n).start()
        return state

    lax.fori_loop(0, chunks, chunk, (start[0], start[1]))
    r_store.wait()
    for n in range(chunks):
        store(n).wait()


def body(nx, ny, nz, initial_thermal_state, thermal_spread_rate, yz_skew_factor):
    planes, rows, lanes = initial_thermal_state.shape
    stages = int(math.log2(nx))
    f32 = jnp.float32
    block = jax.ShapeDtypeStruct((planes, rows, lanes), f32)
    padded = pltpu.VMEM((planes, rows + 16, lanes), f32)
    full = pltpu.VMEM((planes, rows, lanes), f32)
    plane = pltpu.VMEM((rows, lanes), f32)
    faces = pltpu.VMEM((2, 2, planes, lanes), f32)
    maps = pltpu.VMEM((stages - 1, 3, rows, lanes), f32)
    sides = pltpu.VMEM((stages - 1, 2, rows, lanes), f32)
    relation = pltpu.VMEM((4, 1, rows, lanes), f32)
    r, rho, start = pl.pallas_call(
        functools.partial(kernel, nx, ny, nz),
        out_shape=(full, full, pltpu.VMEM((2, rows, lanes), f32)),
        in_specs=[pl.BlockSpec(memory_space=pltpu.HBM)] * 3,
        out_specs=(pl.BlockSpec(memory_space=pltpu.VMEM),) * 3,
        scratch_shapes=[
            padded, padded, padded, padded, full, full,
            pltpu.VMEM((planes, rows, lanes), jnp.bfloat16),
            plane, faces, faces, pltpu.VMEM((2, rows, lanes), f32), pltpu.VMEM((2, rows + 16, lanes), f32),
            pltpu.VMEM((rows + 16, lanes), f32), plane, pltpu.VMEM((2, planes, lanes), f32),
            maps, maps, sides, sides, relation, relation,
            pltpu.SemaphoreType.DMA((3,)),
            pltpu.SemaphoreType.DMA((8,)),
            pltpu.SemaphoreType.DMA((8,)),
            pltpu.SemaphoreType.DMA((2 * stages + 1,)),
            pltpu.SemaphoreType.DMA((2 * stages + 1,)),
        ],
        compiler_params=pltpu.CompilerParams(
            collective_id=0, has_side_effects=True, vmem_limit_bytes=VMEM1
        ),
    )(initial_thermal_state, thermal_spread_rate, yz_skew_factor)
    return pl.pallas_call(
        march_kernel,
        out_shape=(block, block),
        in_specs=[pl.BlockSpec(memory_space=pltpu.VMEM)] * 3,
        out_specs=(pl.BlockSpec(memory_space=pl.ANY),) * 2,
        scratch_shapes=[full, pltpu.SemaphoreType.DMA((5,))],
        compiler_params=pltpu.CompilerParams(vmem_limit_bytes=VMEM2),
    )(r, rho, start)


def solution(mesh):
    shape = dict(mesh.shape)
    spec = P("gx", "gy", "gz")
    return jax.shard_map(
        functools.partial(body, shape["gx"], shape["gy"], shape["gz"]),
        mesh=mesh, in_specs=(spec,) * 3, out_specs=(spec,) * 2, check_vma=False,
    )
```
